32 devices in a mesh: dp: 4 (over z), expert: 8 (over y, x, core).
Axes of the slice: x: 2, y: 2, z: 4, core: 2. Of those that a mesh axis runs over, the one named last changes fastest.
Arguments:
- images: bfloat16 [256, 197, 384], P(('dp', 'expert')), may hold values from -6 to 6
- cotangent: bfloat16 [256, 197, 384], P(('dp', 'expert')), may hold values from -6 to 6
- router_noise: float32 [256, 197, 8], P(('dp', 'expert')), may hold values from -3 to 3
- routes: int32 [256, 197, 2], P(('dp', 'expert')), may hold values from 0 to 7, all different within a row
- seat_order: int32 [32, 3152], P(('dp', 'expert')), may hold values from 0 to 3151, each once within a row
- norm1_gain: float32 [384], replicated, may hold values from 0.5 to 1.5
- norm1_shift: float32 [384], replicated, may hold values from -1 to 1
- query_weight: bfloat16 [384, 384], replicated, may hold values from -0.3125 to 0.3125
- query_bias: float32 [384], replicated, may hold values from -1 to 1
- key_weight: bfloat16 [384, 384], replicated, may hold values from -0.3125 to 0.3125
- value_weight: bfloat16 [384, 384], replicated, may hold values from -0.3125 to 0.3125
- value_bias: float32 [384], replicated, may hold values from -1 to 1
- output_weight: bfloat16 [384, 384], replicated, may hold values from -2.5 to 2.5
- output_bias: float32 [384], replicated, may hold values from -1 to 1
- norm2_gain: float32 [384], replicated, may hold values from 0.5 to 1.5
- norm2_shift: float32 [384], replicated, may hold values from -1 to 1
- router_weight: bfloat16 [384, 8], replicated, may hold values from -0.1796875 to 0.1796875
- expert_in: bfloat16 [8, 384, 1536], P('expert'), may hold values from -0.3125 to 0.3125
- expert_out: bfloat16 [8, 1536, 384], P('expert'), may hold values from -2.5 to 2.5
- master_in: float32 [8, 384, 1536], P('expert', 'dp'), may hold values from -0.3125 to 0.3125
- master_out: float32 [8, 1536, 384], P('expert', 'dp'), may hold values from -0.15625 to 0.15625
- moment_in: float32 [8, 384, 1536], P('expert', 'dp'), may hold values from -6 to 6
- moment_out: float32 [8, 1536, 384], P('expert', 'dp'), may hold values from -6 to 6
- second_in: float32 [8, 384, 1536], P('expert', 'dp'), may hold values from 0.01 to 1
- second_out: float32 [8, 1536, 384], P('expert', 'dp'), may hold values from 0.01 to 1
Outputs:
- block_out: bfloat16 [256, 197, 384], P(('dp', 'expert'))
- images_grad: bfloat16 [256, 197, 384], P(('dp', 'expert'))
- norm1_gain_grad: float32 [384], replicated
- norm1_shift_grad: float32 [384], replicated
- query_weight_grad: float32 [384, 384], replicated
- query_bias_grad: float32 [384], replicated
- key_weight_grad: float32 [384, 384], replicated
- value_weight_grad: float32 [384, 384], replicated
- value_bias_grad: float32 [384], replicated
- output_weight_grad: float32 [384, 384], replicated
- output_bias_grad: float32 [384], replicated
- norm2_gain_grad: float32 [384], replicated
- norm2_shift_grad: float32 [384], replicated
- router_weight_grad: float32 [384, 8], replicated
- new_expert_in: bfloat16 [8, 384, 1536], P('expert')
- new_expert_out: bfloat16 [8, 1536, 384], P('expert')
- new_master_in: float32 [8, 384, 1536], P('expert', 'dp')
- new_master_out: float32 [8, 1536, 384], P('expert', 'dp')
- new_moment_in: float32 [8, 384, 1536], P('expert', 'dp')
- new_moment_out: float32 [8, 1536, 384], P('expert', 'dp')
- new_second_in: float32 [8, 384, 1536], P('expert', 'dp')
- new_second_out: float32 [8, 1536, 384], P('expert', 'dp')
The draws below stay inside these ranges and needn't reach their ends.
Inputs may be any that keep to these rules, and one draw needn't show every extreme that they name: `routes`: each token names 2 different experts. `seat_order`: each row holds every number of 0 to 3151 once.
All inputs are finite; a program needn't handle non-finite values.
Results may differ from the reference program's by a relative error of at most 0.02.
Values may be sent and summed in bfloat16 or wider, within the bound.
No kernel may reach another device: no remote copies, remote signals or barrier semaphores. Data moves between devices by JAX's collectives and lax.ppermute only.
A program may use at most 256 MiB of HBM per device.

```python
import math
import jax
import jax.numpy as jnp
from jax import lax

D = 384
HEADS = 6
HEAD_DIM = 64
FF = 1536
SEQ = 197
TOP = 2
IMG_DEV = 8
EXPERTS = 8
TOK_DEV = 1576
PAIRS = 3152
CAP = 394
IMAGES = 256
N_DP = 4
N_EXPERT = 8
DEVICES = 32


def levels(own_key, dims, cuts, least, high):
    factor_of, own = 1.0, jax.random.fold_in(own_key, 6)
    for dim, shards_of in cuts:
        heights = jnp.exp(jax.random.uniform(jax.random.fold_in(own, dim), (shards_of,), jnp.float32, least / len(cuts), high / len(cuts)))
        factor_of = factor_of * jnp.repeat(heights, dims[dim] // shards_of).reshape([-1 if axis == dim else 1 for axis in range(len(dims))])
    return factor_of


def picks_of(stream_key, rows, number_of, top, lift):
    sequence = jax.random.permutation(jax.random.fold_in(stream_key, 1), number_of)
    pull = sequence
    for power in range(3):
        pull = pull * pull // number_of
    pull = pull * lift // number_of
    tickets = jax.random.randint(jax.random.fold_in(stream_key, 2), (rows, number_of), 0, 4096) + pull
    holders = jax.random.permutation(jax.random.fold_in(stream_key, 3), rows)[jnp.arange(number_of) % rows]
    tickets = jnp.where(jnp.arange(rows)[:, None] == holders[None, :], 1 << 14, tickets)
    priority = tickets * number_of + jnp.arange(number_of)
    return lax.top_k(priority.astype(jnp.int32), top)[1].astype(jnp.int32)


def noise(own_key, shape, spread, limit, pieces=(), kind=jnp.bfloat16):
    array = jax.random.normal(own_key, shape, jnp.float32) * spread
    if len(pieces) > 0:
        array = levels(own_key, shape, pieces, -0.22, 0.18) * array
    return jnp.clip(array, min=-limit, max=limit).astype(kind)


def setup_inputs(seed: int = 0) -> dict:
    seeds = jax.random.split(jax.random.key(seed), 26)
    return {
        "images": noise(seeds[0], (IMAGES, SEQ, D), 1.0, 6.0, ((0, 32),)),
        "cotangent": noise(seeds[1], (IMAGES, SEQ, D), 1.0, 6.0, ((0, 32),)),
        "router_noise": noise(seeds[2], (IMAGES, SEQ, EXPERTS), 0.5, 3.0, ((0, 32),), jnp.float32),
        "routes": picks_of(seeds[3], IMAGES * SEQ, EXPERTS, TOP, 2048).reshape((IMAGES, SEQ, TOP)),
        "seat_order": jax.vmap(lambda own: jax.random.permutation(own, PAIRS))(jax.random.split(seeds[4], DEVICES)).reshape((DEVICES, PAIRS)).astype(jnp.int32),
        "norm1_gain": jnp.clip(1.0 + 0.1 * jax.random.normal(seeds[5], (D,), jnp.float32), 0.5, 1.5),
        "norm1_shift": noise(seeds[6], (D,), 0.2, 1.0, (), jnp.float32),
        "query_weight": noise(seeds[7], (D, D), D ** -0.5, 0.3125),
        "query_bias": noise(seeds[8], (D,), 0.2, 1.0, (), jnp.float32),
        "key_weight": noise(seeds[9], (D, D), D ** -0.5, 0.3125),
        "value_weight": noise(seeds[10], (D, D), D ** -0.5, 0.3125),
        "value_bias": noise(seeds[11], (D,), 0.2, 1.0, (), jnp.float32),
        "output_weight": noise(seeds[12], (D, D), (D // 64) ** -0.5, 2.5),
        "output_bias": noise(seeds[13], (D,), 0.2, 1.0, (), jnp.float32),
        "norm2_gain": jnp.clip(1.0 + 0.1 * jax.random.normal(seeds[14], (D,), jnp.float32), 0.5, 1.5),
        "norm2_shift": noise(seeds[15], (D,), 0.2, 1.0, (), jnp.float32),
        "router_weight": noise(seeds[16], (D, EXPERTS), 0.03, 0.1796875),
        "expert_in": noise(seeds[17], (EXPERTS, D, FF), D ** -0.5, 0.3125, ((0, 8),)),
        "expert_out": noise(seeds[18], (EXPERTS, FF, D), (max(FF // 256, 1)) ** -0.5, 2.5, ((0, 8),)),
        "master_in": noise(seeds[19], (EXPERTS, D, FF), D ** -0.5, 0.3125, ((0, 8), (1, 4)), jnp.float32),
        "master_out": noise(seeds[20], (EXPERTS, FF, D), FF ** -0.5, 0.15625, ((0, 8), (1, 4)), jnp.float32),
        "moment_in": noise(seeds[21], (EXPERTS, D, FF), 1.0, 6.0, ((0, 8), (1, 4)), jnp.float32),
        "moment_out": noise(seeds[22], (EXPERTS, FF, D), 1.0, 6.0, ((0, 8), (1, 4)), jnp.float32),
        "second_in": jnp.clip(jnp.exp(math.log(1.0) - 4.6051702 * jax.random.uniform(seeds[23], (EXPERTS, D, FF), jnp.float32) ** levels(seeds[23], (EXPERTS, D, FF), ((0, 8), (1, 4)), -0.2, 0.2)), 0.01, 1.0),
        "second_out": jnp.clip(jnp.exp(math.log(1.0) - 4.6051702 * jax.random.uniform(seeds[24], (EXPERTS, FF, D), jnp.float32) ** levels(seeds[24], (EXPERTS, FF, D), ((0, 8), (1, 4)), -0.2, 0.2)), 0.01, 1.0),
    }


@jax.custom_vjp
def low(v):
    return lax.optimization_barrier(v.astype(jnp.bfloat16)).astype(jnp.float32)

@jax.custom_vjp
def low_back(v):
    return v

def low_keep(v):
    return (low(v), None)

def low_pass(kept, grad):
    return (grad,)

def back_keep(v):
    return (v, None)

def back_low(kept, grad):
    return (low(grad),)
low.defvjp(low_keep, low_pass)
low_back.defvjp(back_keep, back_low)
HIGH = lax.Precision.HIGHEST
EPS_NORM = 1e-06
BETA_ONE = 0.9
BETA_TWO = 0.999
LEARN_RATE = 0.03
ADAM_EPS = 1e-08
adam_steps = 100.0

def layer_norm(values, gain, shift):
    mean = lax.optimization_barrier(jnp.mean(values, axis=-1, keepdims=True))
    centred = values - mean
    return centred * lax.rsqrt(lax.optimization_barrier(jnp.mean(centred * centred, axis=-1, keepdims=True)) + EPS_NORM) * gain + shift

def softmax_rows(values):
    peak = lax.optimization_barrier(jnp.max(values, axis=-1, keepdims=True))
    expo = jnp.exp(values - peak)
    return expo / lax.optimization_barrier(jnp.sum(expo, axis=-1, keepdims=True))

def front(x_dev, noise_dev, params):
    gain_one, shift_one, w_query, b_query, w_key, w_value, b_value, w_output, b_output, gain_two, shift_two, w_router = params
    normed = low(layer_norm(x_dev, gain_one, shift_one))
    queries = low_back(low(jnp.dot(normed, w_query, precision=HIGH) + b_query))
    keys_all = low_back(low(jnp.dot(normed, w_key, precision=HIGH)))
    values_all = low_back(low(jnp.dot(normed, w_value, precision=HIGH) + b_value))
    split = (IMG_DEV, SEQ, HEADS, HEAD_DIM)
    scores = low_back(jnp.einsum('ishd,ithd->ihst', queries.reshape(split), keys_all.reshape(split), precision=HIGH) * HEAD_DIM ** (-0.5))
    weights = low(softmax_rows(scores))
    mixed = low_back(low(jnp.einsum('ihst,ithd->ishd', weights, values_all.reshape(split), precision=HIGH).reshape(TOK_DEV, D)))
    branch = low_back(jnp.dot(mixed, w_output, precision=HIGH) + b_output)
    state = x_dev + branch
    routed = low(layer_norm(state, gain_two, shift_two))
    logits = low_back(jnp.dot(routed, w_router, precision=HIGH)) + noise_dev
    return (state, routed, softmax_rows(logits))

def expert_rows(rows, weight_in, weight_out):
    pre_act = low_back(jnp.dot(rows, weight_in, precision=HIGH))
    activated = low(jax.nn.gelu(pre_act, approximate=True))
    return low_back(low(jnp.dot(activated, weight_out, precision=HIGH)))

def seating(route_dev, order_dev):
    same = route_dev[:, None] == route_dev[None, :]
    earlier = order_dev[None, :] < order_dev[:, None]
    position = lax.optimization_barrier(jnp.sum((same & earlier).astype(jnp.int32), axis=1))
    seated = position < CAP
    slot = route_dev * CAP + jnp.minimum(position, CAP - 1)
    slot_ids = jnp.arange(EXPERTS * CAP, dtype=jnp.int32)
    match = (slot[None, :] == slot_ids[:, None]) & seated[None, :]
    token_of = jnp.arange(PAIRS, dtype=jnp.int32) // TOP
    slot_token = lax.optimization_barrier(jnp.sum(jnp.where(match, token_of[None, :], 0), axis=1)).astype(jnp.int32)
    slot_live = jnp.any(match, axis=1)
    return (slot.astype(jnp.int32), seated, slot_token, slot_live)

def forward(x_all, params, w_in, w_out, noise_all, tables):
    slot, seated, slot_token, slot_live, route_all = tables

    def front_one(pair):
        return front(pair[0], pair[1], params)
    state, routed, gate_probs = lax.map(jax.checkpoint(front_one), (x_all, noise_all))
    expert_iota = jnp.arange(EXPERTS, dtype=jnp.int32)
    route_hot = route_all[..., None] == expert_iota
    gate_pair = lax.optimization_barrier(jnp.sum(jnp.where(route_hot, gate_probs[:, :, None, :], 0.0), axis=3))
    gates = low(gate_pair * seated)
    rows = jnp.take_along_axis(routed, slot_token[:, :, None], axis=1) * slot_live[:, :, None]
    rows = low_back(rows)
    grouped = rows.reshape(N_DP, N_EXPERT, EXPERTS, CAP, D).transpose(0, 2, 1, 3, 4)
    grouped = grouped.reshape(N_DP, EXPERTS, N_EXPERT * CAP, D)

    def one_expert(item):
        return expert_rows(item[0], item[1], item[2])

    def one_group(group_rows):
        return lax.map(jax.checkpoint(one_expert), (group_rows, w_in, w_out))
    produced = lax.map(jax.checkpoint(one_group), grouped)
    per_device = produced.reshape(N_DP, EXPERTS, N_EXPERT, CAP, D).transpose(0, 2, 1, 3, 4)
    per_device = per_device.reshape(DEVICES, EXPERTS * CAP, D)
    picked = jnp.take_along_axis(per_device, slot[:, :, None], axis=1).reshape(DEVICES, TOK_DEV, TOP, D)
    return state + lax.optimization_barrier(jnp.sum(gates[..., None] * picked, axis=2))

def adam(master, moment, second, grad):
    new_moment = BETA_ONE * moment + (1.0 - BETA_ONE) * grad
    new_second = BETA_TWO * second + (1.0 - BETA_TWO) * grad * grad
    corr_one = 1.0 - BETA_ONE ** adam_steps
    corr_two = 1.0 - BETA_TWO ** adam_steps
    update = LEARN_RATE * (new_moment / corr_one) / (jnp.sqrt(new_second / corr_two) + ADAM_EPS)
    return (master - update, new_moment, new_second)

def reference(images, cotangent, router_noise, routes, seat_order, norm1_gain, norm1_shift, query_weight, query_bias, key_weight, value_weight, value_bias, output_weight, output_bias, norm2_gain, norm2_shift, router_weight, expert_in, expert_out, master_in, master_out, moment_in, moment_out, second_in, second_out):
    f32 = jnp.float32
    x_all = images.astype(f32).reshape(DEVICES, TOK_DEV, D)
    noise_all = router_noise.astype(f32).reshape(DEVICES, TOK_DEV, EXPERTS)
    route_all = routes.reshape(DEVICES, TOK_DEV, TOP)
    slot, seated, slot_token, slot_live = lax.map(lambda pair: seating(pair[0], pair[1]), (routes.reshape(DEVICES, PAIRS), seat_order))
    tables = (slot, seated.reshape(DEVICES, TOK_DEV, TOP).astype(f32), slot_token, slot_live.astype(f32), route_all)
    params = (norm1_gain, norm1_shift, query_weight.astype(f32), query_bias, key_weight.astype(f32), value_weight.astype(f32), value_bias, output_weight.astype(f32), output_bias, norm2_gain, norm2_shift, router_weight.astype(f32))

    def run(x_in, param_set, w_in, w_out):
        return forward(x_in, param_set, w_in, w_out, noise_all, tables)
    result, pullback = jax.vjp(run, x_all, params, expert_in.astype(f32), expert_out.astype(f32))
    grad_x, grad_params, grad_in, grad_out = pullback(cotangent.astype(f32).reshape(DEVICES, TOK_DEV, D))
    new_master_in, new_moment_in, new_second_in = adam(master_in, moment_in, second_in, grad_in)
    new_master_out, new_moment_out, new_second_out = adam(master_out, moment_out, second_out, grad_out)
    block_out = result.astype(jnp.bfloat16).reshape(IMAGES, SEQ, D)
    images_grad = grad_x.astype(jnp.bfloat16).reshape(IMAGES, SEQ, D)
    return (block_out, images_grad, grad_params[0], grad_params[1], grad_params[2], grad_params[3], grad_params[4], grad_params[5], grad_params[6], grad_params[7], grad_params[8], grad_params[9], grad_params[10], grad_params[11], new_master_in.astype(jnp.bfloat16), new_master_out.astype(jnp.bfloat16), new_master_in, new_master_out, new_moment_in, new_moment_out, new_second_in, new_second_out)
```

```python
import functools

import jax
import jax.numpy as jnp
from jax import lax
from jax.experimental import pallas as pl
from jax.experimental.pallas import tpu as pltpu
from jax.sharding import PartitionSpec as P

HEADS = 6
EPS_NORM = 1e-06
BETA_ONE = 0.9
BETA_TWO = 0.999
LEARN_RATE = 0.03
ADAM_EPS = 1e-08
adam_steps = 100.0

lowp = jnp.bfloat16
wide = jnp.float32
LANES = 128
HALF = 64
VMEM_BYTES = 56 * 1024 * 1024


def round_up(value, step):
    return (value + step - 1) // step * step


def dot(left, right):
    return jnp.dot(left, right, preferred_element_type=wide)


def dot_nt(left, right):
    return lax.dot_general(left, right, (((1,), (1,)), ((), ())), preferred_element_type=wide)


def dot_tn(left, right):
    return lax.dot_general(left, right, (((0,), (0,)), ((), ())), preferred_element_type=wide)


def iota(shape, dim):
    return lax.broadcasted_iota(jnp.int32, shape, dim)


def params(dims):
    return pltpu.CompilerParams(
        dimension_semantics=("arbitrary",) * dims, vmem_limit_bytes=VMEM_BYTES
    )


def unit_norm(values):
    mean = jnp.mean(values, axis=-1, keepdims=True)
    centred = values - mean
    inverse = lax.rsqrt(jnp.mean(centred * centred, axis=-1, keepdims=True) + EPS_NORM)
    return centred * inverse, inverse


def norm_back(scaled, unit, inverse):
    return inverse * (
        scaled
        - jnp.mean(scaled, axis=-1, keepdims=True)
        - unit * jnp.mean(scaled * unit, axis=-1, keepdims=True)
    )


def column_to_row(column, width, offset):
    shape = (column.shape[0], width)
    hit = iota(shape, 0) == iota(shape, 1) + offset
    return jnp.sum(jnp.where(hit, column, 0.0), axis=0, keepdims=True)


def row_to_column(row, rows, offset):
    shape = (rows, row.shape[1])
    hit = iota(shape, 0) == iota(shape, 1) + offset
    return jnp.sum(jnp.where(hit, row, 0.0), axis=1, keepdims=True)


def token_hits(table_ref, chunk, rows, tokens):
    slot = iota((rows, LANES), 0)
    lane = iota((rows, LANES), 1)
    picked = jnp.zeros((rows, LANES), wide)
    for high in range((rows + HALF - 1) // HALF):
        line = table_ref[pl.ds(chunk * 8 + high, 1), :]
        picked = jnp.where(slot // HALF == high, line, picked)
    picked = jnp.where(slot % HALF == lane % HALF, picked, 0.0)
    picked = picked * jnp.where(lane < HALF, float(HALF), 1.0)
    token = jnp.sum(picked, axis=1, keepdims=True).astype(jnp.int32) - 1
    return jnp.where(token == iota((rows, tokens), 1), 1.0, 0.0).astype(lowp)


def seat_kernel(experts, cap, cap_rows, seq_rows,
                routes_ref, order_ref, cot_ref, slots_ref, table_ref, rows_ref,
                route_s, order_s, flat_s):
    images, seq, _ = routes_ref.shape
    tokens = images * seq_rows
    step = pl.program_id(0)

    @pl.when(step == 0)
    def _():
        route_s[...] = jnp.full(route_s.shape, -1, jnp.int32)
        order_s[...] = jnp.zeros(order_s.shape, jnp.int32)
        flat_s[...] = jnp.zeros(flat_s.shape, lowp)
        for image in range(images):
            rows = pl.ds(image * seq_rows, seq)
            route_s[rows, :] = routes_ref[image]
            order_s[rows, :] = order_ref[image]
            flat_s[rows, :] = cot_ref[image]
        lane = iota((tokens, LANES), 1)
        wide_lane = iota((tokens, experts * HALF), 1)
        route = [route_s[:, k : k + 1] for k in range(2)]
        order = [order_s[:, k : k + 1] for k in range(2)]
        low_hit = [(order[k] % HALF == lane % HALF) for k in range(2)]
        low_b = [jnp.where(low_hit[k], 1.0, 0.0).astype(lowp) for k in range(2)]
        high_b = [
            jnp.where((route[k] * HALF + order[k] // HALF) == wide_lane, 1.0, 0.0).astype(lowp)
            for k in range(2)
        ]
        counts = (dot_tn(low_b[0], high_b[0]) + dot_tn(low_b[1], high_b[1])).astype(lowp)
        before = iota((LANES, LANES), 0)
        after = iota((LANES, LANES), 1)
        upper = jnp.where((after < HALF) & (after < before % HALF), 1.0, 0.0).astype(lowp)
        within = dot(upper, counts)
        block = (experts * HALF, experts * HALF)
        earlier = jnp.where(
            (iota(block, 0) // HALF == iota(block, 1) // HALF) & (iota(block, 0) < iota(block, 1)),
            1.0, 0.0,
        ).astype(lowp)
        base = jnp.sum(dot(counts, earlier)[:HALF], axis=0, keepdims=True)
        place = within + base
        place_high = jnp.floor(place * (1.0 / HALF))
        place_low = place - place_high * HALF
        split = jnp.where(iota(place.shape, 0) < HALF, place_high, place_low).astype(lowp)
        weight = jnp.where(lane < HALF, float(HALF), 1.0)
        token = iota((tokens, LANES), 0) + 1
        table = jnp.zeros((experts * 8, LANES), wide)
        row = iota((tokens, experts * 8), 1)
        columns = iota((tokens, 4), 1)
        found = jnp.zeros((tokens, 4), jnp.int32)
        for k in range(2):
            gathered = dot_nt(high_b[k], split)
            position = jnp.sum(
                jnp.where(low_hit[k], gathered * weight, 0.0), axis=1, keepdims=True
            ).astype(jnp.int32)
            seated = (position < cap) & (route[k] >= 0)
            slot = jnp.where(seated, route[k] * cap_rows + position, -1)
            found = jnp.where(columns == k, slot, found)
            found = jnp.where(columns == 2 + k, route[k], found)
            which = jnp.where(seated, route[k] * 8 + position // HALF, -1)
            which_b = jnp.where(which == row, 1.0, 0.0).astype(lowp)
            value = jnp.where(lane < HALF, token // HALF, token % HALF).astype(wide)
            value_b = jnp.where(position % HALF == lane % HALF, value, 0.0).astype(lowp)
            table = table + dot_tn(which_b, value_b)
        table_ref[...] = table
        for image in range(images):
            slots_ref[image] = found[image * seq_rows : (image + 1) * seq_rows]

    hits = token_hits(table_ref, step, cap_rows, tokens)
    rows_ref[0] = dot(hits, flat_s[...]).astype(lowp)


def front_kernel(seq, experts,
                 me_ref, x_ref, noise_ref, vec_ref, wq_ref, wk_ref, wv_ref, wo_ref, wr_ref,
                 q_ref, k_ref, v_ref, lse_ref, mix_ref, state_ref, aug_ref, probs_ref,
                 x_s, noise_s):
    rows, width = x_s.shape

    @pl.when(pl.program_id(0) == 0)
    def _():
        x_s[...] = jnp.zeros(x_s.shape, wide)
        noise_s[...] = jnp.zeros(noise_s.shape, wide)

    x_s[0:seq, :] = x_ref[0].astype(wide)
    noise_s[0:seq, :] = noise_ref[0]
    x = x_s[...]
    unit, _ = unit_norm(x)
    normed = (unit * vec_ref[0:1, :] + vec_ref[1:2, :]).astype(lowp)
    head_size = width // HEADS
    query = (dot(normed, wq_ref[...]) + vec_ref[2:3, :]).astype(lowp)
    query = query * (head_size ** -0.5)
    key = dot(normed, wk_ref[...]).astype(lowp)
    value = (dot(normed, wv_ref[...]) + vec_ref[3:4, :]).astype(lowp)
    q_ref[0] = query
    k_ref[0] = key
    v_ref[0] = value
    live = iota((rows, rows), 1) < seq
    lane = iota((rows, LANES), 1)
    lse_all = jnp.zeros((rows, LANES), wide)
    mixed = []
    for pair in range(HEADS // 2):
        cols = slice(pair * LANES, (pair + 1) * LANES)
        q2, k2, v2 = query[:, cols], key[:, cols], value[:, cols]
        outs = []
        for half in range(2):
            mine = (lane < HALF) if half == 0 else (lane >= HALF)
            scores = dot_nt(jnp.where(mine, q2, jnp.zeros_like(q2)), k2)
            scores = jnp.where(live, scores, -1e30)
            peak = jnp.max(scores, axis=1, keepdims=True)
            expo = jnp.exp(scores - peak)
            total = jnp.sum(expo, axis=1, keepdims=True)
            lse_all = jnp.where(lane == pair * 2 + half, peak + jnp.log(total), lse_all)
            outs.append(dot((expo / total).astype(lowp), v2))
        mixed.append(jnp.where(lane < HALF, outs[0], outs[1]).astype(lowp))
    mixed = jnp.concatenate(mixed, axis=1)
    lse_ref[0] = lse_all
    mix_ref[0] = mixed
    state = x + dot(mixed, wo_ref[...]) + vec_ref[4:5, :]
    state_ref[0] = state
    unit_two, _ = unit_norm(state)
    routed = (unit_two * vec_ref[5:6, :] + vec_ref[6:7, :]).astype(lowp)
    logits = dot(routed, wr_ref[...]) + noise_s[...]
    top = jnp.max(logits, axis=1, keepdims=True)
    expo = jnp.exp(logits - top)
    probs = expo / jnp.sum(expo, axis=1, keepdims=True)
    probs_ref[0] = probs
    me = me_ref[0]
    shape = (experts, LANES)
    swap = jnp.where(iota(shape, 0) == (iota(shape, 1) ^ me), 1.0, 0.0).astype(lowp)
    aug_ref[0, :, 0:width] = routed
    aug_ref[0, :, width : width + LANES] = dot(probs.astype(lowp), swap).astype(lowp)


def send_kernel(cap, gate_rows, table_ref, aug_ref, out_ref):
    _, cap_rows, width = out_ref.shape
    tokens = aug_ref.shape[0]
    chunk = pl.program_id(0)
    hits = token_hits(table_ref, chunk, cap_rows, tokens)
    full = dot(hits, aug_ref[...])
    rows = full[:, 0:width]
    lane = iota((cap_rows, LANES), 1)
    gate = jnp.sum(jnp.where(lane == chunk, full[:, width:], 0.0), axis=1, keepdims=True)
    at = iota((cap_rows, width), 0)
    for part in range(gate_rows):
        line = column_to_row(gate, width, part * width)
        rows = jnp.where(at == cap + part, line, rows)
    out_ref[0] = rows.astype(lowp)


def expert_kernel(cap, gate_rows, blocks, x_ref, g_ref, win_ref, wout_ref,
                  back_ref, prod_ref, act_ref, pre_ref, slot_ref):
    _, cap_rows, width = x_ref.shape
    inner = win_ref.shape[1]
    x = x_ref[0]
    grad = g_ref[0].astype(wide)
    gate = jnp.zeros((cap_rows, 1), wide)
    for part in range(gate_rows):
        line = x_ref[0, cap + part : cap + part + 1, :].astype(wide)
        gate = gate + row_to_column(line, cap_rows, part * width)
    gate = jnp.where(iota((cap_rows, 1), 0) < cap, gate, 0.0)
    slot_grad = (gate * grad).astype(lowp)
    slot_ref[...] = slot_grad
    made = jnp.zeros((cap_rows, width), wide)
    back = jnp.zeros((cap_rows, width), wide)
    size = inner // blocks
    outer = (2.0 / jnp.pi) ** 0.5
    for block in range(blocks):
        cols = slice(block * size, (block + 1) * size)
        win = win_ref[:, cols]
        wout = wout_ref[cols, :]
        pre = dot(x, win)
        hidden = dot_nt(slot_grad, wout)
        square = pre * pre
        angle = pre * (outer + (outer * 0.044715) * square)
        half = 0.5 * jnp.tanh(angle) + 0.5
        act = (pre * half).astype(lowp)
        slope = half * (
            1.0 + (1.0 - half) * (pre * (2.0 * outer + (6.0 * outer * 0.044715) * square))
        )
        pre_grad = (hidden * slope).astype(lowp)
        act_ref[:, cols] = act
        pre_ref[:, cols] = pre_grad
        made = made + dot(act, wout)
        back = back + dot_nt(pre_grad, win)
    made_b = made.astype(lowp)
    prod_ref[0] = made_b
    gate_grad = jnp.sum(grad * made_b.astype(wide), axis=1, keepdims=True)
    at = iota((cap_rows, width), 0)
    for part in range(gate_rows):
        line = column_to_row(gate_grad, width, part * width)
        high = line.astype(lowp).astype(wide)
        back = jnp.where(at == cap + part, high, back)
        back = jnp.where(at == cap + gate_rows + part, line - high, back)
    back_ref[0] = back.astype(lowp)


def weight_kernel(x_ref, slot_ref, act_ref, pre_ref, din_ref, dout_ref, in_s, out_s):
    step = pl.program_id(0)

    @pl.when(step == 0)
    def _():
        in_s[...] = jnp.zeros(in_s.shape, wide)
        out_s[...] = jnp.zeros(out_s.shape, wide)

    in_s[...] += dot_tn(x_ref[...], pre_ref[...])
    out_s[...] += dot_tn(slot_ref[...], act_ref[...])

    @pl.when(step == pl.num_programs(0) - 1)
    def _():
        din_ref[...] = in_s[...].astype(lowp)
        dout_ref[...] = out_s[...].T.astype(lowp)


def slot_hits(slots_ref, shape):
    at = iota(shape, 1)
    return slots_ref[0, :, 0:1] == at, slots_ref[0, :, 1:2] == at


def back_kernel(seq, experts, cap, cap_rows, gate_rows,
                me_ref, slots_ref, x_ref, cot_ref, q_ref, k_ref, v_ref, lse_ref, mix_ref,
                state_ref, probs_ref, vec_ref, rows_ref, wq_ref, wk_ref, wv_ref, wo_ref, wr_ref,
                grad_ref, sums_ref, small_ref,
                x_s, cot_s, aug_s):
    step = pl.program_id(0)
    rows, width = x_s.shape
    slot_total = experts * cap_rows

    @pl.when(step == 0)
    def _():
        x_s[...] = jnp.zeros(x_s.shape, wide)
        cot_s[...] = jnp.zeros(cot_s.shape, wide)
        sums_ref[...] = jnp.zeros(sums_ref.shape, wide)
        small_ref[...] = jnp.zeros(small_ref.shape, wide)

        @pl.loop(0, experts)
        def _(chunk):
            lane = iota((cap_rows, LANES), 1)
            extra = jnp.zeros((cap_rows, LANES), wide)
            for part in range(gate_rows):
                for piece in range(2):
                    line = rows_ref[chunk, cap + piece * gate_rows + part :
                                    cap + piece * gate_rows + part + 1, :].astype(wide)
                    column = row_to_column(line, cap_rows, part * width)
                    extra = jnp.where(lane == chunk + piece * HALF, extra + column, extra)
            at = pl.ds(pl.multiple_of(chunk * cap_rows, 16), cap_rows)
            aug_s[at, 0:width] = rows_ref[chunk]
            aug_s[at, width : width + LANES] = extra.astype(lowp)

    x_s[0:seq, :] = x_ref[0].astype(wide)
    cot_s[0:seq, :] = cot_ref[0].astype(wide)
    first, second = slot_hits(slots_ref, (rows, slot_total))
    hits = jnp.where(first | second, 1.0, 0.0).astype(lowp)
    full = dot(hits, aug_s[...])
    me = me_ref[0]
    shape = (LANES, experts)
    swap = jnp.where((iota(shape, 0) % HALF) == (iota(shape, 1) ^ me), 1.0, 0.0).astype(lowp)
    prob_grad = dot(full[:, width:].astype(lowp), swap)
    probs = probs_ref[0]
    logit_grad = (
        probs * (prob_grad - jnp.sum(probs * prob_grad, axis=1, keepdims=True))
    ).astype(lowp)
    routed_grad = full[:, 0:width] + dot_nt(logit_grad, wr_ref[...])
    unit_two, inverse_two = unit_norm(state_ref[0])
    gain_two = vec_ref[5:6, :]
    routed = (unit_two * gain_two + vec_ref[6:7, :]).astype(lowp)
    router_grad = dot_tn(logit_grad, routed)
    state_grad = cot_s[...] + norm_back(routed_grad * gain_two, unit_two, inverse_two)
    branch = state_grad.astype(lowp)
    mixed_grad = dot_nt(branch, wo_ref[...]).astype(lowp)
    sums_ref[3 * width : 4 * width, :] += dot_tn(mix_ref[0], branch)

    query, key, value = q_ref[0], k_ref[0], v_ref[0]
    lse = lse_ref[0]
    live = iota((rows, rows), 1) < seq
    lane = iota((rows, LANES), 1)
    scale = (width // HEADS) ** -0.5
    parts = [[], [], []]
    for pair in range(HEADS // 2):
        cols = slice(pair * LANES, (pair + 1) * LANES)
        q2, k2, v2, g2 = query[:, cols], key[:, cols], value[:, cols], mixed_grad[:, cols]
        outs = [[], [], []]
        for half in range(2):
            mine = (lane < HALF) if half == 0 else (lane >= HALF)
            scores = dot_nt(jnp.where(mine, q2, jnp.zeros_like(q2)), k2)
            head = pair * 2 + half
            weights = jnp.exp(jnp.where(live, scores - lse[:, head : head + 1], -1e30))
            weight_grad = dot_nt(jnp.where(mine, g2, jnp.zeros_like(g2)), v2)
            product = weights * weight_grad
            score_grad = (
                product - weights * jnp.sum(product, axis=1, keepdims=True)
            ).astype(lowp)
            outs[0].append(dot(score_grad, k2))
            outs[1].append(dot_tn(score_grad, q2))
            outs[2].append(dot_tn(weights.astype(lowp), g2))
        for which in range(3):
            joined = jnp.where(lane < HALF, outs[which][0], outs[which][1])
            if which == 0:
                joined = joined * scale
            parts[which].append(joined.astype(lowp))
    query_grad, key_grad, value_grad = (jnp.concatenate(p, axis=1) for p in parts)
    unit_one, inverse_one = unit_norm(x_s[...])
    gain_one = vec_ref[0:1, :]
    normed = (unit_one * gain_one + vec_ref[1:2, :]).astype(lowp)
    sums_ref[0:width, :] += dot_tn(normed, query_grad)
    sums_ref[width : 2 * width, :] += dot_tn(normed, key_grad)
    sums_ref[2 * width : 3 * width, :] += dot_tn(normed, value_grad)
    normed_grad = (
        dot_nt(query_grad, wq_ref[...])
        + dot_nt(key_grad, wk_ref[...])
        + dot_nt(value_grad, wv_ref[...])
    )
    result = state_grad + norm_back(normed_grad * gain_one, unit_one, inverse_one)
    grad_ref[0] = result.astype(lowp)[0:seq]
    lines = [
        query_grad.astype(wide),
        value_grad.astype(wide),
        branch.astype(wide),
        normed_grad * unit_one,
        normed_grad,
        routed_grad * unit_two,
        routed_grad,
    ]
    small = jnp.concatenate(
        [jnp.sum(line, axis=0, keepdims=True) for line in lines]
        + [jnp.zeros((1, width), wide)], axis=0
    )
    small_ref[0:8, :] += small
    small_ref[8 : 8 + experts, :] += router_grad


def out_kernel(slots_ref, aug_ref, state_ref, rows_ref, out_ref):
    _, rows, width = state_ref.shape
    seq = out_ref.shape[1]
    slot_total = rows_ref.shape[0]
    lane = iota((rows, LANES), 1)
    gates = aug_ref[0, :, width : width + LANES].astype(wide)
    gate = [
        jnp.sum(jnp.where(lane == slots_ref[0, :, 2 + k : 3 + k], gates, 0.0), axis=1, keepdims=True)
        for k in range(2)
    ]
    first, second = slot_hits(slots_ref, (rows, slot_total))
    hits = jnp.where(first, gate[0], jnp.where(second, gate[1], 0.0)).astype(lowp)
    out_ref[0] = (state_ref[0] + dot(hits, rows_ref[...])).astype(lowp)[0:seq]


def adam_step(master, moment, second, grad):
    new_moment = BETA_ONE * moment + (1.0 - BETA_ONE) * grad
    new_second = BETA_TWO * second + (1.0 - BETA_TWO) * grad * grad
    corr_one = 1.0 - BETA_ONE**adam_steps
    corr_two = 1.0 - BETA_TWO**adam_steps
    update = LEARN_RATE * (new_moment / corr_one) / (jnp.sqrt(new_second / corr_two) + ADAM_EPS)
    return (master - update, new_moment, new_second)


def whole(shape):
    return pl.BlockSpec(shape, lambda i: (0,) * len(shape))


def one(shape):
    return pl.BlockSpec((1,) + shape, lambda i: (i,) + (0,) * len(shape))


def smem():
    return pl.BlockSpec(memory_space=pltpu.SMEM)


def like(shape, dtype):
    return jax.ShapeDtypeStruct(shape, dtype)


def sum_all(values, n_expert, n_dp):
    rows, width = values.shape
    part = rows // n_expert
    pieces = lax.all_to_all(
        values.reshape(n_expert, part, width), "expert", split_axis=0, concat_axis=0, tiled=True
    )
    mine = jnp.sum(pieces.astype(wide), axis=0).astype(lowp)
    others = [
        lax.ppermute(mine, "dp", [(i, (i + shift) % n_dp) for i in range(n_dp)])
        for shift in range(1, n_dp)
    ]
    total = mine.astype(wide)
    for other in others:
        total = total + other.astype(wide)
    return lax.all_gather(total.astype(lowp), "expert", axis=0, tiled=True)


def on_device(n_expert, n_dp, images, cotangent, router_noise, routes, seat_order,
              norm1_gain, norm1_shift, query_weight, query_bias, key_weight, value_weight,
              value_bias, output_weight, output_bias, norm2_gain, norm2_shift, router_weight,
              expert_in, expert_out, master_in, master_out, moment_in, moment_out,
              second_in, second_out):
    count, seq, width = images.shape
    experts = router_noise.shape[2]
    cap = (count * seq * 2 + experts - 1) // experts
    gate_rows = (cap + width - 1) // width
    cap_rows = round_up(cap + 2 * gate_rows, 16)
    seq_rows = round_up(seq, 16)
    tokens = count * seq_rows
    inner = expert_in.shape[2]
    slot_total = experts * cap_rows
    aug = width + LANES
    me = jnp.zeros((1,), jnp.int32)
    vecs = jnp.stack([norm1_gain, norm1_shift, query_bias, value_bias, output_bias,
                      norm2_gain, norm2_shift, norm2_shift])

    slots, table, grad_rows = pl.pallas_call(
        functools.partial(seat_kernel, experts, cap, cap_rows, seq_rows),
        grid=(experts,),
        in_specs=[whole(routes.shape), whole(routes.shape), whole(cotangent.shape)],
        out_specs=[whole((count, seq_rows, 4)), whole((experts * 8, LANES)),
                   one((cap_rows, width))],
        out_shape=[like((count, seq_rows, 4), jnp.int32), like((experts * 8, LANES), wide),
                   like((experts, cap_rows, width), lowp)],
        scratch_shapes=[pltpu.VMEM((tokens, 2), jnp.int32), pltpu.VMEM((tokens, 2), jnp.int32),
                        pltpu.VMEM((tokens, width), lowp)],
        compiler_params=params(1),
        name="seat",
    )(routes, seat_order.reshape(routes.shape), cotangent)
    grad_in = lax.all_to_all(grad_rows, "expert", split_axis=0, concat_axis=0, tiled=True)

    square = (width, width)
    token_shape = (count, seq_rows, width)
    query, key, value, lse, mixed, state, routed, probs = pl.pallas_call(
        functools.partial(front_kernel, seq, experts),
        grid=(count,),
        in_specs=[smem(), one((seq, width)), one((seq, experts)), whole((8, width)),
                  whole(square), whole(square), whole(square), whole(square),
                  whole((width, experts))],
        out_specs=[one((seq_rows, width))] * 3 + [
            one((seq_rows, LANES)), one((seq_rows, width)), one((seq_rows, width)),
            one((seq_rows, aug)), one((seq_rows, experts))],
        out_shape=[like(token_shape, lowp)] * 3 + [
            like((count, seq_rows, LANES), wide), like(token_shape, lowp),
            like(token_shape, wide), like((count, seq_rows, aug), lowp),
            like((count, seq_rows, experts), wide)],
        scratch_shapes=[pltpu.VMEM((seq_rows, width), wide),
                        pltpu.VMEM((seq_rows, experts), wide)],
        compiler_params=params(1),
        name="front",
    )(me, images, router_noise, vecs, query_weight, key_weight, value_weight, output_weight,
      router_weight)

    sent = pl.pallas_call(
        functools.partial(send_kernel, cap, gate_rows),
        grid=(experts,),
        in_specs=[whole((experts * 8, LANES)), whole((tokens, aug))],
        out_specs=one((cap_rows, width)),
        out_shape=like((experts, cap_rows, width), lowp),
        compiler_params=params(1),
        name="send",
    )(table, routed.reshape(tokens, aug))
    sent, grad_in = lax.optimization_barrier((sent, grad_in))
    arrived = lax.all_to_all(sent, "expert", split_axis=0, concat_axis=0, tiled=True)

    back, produced, act, pre_grad, slot_grad = pl.pallas_call(
        functools.partial(expert_kernel, cap, gate_rows, 3),
        grid=(experts,),
        in_specs=[one((cap_rows, width)), one((cap_rows, width)), whole((width, inner)),
                  whole((inner, width))],
        out_specs=[one((cap_rows, width)), one((cap_rows, width)),
                   pl.BlockSpec((cap_rows, inner), lambda i: (i, 0)),
                   pl.BlockSpec((cap_rows, inner), lambda i: (i, 0)),
                   pl.BlockSpec((cap_rows, width), lambda i: (i, 0))],
        out_shape=[like((experts, cap_rows, width), lowp), like((experts, cap_rows, width), lowp),
                   like((slot_total, inner), lowp), like((slot_total, inner), lowp),
                   like((slot_total, width), lowp)],
        compiler_params=params(1),
        name="expert",
    )(arrived, grad_in, expert_in[0], expert_out[0])

    back_rows = lax.all_to_all(back, "expert", split_axis=0, concat_axis=0, tiled=True)

    steps = 4
    per = slot_total // steps
    row_block = lambda size: pl.BlockSpec((per, size), lambda i: (i, 0))
    grad_weight_in, grad_weight_out = pl.pallas_call(
        weight_kernel,
        grid=(steps,),
        in_specs=[row_block(width), row_block(width), row_block(inner), row_block(inner)],
        out_specs=[whole((width, inner)), whole((inner, width))],
        out_shape=[like((width, inner), lowp), like((inner, width), lowp)],
        scratch_shapes=[pltpu.VMEM((width, inner), wide), pltpu.VMEM((width, inner), wide)],
        compiler_params=params(1),
        name="weight",
    )(arrived.reshape(slot_total, width), slot_grad, act, pre_grad)

    back_rows, grad_weight_in, grad_weight_out = lax.optimization_barrier(
        (back_rows, grad_weight_in, grad_weight_out))
    share_in = lax.psum_scatter(grad_weight_in[None], "dp", scatter_dimension=1, tiled=True)
    share_out = lax.psum_scatter(grad_weight_out[None], "dp", scatter_dimension=1, tiled=True)
    returned = lax.all_to_all(produced, "expert", split_axis=0, concat_axis=0, tiled=True)

    small_rows = 8 + round_up(experts, 8)
    images_grad, sums, small = pl.pallas_call(
        functools.partial(back_kernel, seq, experts, cap, cap_rows, gate_rows),
        grid=(count,),
        in_specs=[smem(), one((seq_rows, 4)), one((seq, width)), one((seq, width))]
        + [one((seq_rows, width))] * 3
        + [one((seq_rows, LANES)), one((seq_rows, width)), one((seq_rows, width)),
           one((seq_rows, experts)), whole((8, width)), whole((experts, cap_rows, width)),
           whole(square), whole(square), whole(square), whole(square), whole((width, experts))],
        out_specs=[one((seq, width)), whole((4 * width, width)), whole((small_rows, width))],
        out_shape=[like(images.shape, lowp), like((4 * width, width), wide),
                   like((small_rows, width), wide)],
        scratch_shapes=[pltpu.VMEM((seq_rows, width), wide), pltpu.VMEM((seq_rows, width), wide),
                        pltpu.VMEM((slot_total, aug), lowp)],
        compiler_params=params(1),
        name="back",
    )(me, slots, images, cotangent, query, key, value, lse, mixed, state, probs, vecs, back_rows,
      query_weight, key_weight, value_weight, output_weight, router_weight)

    block_out = pl.pallas_call(
        out_kernel,
        grid=(count,),
        in_specs=[one((seq_rows, 4)), one((seq_rows, aug)), one((seq_rows, width)),
                  whole((slot_total, width))],
        out_specs=one((seq, width)),
        out_shape=like(images.shape, lowp),
        compiler_params=params(1),
        name="block_out",
    )(slots, routed, state, returned.reshape(slot_total, width))

    small_high = small.astype(lowp)
    small_low = (small - small_high.astype(wide)).astype(lowp)
    packed = jnp.concatenate([sums.astype(lowp), small_high, small_low], axis=0)
    packed_rows = packed.shape[0]
    packed = jnp.pad(packed, ((0, round_up(packed_rows, 16 * n_expert) - packed_rows), (0, 0)))
    total = sum_all(packed, n_expert, n_dp)
    big = total[0 : 4 * width].astype(wide).reshape(4, width, width)
    small_sum = (total[4 * width : 4 * width + small_rows].astype(wide)
                 + total[4 * width + small_rows : 4 * width + 2 * small_rows].astype(wide))

    new_master_in, new_moment_in, new_second_in = adam_step(
        master_in, moment_in, second_in, share_in.astype(wide))
    new_master_out, new_moment_out, new_second_out = adam_step(
        master_out, moment_out, second_out, share_out.astype(wide))
    new_expert_in = lax.all_gather(new_master_in.astype(lowp), "dp", axis=1, tiled=True)
    new_expert_out = lax.all_gather(new_master_out.astype(lowp), "dp", axis=1, tiled=True)
    return (
        block_out,
        images_grad,
        small_sum[3],
        small_sum[4],
        big[0],
        small_sum[0],
        big[1],
        big[2],
        small_sum[1],
        big[3],
        small_sum[2],
        small_sum[5],
        small_sum[6],
        small_sum[8 : 8 + experts].T,
        new_expert_in,
        new_expert_out,
        new_master_in,
        new_master_out,
        new_moment_in,
        new_moment_out,
        new_second_in,
        new_second_out,
    )


def solution(mesh):
    both = ("dp", "expert")
    in_specs = (
        (P(both, None, None),) * 4
        + (P(both, None),)
        + (P(),) * 12
        + (P("expert", None, None),) * 2
        + (P("expert", "dp", None),) * 6
    )
    out_specs = (
        (P(both, None, None),) * 2
        + (P(),) * 12
        + (P("expert", None, None),) * 2
        + (P("expert", "dp", None),) * 6
    )
    body = functools.partial(on_device, mesh.shape["expert"], mesh.shape["dp"])
    return jax.shard_map(body, mesh=mesh, in_specs=in_specs, out_specs=out_specs, check_vma=False)
```

```python
import functools

import jax
import jax.numpy as jnp
from jax import lax
from jax.experimental import pallas as pl
from jax.experimental.pallas import tpu as pltpu
from jax.sharding import PartitionSpec as P

HEADS = 6
EPS_NORM = 1e-06
BETA_ONE = 0.9
BETA_TWO = 0.999
LEARN_RATE = 0.03
ADAM_EPS = 1e-08
adam_steps = 100.0

lowp = jnp.bfloat16
wide = jnp.float32
LANES = 128
HALF = 64
SHIFT = 6
PACK = 2


def round_up(value, step):
    return (value + step - 1) // step * step


def dot(left, right):
    return jnp.dot(left, right, preferred_element_type=wide)


def dot_nt(left, right):
    return lax.dot_general(left, right, (((1,), (1,)), ((), ())), preferred_element_type=wide)


def dot_tn(left, right):
    return lax.dot_general(left, right, (((0,), (0,)), ((), ())), preferred_element_type=wide)


def iota(shape, dim):
    return lax.broadcasted_iota(jnp.int32, shape, dim)


def cost(micros):
    return pl.CostEstimate(
        flops=int(micros * 1.1e9), bytes_accessed=int(micros * 3.5e6), transcendentals=0
    )


def params(dims, megabytes=24):
    return pltpu.CompilerParams(
        dimension_semantics=("arbitrary",) * dims, vmem_limit_bytes=megabytes * 1024 * 1024
    )


def unit_norm(values):
    mean = jnp.mean(values, axis=-1, keepdims=True)
    centred = values - mean
    inverse = lax.rsqrt(jnp.mean(centred * centred, axis=-1, keepdims=True) + EPS_NORM)
    return centred * inverse, inverse


def norm_back(scaled, unit, inverse):
    return inverse * (
        scaled
        - jnp.mean(scaled, axis=-1, keepdims=True)
        - unit * jnp.mean(scaled * unit, axis=-1, keepdims=True)
    )


def column_to_row(column, width, offset):
    shape = (column.shape[0], width)
    hit = iota(shape, 0) == iota(shape, 1) + offset
    return jnp.sum(jnp.where(hit, column, 0.0), axis=0, keepdims=True)


def row_to_column(row, rows, offset):
    shape = (rows, row.shape[1])
    hit = iota(shape, 0) == iota(shape, 1) + offset
    return jnp.sum(jnp.where(hit, row, 0.0), axis=1, keepdims=True)


def token_hits(table_ref, chunk, rows, tokens):
    slot = iota((rows, LANES), 0)
    lane = iota((rows, LANES), 1)
    picked = jnp.zeros((rows, LANES), wide)
    for high in range((rows + HALF - 1) // HALF):
        line = table_ref[pl.ds(chunk * 8 + high, 1), :]
        picked = jnp.where((slot >> SHIFT) == high, line, picked)
    picked = jnp.where((slot & (HALF - 1)) == (lane & (HALF - 1)), picked, 0.0)
    picked = picked * jnp.where(lane < HALF, float(HALF), 1.0)
    token = jnp.sum(picked, axis=1, keepdims=True).astype(jnp.int32) - 1
    return jnp.where(token == iota((rows, tokens), 1), 1.0, 0.0).astype(lowp)


def seat_kernel(experts, cap, cap_rows, seq_rows,
                routes_ref, order_ref, cot_ref, slots_ref, table_ref, rows_ref,
                route_s, order_s, flat_s):
    images, seq, _ = routes_ref.shape
    tokens = images * seq_rows
    step = pl.program_id(0)

    @pl.when(step == 0)
    def _():
        route_s[...] = jnp.full(route_s.shape, -1, jnp.int32)
        order_s[...] = jnp.zeros(order_s.shape, jnp.int32)
        flat_s[...] = jnp.zeros(flat_s.shape, lowp)
        for image in range(images):
            rows = pl.ds(image * seq_rows, seq)
            route_s[rows, :] = routes_ref[image]
            order_s[rows, :] = order_ref[image]
            flat_s[rows, :] = cot_ref[image]
        lane = iota((tokens, LANES), 1)
        wide_lane = iota((tokens, experts * HALF), 1)
        route = [route_s[:, k : k + 1] for k in range(2)]
        order = [order_s[:, k : k + 1] for k in range(2)]
        low_hit = [(order[k] & (HALF - 1)) == (lane & (HALF - 1)) for k in range(2)]
        low_b = [jnp.where(low_hit[k], 1.0, 0.0).astype(lowp) for k in range(2)]
        high_b = [
            jnp.where((route[k] * HALF + (order[k] >> SHIFT)) == wide_lane, 1.0, 0.0).astype(lowp)
            for k in range(2)
        ]
        counts = (dot_tn(low_b[0], high_b[0]) + dot_tn(low_b[1], high_b[1])).astype(lowp)
        before = iota((LANES, LANES), 0)
        after = iota((LANES, LANES), 1)
        upper = jnp.where((after < HALF) & (after < (before & (HALF - 1))), 1.0, 0.0).astype(lowp)
        within = dot(upper, counts)
        block = (experts * HALF, experts * HALF)
        earlier = jnp.where(
            ((iota(block, 0) >> SHIFT) == (iota(block, 1) >> SHIFT)) & (iota(block, 0) < iota(block, 1)),
            1.0, 0.0,
        ).astype(lowp)
        base = jnp.sum(dot(counts, earlier)[:HALF], axis=0, keepdims=True)
        place = within + base
        place_high = jnp.floor(place * (1.0 / HALF))
        place_low = place - place_high * HALF
        split = jnp.where(iota(place.shape, 0) < HALF, place_high, place_low).astype(lowp)
        weight = jnp.where(lane < HALF, float(HALF), 1.0)
        token = iota((tokens, LANES), 0) + 1
        table = jnp.zeros((experts * 8, LANES), wide)
        row = iota((tokens, experts * 8), 1)
        columns = iota((tokens, 4), 1)
        found = jnp.zeros((tokens, 4), jnp.int32)
        for k in range(2):
            gathered = dot_nt(high_b[k], split)
            position = jnp.sum(
                jnp.where(low_hit[k], gathered * weight, 0.0), axis=1, keepdims=True
            ).astype(jnp.int32)
            seated = (position < cap) & (route[k] >= 0)
            slot = jnp.where(seated, route[k] * cap_rows + position, -1)
            found = jnp.where(columns == k, slot, found)
            found = jnp.where(columns == 2 + k, route[k], found)
            which = jnp.where(seated, route[k] * 8 + (position >> SHIFT), -1)
            which_b = jnp.where(which == row, 1.0, 0.0).astype(lowp)
            value = jnp.where(lane < HALF, token >> SHIFT, token & (HALF - 1)).astype(wide)
            value_b = jnp.where((position & (HALF - 1)) == (lane & (HALF - 1)), value, 0.0).astype(lowp)
            table = table + dot_tn(which_b, value_b)
        table_ref[...] = table
        for image in range(images):
            slots_ref[image] = found[image * seq_rows : (image + 1) * seq_rows]

    hits = token_hits(table_ref, step, cap_rows, tokens)
    rows_ref[0] = dot(hits, flat_s[...]).astype(lowp)


def spread_rows(flat, rows):
    return flat.reshape(flat.shape[0] // rows, rows, flat.shape[1])


def load_rows(scratch, ref, rows):
    for image in range(ref.shape[0]):
        scratch[image * rows : image * rows + ref.shape[1], :] = ref[image].astype(wide)


def front_kernel(seq, experts, rows,
                 me_ref, x_ref, noise_ref, vec_ref, wq_ref, wk_ref, wv_ref, wo_ref, wr_ref,
                 q_ref, k_ref, v_ref, lse_ref, mix_ref, state_ref, aug_ref, probs_ref,
                 x_s, noise_s):
    pack, width = x_ref.shape[0], x_s.shape[1]

    @pl.when(pl.program_id(0) == 0)
    def _():
        x_s[...] = jnp.zeros(x_s.shape, wide)
        noise_s[...] = jnp.zeros(noise_s.shape, wide)

    load_rows(x_s, x_ref, rows)
    load_rows(noise_s, noise_ref, rows)
    x = x_s[...]
    unit, _ = unit_norm(x)
    normed = (unit * vec_ref[0:1, :] + vec_ref[1:2, :]).astype(lowp)
    head_size = width // HEADS
    query = (dot(normed, wq_ref[...]) + vec_ref[2:3, :]).astype(lowp)
    query = query * (head_size ** -0.5)
    key = dot(normed, wk_ref[...]).astype(lowp)
    value = (dot(normed, wv_ref[...]) + vec_ref[3:4, :]).astype(lowp)
    q_ref[...] = spread_rows(query, rows)
    k_ref[...] = spread_rows(key, rows)
    v_ref[...] = spread_rows(value, rows)
    live = iota((rows, rows), 1) < seq
    lane = iota((rows, LANES), 1)
    mixed = []
    for image in range(pack):
        span = slice(image * rows, (image + 1) * rows)
        lse_all = jnp.zeros((rows, LANES), wide)
        joined = []
        for pair in range(HEADS // 2):
            cols = slice(pair * LANES, (pair + 1) * LANES)
            q2, k2, v2 = query[span, cols], key[span, cols], value[span, cols]
            outs = []
            for half in range(2):
                mine = (lane < HALF) if half == 0 else (lane >= HALF)
                scores = dot_nt(jnp.where(mine, q2, jnp.zeros_like(q2)), k2)
                scores = jnp.where(live, scores, -1e30)
                peak = jnp.max(scores, axis=1, keepdims=True)
                expo = jnp.exp(scores - peak)
                total = jnp.sum(expo, axis=1, keepdims=True)
                lse_all = jnp.where(lane == pair * 2 + half, peak + jnp.log(total), lse_all)
                outs.append(dot((expo / total).astype(lowp), v2))
            joined.append(jnp.where(lane < HALF, outs[0], outs[1]).astype(lowp))
        lse_ref[image] = lse_all
        mixed.append(jnp.concatenate(joined, axis=1))
    mixed = jnp.concatenate(mixed, axis=0)
    mix_ref[...] = spread_rows(mixed, rows)
    state = x + dot(mixed, wo_ref[...]) + vec_ref[4:5, :]
    state_ref[...] = spread_rows(state, rows)
    unit_two, _ = unit_norm(state)
    routed = (unit_two * vec_ref[5:6, :] + vec_ref[6:7, :]).astype(lowp)
    logits = dot(routed, wr_ref[...]) + noise_s[...]
    top = jnp.max(logits, axis=1, keepdims=True)
    expo = jnp.exp(logits - top)
    probs = expo / jnp.sum(expo, axis=1, keepdims=True)
    probs_ref[...] = spread_rows(probs, rows)
    shape = (experts, LANES)
    swap = jnp.where(iota(shape, 0) == (iota(shape, 1) ^ me_ref[0]), 1.0, 0.0).astype(lowp)
    aug_ref[:, :, 0:width] = spread_rows(routed, rows)
    aug_ref[:, :, width : width + LANES] = spread_rows(
        dot(probs.astype(lowp), swap).astype(lowp), rows)


def send_kernel(cap, gate_rows, first, me_ref, table_ref, aug_ref, *out_refs):
    cap_rows, width = out_refs[0].shape
    tokens = aug_ref.shape[0]
    for index, out_ref in enumerate(out_refs):
        chunk = me_ref[1] ^ (first + index)
        hits = token_hits(table_ref, chunk, cap_rows, tokens)
        full = dot(hits, aug_ref[...])
        rows = full[:, 0:width]
        lane = iota((cap_rows, LANES), 1)
        gate = jnp.sum(jnp.where(lane == chunk, full[:, width:], 0.0), axis=1, keepdims=True)
        at = iota((cap_rows, width), 0)
        for part in range(gate_rows):
            line = column_to_row(gate, width, part * width)
            rows = jnp.where(at == cap + part, line, rows)
        out_ref[...] = rows.astype(lowp)


def expert_kernel(cap, gate_rows, size, me_ref, *refs):
    x_refs, (g_ref, win_ref, wout_ref) = refs[:size], refs[size : size + 3]
    back_refs = refs[-size - 4 : -4]
    prod_ref, inner_ref, rows_ref, x_s = refs[-4:]
    cap_rows, width = x_s.shape
    step = pl.program_id(0)
    for index in range(size):

        @pl.when(step == index)
        def _(index=index):
            x_s[...] = x_refs[index][...]

    x = x_s[...]
    rows_ref[0] = x
    place = (me_ref[1] ^ step) % size
    grad = g_ref[place].astype(wide)
    gate = jnp.zeros((cap_rows, 1), wide)
    for part in range(gate_rows):
        line = x_s[cap + part : cap + part + 1, :].astype(wide)
        gate = gate + row_to_column(line, cap_rows, part * width)
    gate = jnp.where(iota((cap_rows, 1), 0) < cap, gate, 0.0)
    slot_grad = (gate * grad).astype(lowp)
    rows_ref[1] = slot_grad
    outer = (2.0 / jnp.pi) ** 0.5
    pre = dot(x, win_ref[...])
    hidden = dot_nt(slot_grad, wout_ref[...])
    square = pre * pre
    half = 0.5 * jnp.tanh(pre * (outer + (outer * 0.044715) * square)) + 0.5
    act = (pre * half).astype(lowp)
    slope = half * (
        1.0 + (1.0 - half) * (pre * (2.0 * outer + (6.0 * outer * 0.044715) * square))
    )
    pre_grad = (hidden * slope).astype(lowp)
    inner_ref[0] = pre_grad
    inner_ref[1] = act
    back = dot_nt(pre_grad, win_ref[...])
    made = dot(act, wout_ref[...]).astype(lowp)
    prod_ref[place] = made
    gate_grad = jnp.sum(grad * made.astype(wide), axis=1, keepdims=True)
    at = iota((cap_rows, width), 0)
    for part in range(gate_rows):
        line = column_to_row(gate_grad, width, part * width)
        high = line.astype(lowp).astype(wide)
        back = jnp.where(at == cap + part, high, back)
        back = jnp.where(at == cap + gate_rows + part, line - high, back)
    for index in range(size):

        @pl.when(step == index)
        def _(index=index):
            back_refs[index][...] = back.astype(lowp)


def weight_kernel(n_dp, rows_ref, inner_ref, through_ref, out_ref, passed_ref, in_s, out_s):
    step = pl.program_id(0)
    width, inner = in_s.shape

    @pl.when(step == 0)
    def _():
        in_s[...] = jnp.zeros(in_s.shape, wide)
        out_s[...] = jnp.zeros(out_s.shape, wide)

    in_s[...] += dot_tn(rows_ref[0], inner_ref[0])
    out_s[...] += dot_tn(rows_ref[1], inner_ref[1])

    @pl.when(step == pl.num_programs(0) - 1)
    def _():
        tall, flat = inner // n_dp, width // n_dp
        for owner in range(n_dp):
            base = owner * 2 * tall
            for block in range(inner // width):
                out_ref[base + block * flat : base + (block + 1) * flat, :] = in_s[
                    owner * flat : (owner + 1) * flat, block * width : (block + 1) * width
                ].astype(lowp)
            out_ref[base + tall : base + 2 * tall, :] = (
                out_s[:, owner * tall : (owner + 1) * tall].T.astype(lowp))


def slot_hits(slots, shape):
    at = iota(shape, 1)
    return slots[:, 0:1] == at, slots[:, 1:2] == at


def combine_kernel(experts, cap, cap_rows, gate_rows, rows,
                   me_ref, slots_ref, cot_ref, mix_ref, state_ref, probs_ref, vec_ref, wo_ref,
                   wr_ref, *rest):
    rows_refs, (state_grad_ref, mixed_grad_ref, sums_ref, cot_s, aug_s) = (
        rest[:experts], rest[experts:])
    step = pl.program_id(0)
    width = cot_s.shape[1]

    @pl.when(step == 0)
    def _():
        cot_s[...] = jnp.zeros(cot_s.shape, wide)
        sums_ref[...] = jnp.zeros(sums_ref.shape, wide)
        for away in range(experts):
            rows_ref = rows_refs[away]
            chunk = me_ref[1] ^ away
            lane = iota((cap_rows, LANES), 1)
            extra = jnp.zeros((cap_rows, LANES), wide)
            for part in range(gate_rows):
                for piece in range(2):
                    row = cap + piece * gate_rows + part
                    line = rows_ref[row : row + 1, :].astype(wide)
                    column = row_to_column(line, cap_rows, part * width)
                    extra = jnp.where(lane == chunk + piece * HALF, extra + column, extra)
            at = pl.ds(pl.multiple_of(chunk * cap_rows, 16), cap_rows)
            aug_s[at, 0:width] = rows_ref[...]
            aug_s[at, width : width + LANES] = extra.astype(lowp)

    load_rows(cot_s, cot_ref, rows)
    slots = slots_ref[...].reshape(cot_s.shape[0], 4)
    first, second = slot_hits(slots, (cot_s.shape[0], experts * cap_rows))
    hits = jnp.where(first | second, 1.0, 0.0).astype(lowp)
    full = dot(hits, aug_s[...])
    shape = (LANES, experts)
    swap = jnp.where((iota(shape, 0) & (HALF - 1)) == (iota(shape, 1) ^ me_ref[0]), 1.0, 0.0)
    prob_grad = dot(full[:, width:].astype(lowp), swap.astype(lowp))
    flat = lambda ref: ref[...].reshape(cot_s.shape[0], ref.shape[2])
    probs = flat(probs_ref)
    logit_grad = (
        probs * (prob_grad - jnp.sum(probs * prob_grad, axis=1, keepdims=True))
    ).astype(lowp)
    routed_grad = full[:, 0:width] + dot_nt(logit_grad, wr_ref[...])
    unit_two, inverse_two = unit_norm(flat(state_ref))
    gain_two = vec_ref[5:6, :]
    routed = (unit_two * gain_two + vec_ref[6:7, :]).astype(lowp)
    state_grad = cot_s[...] + norm_back(routed_grad * gain_two, unit_two, inverse_two)
    branch = state_grad.astype(lowp)
    state_grad_ref[...] = spread_rows(state_grad, rows)
    mixed_grad_ref[...] = spread_rows(dot_nt(branch, wo_ref[...]).astype(lowp), rows)
    sums_ref[0:width, :] += dot_tn(flat(mix_ref), branch)
    lines = [branch.astype(wide), routed_grad * unit_two, routed_grad]
    small = jnp.concatenate(
        [jnp.sum(line, axis=0, keepdims=True) for line in lines]
        + [jnp.zeros((5, width), wide)], axis=0
    )
    sums_ref[width : width + 8, :] += small
    sums_ref[width + 8 : width + 8 + experts, :] += dot_tn(logit_grad, routed)


def back_kernel(seq, experts, small_rows, rows,
                me_ref, x_ref, q_ref, k_ref, v_ref, lse_ref, state_grad_ref, mixed_grad_ref,
                vec_ref, early_ref, wq_ref, wk_ref, wv_ref, grad_ref, *rest):
    piece_refs, (x_s, sums_ref) = rest[:experts], rest[experts:]
    step = pl.program_id(0)
    width = x_s.shape[1]
    pack = x_ref.shape[0]
    part_rows = piece_refs[0].shape[0]
    small_at = 4 * width

    @pl.when(step == 0)
    def _():
        x_s[...] = jnp.zeros(x_s.shape, wide)
        sums_ref[...] = jnp.zeros(sums_ref.shape, wide)

    load_rows(x_s, x_ref, rows)
    live = iota((rows, rows), 1) < seq
    lane = iota((rows, LANES), 1)
    scale = (width // HEADS) ** -0.5
    parts = [[], [], []]
    for image in range(pack):
        query, key, value = q_ref[image], k_ref[image], v_ref[image]
        mixed_grad, lse = mixed_grad_ref[image], lse_ref[image]
        lines = [[], [], []]
        for pair in range(HEADS // 2):
            cols = slice(pair * LANES, (pair + 1) * LANES)
            q2, k2, v2, g2 = query[:, cols], key[:, cols], value[:, cols], mixed_grad[:, cols]
            outs = [[], [], []]
            for half in range(2):
                mine = (lane < HALF) if half == 0 else (lane >= HALF)
                scores = dot_nt(jnp.where(mine, q2, jnp.zeros_like(q2)), k2)
                head = pair * 2 + half
                weights = jnp.exp(jnp.where(live, scores - lse[:, head : head + 1], -1e30))
                weight_grad = dot_nt(jnp.where(mine, g2, jnp.zeros_like(g2)), v2)
                product = weights * weight_grad
                score_grad = (
                    product - weights * jnp.sum(product, axis=1, keepdims=True)
                ).astype(lowp)
                outs[0].append(dot(score_grad, k2))
                outs[1].append(dot_tn(score_grad, q2))
                outs[2].append(dot_tn(weights.astype(lowp), g2))
            for which in range(3):
                joined = jnp.where(lane < HALF, outs[which][0], outs[which][1])
                if which == 0:
                    joined = joined * scale
                lines[which].append(joined.astype(lowp))
        for which in range(3):
            parts[which].append(jnp.concatenate(lines[which], axis=1))
    query_grad, key_grad, value_grad = (jnp.concatenate(p, axis=0) for p in parts)
    unit_one, inverse_one = unit_norm(x_s[...])
    gain_one = vec_ref[0:1, :]
    normed = (unit_one * gain_one + vec_ref[1:2, :]).astype(lowp)
    sums_ref[0:width, :] += dot_tn(normed, query_grad)
    sums_ref[width : 2 * width, :] += dot_tn(normed, key_grad)
    sums_ref[2 * width : 3 * width, :] += dot_tn(normed, value_grad)
    normed_grad = (
        dot_nt(query_grad, wq_ref[...])
        + dot_nt(key_grad, wk_ref[...])
        + dot_nt(value_grad, wv_ref[...])
    )
    result = state_grad_ref[...].reshape(x_s.shape) + norm_back(
        normed_grad * gain_one, unit_one, inverse_one)
    grad_ref[...] = spread_rows(result.astype(lowp), rows)[:, 0:seq]
    lines = [query_grad.astype(wide), value_grad.astype(wide), normed_grad * unit_one, normed_grad]
    small = jnp.concatenate(
        [jnp.sum(line, axis=0, keepdims=True) for line in lines]
        + [jnp.zeros((4, width), wide)], axis=0
    )
    sums_ref[small_at : small_at + 8, :] += small

    @pl.when(step == pl.num_programs(0) - 1)
    def _():
        sums_ref[3 * width : 4 * width, :] = early_ref[0:width, :]
        sums_ref[small_at + 8 : small_at + small_rows, :] = early_ref[width:, :]
        exact = sums_ref[small_at : small_at + small_rows, :]
        sums_ref[small_at + small_rows : small_at + 2 * small_rows, :] = (
            exact - exact.astype(lowp).astype(wide)
        )
        for away in range(experts):
            start = pl.multiple_of((me_ref[1] ^ away) * part_rows, 16)
            piece_refs[away][...] = sums_ref[pl.ds(start, part_rows), :].astype(lowp)


def sum_kernel(*refs):
    total = refs[0][...].astype(wide)
    for ref in refs[1:-1]:
        total = total + ref[...].astype(wide)
    refs[-1][...] = total.astype(lowp)


def unpack_kernel(experts, me_ref, *refs):
    piece_refs, weight_refs = refs[:experts], refs[experts : experts + 4]
    small_ref, all_s = refs[experts + 4], refs[experts + 5]
    part_rows, width = piece_refs[0].shape
    small_rows = small_ref.shape[0]
    for away in range(experts):
        start = pl.multiple_of((me_ref[1] ^ away) * part_rows, 16)
        all_s[pl.ds(start, part_rows), :] = piece_refs[away][...].astype(wide)
    for which in range(4):
        weight_refs[which][...] = all_s[which * width : (which + 1) * width, :]
    at = 4 * width
    small_ref[...] = (all_s[at : at + small_rows, :]
                      + all_s[at + small_rows : at + 2 * small_rows, :])


def out_kernel(slots_ref, aug_ref, state_ref, rows_ref, out_ref):
    _, rows, width = state_ref.shape
    seq = out_ref.shape[1]
    slot_total = rows_ref.shape[0]
    lane = iota((rows, LANES), 1)
    gates = aug_ref[0, :, width : width + LANES].astype(wide)
    gate = [
        jnp.sum(jnp.where(lane == slots_ref[0, :, 2 + k : 3 + k], gates, 0.0), axis=1, keepdims=True)
        for k in range(2)
    ]
    first, second = slot_hits(slots_ref[0], (rows, slot_total))
    hits = jnp.where(first, gate[0], jnp.where(second, gate[1], 0.0)).astype(lowp)
    out_ref[0] = (state_ref[0] + dot(hits, rows_ref[...])).astype(lowp)[0:seq]


def adam_kernel(*refs):
    grad_ref, states, results, rounded_ref = refs[0], refs[1:7], refs[7:13], refs[13]
    corr_one = 1.0 - BETA_ONE**adam_steps
    corr_two = 1.0 - BETA_TWO**adam_steps
    for which in range(2):
        master, moment, second = (ref[0] for ref in states[which::2])
        grad = grad_ref[which].astype(wide)
        new_moment = BETA_ONE * moment + (1.0 - BETA_ONE) * grad
        new_second = BETA_TWO * second + (1.0 - BETA_TWO) * grad * grad
        update = (
            LEARN_RATE * (new_moment / corr_one) / (jnp.sqrt(new_second / corr_two) + ADAM_EPS)
        )
        new_master = master - update
        for ref, value in zip(results[which::2], (new_master, new_moment, new_second)):
            ref[0] = value
        rounded_ref[which] = new_master.astype(lowp)


def spread_kernel(rounded_ref, in_ref, out_ref):
    _, flat, inner = in_ref.shape
    width = out_ref.shape[2]
    for block in range(inner // width):
        in_ref[0, :, block * width : (block + 1) * width] = rounded_ref[
            0, block * flat : (block + 1) * flat, :]
    out_ref[0] = rounded_ref[1]


def whole(shape):
    return pl.BlockSpec(shape, lambda i: (0,) * len(shape))


def one(shape, pack=1):
    return pl.BlockSpec((pack,) + shape, lambda i: (i,) + (0,) * len(shape))


def smem():
    return pl.BlockSpec(memory_space=pltpu.SMEM)


def hbm():
    return pl.BlockSpec(memory_space=pl.ANY)


def call(kernel, micros, megabytes, name, grid, inputs, in_specs, out_specs, out_shape,
         scratch=(), after=(), aliases=None, prefetch=0):
    count, extra = len(inputs), len(after)

    def body(*refs):
        kernel(*refs[:count], *refs[count + extra :])

    return pl.pallas_call(
        body,
        grid_spec=pltpu.PrefetchScalarGridSpec(
            num_scalar_prefetch=prefetch, grid=grid, in_specs=in_specs + [hbm()] * extra,
            out_specs=out_specs, scratch_shapes=list(scratch)),
        out_shape=out_shape,
        input_output_aliases=aliases or {},
        compiler_params=params(len(grid), megabytes),
        cost_estimate=cost(micros),
        name=name,
    )(*inputs, *after)


def like(shape, dtype):
    return jax.ShapeDtypeStruct(shape, dtype)


def swap_expert(value, away, n_expert):
    return lax.ppermute(value, "expert", [(i, i ^ away) for i in range(n_expert)])


def on_device(n_expert, n_dp, images, cotangent, router_noise, routes, seat_order,
              norm1_gain, norm1_shift, query_weight, query_bias, key_weight, value_weight,
              value_bias, output_weight, output_bias, norm2_gain, norm2_shift, router_weight,
              expert_in, expert_out, master_in, master_out, moment_in, moment_out,
              second_in, second_out):
    count, seq, width = images.shape
    experts = router_noise.shape[2]
    cap = (count * seq * 2 + experts - 1) // experts
    gate_rows = (cap + width - 1) // width
    cap_rows = round_up(cap + 2 * gate_rows, 16)
    seq_rows = round_up(seq, 16)
    tokens = count * seq_rows
    inner = expert_in.shape[2]
    slot_total = experts * cap_rows
    aug = width + LANES
    me = jnp.stack([jnp.int32(0), lax.axis_index("expert").astype(jnp.int32)])
    vecs = jnp.stack([norm1_gain, norm1_shift, query_bias, value_bias, output_bias,
                      norm2_gain, norm2_shift, norm2_shift])

    slots, table, grad_rows = call(
        functools.partial(seat_kernel, experts, cap, cap_rows, seq_rows), 17, 56, "seat",
        (experts,), (routes, seat_order.reshape(routes.shape), cotangent),
        [whole(routes.shape), whole(routes.shape), whole(cotangent.shape)],
        [whole((count, seq_rows, 4)), whole((experts * 8, LANES)), one((cap_rows, width))],
        [like((count, seq_rows, 4), jnp.int32), like((experts * 8, LANES), wide),
         like((experts, cap_rows, width), lowp)],
        [pltpu.VMEM((tokens, 2), jnp.int32), pltpu.VMEM((tokens, 2), jnp.int32),
         pltpu.VMEM((tokens, width), lowp)])
    grad_in = lax.all_to_all(grad_rows, "expert", split_axis=0, concat_axis=0, tiled=True)

    square = (width, width)
    token_shape = (count, seq_rows, width)
    pack = PACK if count % PACK == 0 else 1
    query, key, value, lse, mixed, state, routed, probs = call(
        functools.partial(front_kernel, seq, experts, seq_rows), 19, 56, "front", (count // pack,),
        (me, images, router_noise, vecs, query_weight, key_weight, value_weight, output_weight,
         router_weight),
        [smem(), one((seq, width), pack), one((seq, experts), pack), whole((8, width)),
         whole(square), whole(square), whole(square), whole(square), whole((width, experts))],
        [one((seq_rows, width), pack)] * 3 + [
            one((seq_rows, LANES), pack), one((seq_rows, width), pack), one((seq_rows, width), pack),
            one((seq_rows, aug), pack), one((seq_rows, experts), pack)],
        [like(token_shape, lowp)] * 3 + [
            like((count, seq_rows, LANES), wide), like(token_shape, lowp),
            like(token_shape, wide), like((count, seq_rows, aug), lowp),
            like((count, seq_rows, experts), wide)],
        [pltpu.VMEM((pack * seq_rows, width), wide),
         pltpu.VMEM((pack * seq_rows, experts), wide)])

    groups = min(4, experts)
    size = experts // groups
    sent = [None] * experts
    chunk_spec, chunk_like = whole((cap_rows, width)), like((cap_rows, width), lowp)
    before = ()
    for group in list(range(1, groups)) + [0]:
        outs = call(
            functools.partial(send_kernel, cap, gate_rows, group * size), 0.3, 32, f"send{group}",
            (1,), (me, table, routed.reshape(tokens, aug)),
            [smem(), whole((experts * 8, LANES)), whole((tokens, aug))],
            [chunk_spec] * size, [chunk_like] * size, after=before)
        sent[group * size : (group + 1) * size] = outs
        before = (outs[0],)
    arrived = [sent[0]] + [swap_expert(sent[away], away, n_expert) for away in range(1, experts)]

    buffers = ()
    back_rows = []
    for group in range(groups):
        block = lambda i, ref, group=group: ((ref[1] // size) ^ group, 0, 0)
        fixed = lambda i, ref: (0, 0)
        line = lambda i, ref, group=group: (0, group * size + i, 0)
        chunk_at = pl.BlockSpec((cap_rows, width), fixed)
        outs = call(
            functools.partial(expert_kernel, cap, gate_rows, size), 0.3, 52, f"expert{group}",
            (size,),
            (me, *arrived[group * size : (group + 1) * size], grad_in, expert_in[0],
             expert_out[0], *buffers),
            [chunk_at] * size + [
                pl.BlockSpec((size, cap_rows, width), block),
                pl.BlockSpec((width, inner), fixed), pl.BlockSpec((inner, width), fixed)]
            + [hbm()] * len(buffers),
            [chunk_at] * size + [
                pl.BlockSpec((size, cap_rows, width), block),
                pl.BlockSpec((2, cap_rows, inner), line), pl.BlockSpec((2, cap_rows, width), line)],
            [chunk_like] * size + [
                like((experts, cap_rows, width), lowp),
                like((2, slot_total, inner), lowp), like((2, slot_total, width), lowp)],
            [pltpu.VMEM((cap_rows, width), lowp)], prefetch=1,
            aliases={size + 4 + k: size + k for k in range(len(buffers))})
        back_rows += outs[:size]
        buffers = tuple(outs[size:])
    produced, inner_rows, outer_rows = buffers
    back_rows = [back_rows[0]] + [
        swap_expert(back_rows[away], away, n_expert) for away in range(1, experts)]

    steps = 4
    per = slot_total // steps

    line = lambda size: pl.BlockSpec((2, per, size), lambda i: (0, i, 0))
    weight_grads, produced = call(
        functools.partial(weight_kernel, n_dp), 0.02, 52, "weight", (steps,),
        (outer_rows, inner_rows, produced), [line(width), line(inner), hbm()],
        [whole((2 * inner, width)), hbm()],
        [like((2 * inner, width), lowp), like(produced.shape, lowp)],
        [pltpu.VMEM((width, inner), wide), pltpu.VMEM((width, inner), wide)],
        after=back_rows[1 : 2 * size], aliases={2: 1})
    tall, flat = inner // n_dp, width // n_dp
    share = lax.psum_scatter(weight_grads, "dp", scatter_dimension=0, tiled=True)
    returned = lax.all_to_all(produced, "expert", split_axis=0, concat_axis=0, tiled=True)

    early_small = 8 + round_up(experts, 8)
    early_rows = width + early_small
    state_grad, mixed_grad, early = call(
        functools.partial(combine_kernel, experts, cap, cap_rows, gate_rows, seq_rows), 300,
        56,
        "combine", (count // pack,),
        (me, slots, cotangent, mixed, state, probs, vecs, output_weight, router_weight,
         *back_rows),
        [smem(), one((seq_rows, 4), pack), one((seq, width), pack), one((seq_rows, width), pack),
         one((seq_rows, width), pack), one((seq_rows, experts), pack), whole((8, width)), whole(square),
         whole((width, experts))] + [chunk_spec] * experts,
        [one((seq_rows, width), pack), one((seq_rows, width), pack), whole((early_rows, width))],
        [like(token_shape, wide), like(token_shape, lowp), like((early_rows, width), wide)],
        [pltpu.VMEM((pack * seq_rows, width), wide), pltpu.VMEM((slot_total, aug), lowp)],
        after=(weight_grads,))

    small_rows = 8 + early_small
    part_rows = round_up(4 * width + 2 * small_rows, 16 * experts) // experts
    part_spec, part_like = whole((part_rows, width)), like((part_rows, width), lowp)
    images_grad, *pieces = call(
        functools.partial(back_kernel, seq, experts, small_rows, seq_rows), 300, 56, "back",
        (count // pack,),
        (me, images, query, key, value, lse, state_grad, mixed_grad, vecs, early, query_weight,
         key_weight, value_weight),
        [smem(), one((seq, width), pack)] + [one((seq_rows, width), pack)] * 3
        + [one((seq_rows, LANES), pack), one((seq_rows, width), pack), one((seq_rows, width), pack),
           whole((8, width)), whole((early_rows, width)), whole(square), whole(square),
           whole(square)],
        [one((seq, width), pack)] + [part_spec] * experts,
        [like(images.shape, lowp)] + [part_like] * experts,
        [pltpu.VMEM((pack * seq_rows, width), wide), pltpu.VMEM((part_rows * experts, width), wide)],
        )

    def add(parts, name, after=()):
        return call(sum_kernel, 1, 56, name, (1,), parts, [part_spec] * len(parts), part_spec,
                    part_like, after=after)

    across = pl.BlockSpec((1, flat, width), lambda i: (0, 0, i))
    down = pl.BlockSpec((1, flat, width), lambda i: (0, i, 0))
    both = pl.BlockSpec((2, flat, width), lambda i: (0, i, 0))
    *states, rounded = call(
        adam_kernel, 1, 56, "adam", (inner // width,),
        (share.reshape(2, tall, width), master_in, master_out, moment_in, moment_out,
         second_in, second_out),
        [both] + [across, down] * 3, [across, down] * 3 + [both],
        [like(master_in.shape, wide), like(master_out.shape, wide)] * 3
        + [like((2, tall, width), lowp)], after=(pieces[0], returned))
    spread = lax.all_gather(rounded, "dp", axis=0, tiled=True)
    new_expert_in, new_expert_out = call(
        spread_kernel, 2, 56, "spread", (n_dp,), (spread,), [
            pl.BlockSpec((2, tall, width), lambda i: (i, 0, 0))],
        [pl.BlockSpec((1, flat, inner), lambda i: (0, i, 0)),
         pl.BlockSpec((1, tall, width), lambda i: (0, i, 0))],
        [like(expert_in.shape, lowp), like(expert_out.shape, lowp)])
    mine = add([pieces[0]] + [swap_expert(pieces[away], away, n_expert)
                              for away in range(1, experts)], "sum_plane",
               (returned, rounded))
    block_out = call(
        out_kernel, 1, 56, "block_out", (count,),
        (slots, routed, state, returned.reshape(slot_total, width)),
        [one((seq_rows, 4)), one((seq_rows, aug)), one((seq_rows, width)),
         whole((slot_total, width))],
        one((seq, width)), like(images.shape, lowp), after=(mine,))
    share = add([mine] + [
        lax.ppermute(mine, "dp", [(i, (i + shift) % n_dp) for i in range(n_dp)])
        for shift in range(1, n_dp)], "sum_dp", (block_out,))
    shares = [share] + [swap_expert(share, away, n_expert) for away in range(1, experts)]

    *big, small_sum = call(
        functools.partial(unpack_kernel, experts), 3, 56, "unpack", (1,), (me, *shares),
        [smem()] + [part_spec] * experts,
        [whole(square)] * 4 + [whole((small_rows, width))],
        [like(square, wide)] * 4 + [like((small_rows, width), wide)],
        [pltpu.VMEM((part_rows * experts, width), wide)])
    return (
        block_out,
        images_grad,
        small_sum[2],
        small_sum[3],
        big[0],
        small_sum[0],
        big[1],
        big[2],
        small_sum[1],
        big[3],
        small_sum[8],
        small_sum[9],
        small_sum[10],
        small_sum[16 : 16 + experts].T,
        new_expert_in,
        new_expert_out,
        *states,
    )


def solution(mesh):
    both = ("dp", "expert")
    in_specs = (
        (P(both, None, None),) * 4
        + (P(both, None),)
        + (P(),) * 12
        + (P("expert", None, None),) * 2
        + (P("expert", "dp", None),) * 6
    )
    out_specs = (
        (P(both, None, None),) * 2
        + (P(),) * 12
        + (P("expert", None, None),) * 2
        + (P("expert", "dp", None),) * 6
    )
    body = functools.partial(on_device, mesh.shape["expert"], mesh.shape["dp"])
    return jax.shard_map(body, mesh=mesh, in_specs=in_specs, out_specs=out_specs, check_vma=False)
```

```python
import functools

import jax
import jax.numpy as jnp
from jax import lax
from jax.experimental import pallas as pl
from jax.experimental.pallas import tpu as pltpu
from jax.sharding import PartitionSpec as P

HEADS = 6
EPS_NORM = 1e-06
BETA_ONE = 0.9
BETA_TWO = 0.999
LEARN_RATE = 0.03
ADAM_EPS = 1e-08
adam_steps = 100.0

lowp = jnp.bfloat16
wide = jnp.float32
LANES = 128
HALF = 64
SHIFT = 6
PACK = 4


def round_up(value, step):
    return (value + step - 1) // step * step


def dot(left, right):
    return jnp.dot(left, right, preferred_element_type=wide)


def dot_nt(left, right):
    return lax.dot_general(left, right, (((1,), (1,)), ((), ())), preferred_element_type=wide)


def dot_tn(left, right):
    return lax.dot_general(left, right, (((0,), (0,)), ((), ())), preferred_element_type=wide)


def iota(shape, dim):
    return lax.broadcasted_iota(jnp.int32, shape, dim)


def cost(micros):
    return pl.CostEstimate(
        flops=int(micros * 1.1e9), bytes_accessed=int(micros * 3.5e6), transcendentals=0
    )


def params(dims, megabytes=24):
    return pltpu.CompilerParams(
        dimension_semantics=("arbitrary",) * dims, vmem_limit_bytes=megabytes * 1024 * 1024
    )


def unit_norm(values):
    mean = jnp.mean(values, axis=-1, keepdims=True)
    centred = values - mean
    inverse = lax.rsqrt(jnp.mean(centred * centred, axis=-1, keepdims=True) + EPS_NORM)
    return centred * inverse, inverse


def norm_back(scaled, unit, inverse):
    return inverse * (
        scaled
        - jnp.mean(scaled, axis=-1, keepdims=True)
        - unit * jnp.mean(scaled * unit, axis=-1, keepdims=True)
    )


def column_to_row(column, width, offset):
    shape = (column.shape[0], width)
    hit = iota(shape, 0) == iota(shape, 1) + offset
    return jnp.sum(jnp.where(hit, column, 0.0), axis=0, keepdims=True)


def row_to_column(row, rows, offset):
    shape = (rows, row.shape[1])
    hit = iota(shape, 0) == iota(shape, 1) + offset
    return jnp.sum(jnp.where(hit, row, 0.0), axis=1, keepdims=True)


def token_hits(table_ref, chunk, rows, tokens):
    slot = iota((rows, LANES), 0)
    lane = iota((rows, LANES), 1)
    picked = jnp.zeros((rows, LANES), wide)
    for high in range((rows + HALF - 1) // HALF):
        line = table_ref[pl.ds(chunk * 8 + high, 1), :]
        picked = jnp.where((slot >> SHIFT) == high, line, picked)
    picked = jnp.where((slot & (HALF - 1)) == (lane & (HALF - 1)), picked, 0.0)
    picked = picked * jnp.where(lane < HALF, float(HALF), 1.0)
    token = jnp.sum(picked, axis=1, keepdims=True).astype(jnp.int32) - 1
    return jnp.where(token == iota((rows, tokens), 1), 1.0, 0.0).astype(lowp)


def seat_kernel(experts, cap, cap_rows, seq_rows,
                routes_ref, order_ref, cot_ref, slots_ref, table_ref, rows_ref,
                route_s, order_s, flat_s):
    images, seq, _ = routes_ref.shape
    tokens = images * seq_rows
    step = pl.program_id(0)

    @pl.when(step == 0)
    def _():
        route_s[...] = jnp.full(route_s.shape, -1, jnp.int32)
        order_s[...] = jnp.zeros(order_s.shape, jnp.int32)
        flat_s[...] = jnp.zeros(flat_s.shape, lowp)
        for image in range(images):
            rows = pl.ds(image * seq_rows, seq)
            route_s[rows, :] = routes_ref[image]
            order_s[rows, :] = order_ref[image]
            flat_s[rows, :] = cot_ref[image]
        lane = iota((tokens, LANES), 1)
        wide_lane = iota((tokens, experts * HALF), 1)
        route = [route_s[:, k : k + 1] for k in range(2)]
        order = [order_s[:, k : k + 1] for k in range(2)]
        low_hit = [(order[k] & (HALF - 1)) == (lane & (HALF - 1)) for k in range(2)]
        low_b = [jnp.where(low_hit[k], 1.0, 0.0).astype(lowp) for k in range(2)]
        high_b = [
            jnp.where((route[k] * HALF + (order[k] >> SHIFT)) == wide_lane, 1.0, 0.0).astype(lowp)
            for k in range(2)
        ]
        counts = (dot_tn(low_b[0], high_b[0]) + dot_tn(low_b[1], high_b[1])).astype(lowp)
        before = iota((LANES, LANES), 0)
        after = iota((LANES, LANES), 1)
        upper = jnp.where((after < HALF) & (after < (before & (HALF - 1))), 1.0, 0.0).astype(lowp)
        within = dot(upper, counts)
        block = (experts * HALF, experts * HALF)
        earlier = jnp.where(
            ((iota(block, 0) >> SHIFT) == (iota(block, 1) >> SHIFT)) & (iota(block, 0) < iota(block, 1)),
            1.0, 0.0,
        ).astype(lowp)
        base = jnp.sum(dot(counts, earlier)[:HALF], axis=0, keepdims=True)
        place = within + base
        place_high = jnp.floor(place * (1.0 / HALF))
        place_low = place - place_high * HALF
        split = jnp.where(iota(place.shape, 0) < HALF, place_high, place_low).astype(lowp)
        weight = jnp.where(lane < HALF, float(HALF), 1.0)
        token = iota((tokens, LANES), 0) + 1
        table = jnp.zeros((experts * 8, LANES), wide)
        row = iota((tokens, experts * 8), 1)
        columns = iota((tokens, 4), 1)
        found = jnp.zeros((tokens, 4), jnp.int32)
        for k in range(2):
            gathered = dot_nt(high_b[k], split)
            position = jnp.sum(
                jnp.where(low_hit[k], gathered * weight, 0.0), axis=1, keepdims=True
            ).astype(jnp.int32)
            seated = (position < cap) & (route[k] >= 0)
            slot = jnp.where(seated, route[k] * cap_rows + position, -1)
            found = jnp.where(columns == k, slot, found)
            found = jnp.where(columns == 2 + k, route[k], found)
            which = jnp.where(seated, route[k] * 8 + (position >> SHIFT), -1)
            which_b = jnp.where(which == row, 1.0, 0.0).astype(lowp)
            value = jnp.where(lane < HALF, token >> SHIFT, token & (HALF - 1)).astype(wide)
            value_b = jnp.where((position & (HALF - 1)) == (lane & (HALF - 1)), value, 0.0).astype(lowp)
            table = table + dot_tn(which_b, value_b)
        table_ref[...] = table
        for image in range(images):
            slots_ref[image] = found[image * seq_rows : (image + 1) * seq_rows]

    hits = token_hits(table_ref, step, cap_rows, tokens)
    rows_ref[0] = dot(hits, flat_s[...]).astype(lowp)


def spread_rows(flat, rows):
    return flat.reshape(flat.shape[0] // rows, rows, flat.shape[1])


def load_rows(scratch, ref, rows):
    for image in range(ref.shape[0]):
        scratch[image * rows : image * rows + ref.shape[1], :] = ref[image].astype(wide)


def front_kernel(seq, experts, rows,
                 me_ref, x_ref, noise_ref, vec_ref, wq_ref, wk_ref, wv_ref, wo_ref, wr_ref,
                 q_ref, k_ref, v_ref, lse_ref, mix_ref, state_ref, aug_ref, probs_ref,
                 x_s, noise_s):
    pack, width = x_ref.shape[0], x_s.shape[1]

    @pl.when(pl.program_id(0) == 0)
    def _():
        x_s[...] = jnp.zeros(x_s.shape, wide)
        noise_s[...] = jnp.zeros(noise_s.shape, wide)

    load_rows(x_s, x_ref, rows)
    load_rows(noise_s, noise_ref, rows)
    x = x_s[...]
    unit, _ = unit_norm(x)
    normed = (unit * vec_ref[0:1, :] + vec_ref[1:2, :]).astype(lowp)
    head_size = width // HEADS
    query = (dot(normed, wq_ref[...]) + vec_ref[2:3, :]).astype(lowp)
    query = query * (head_size ** -0.5)
    key = dot(normed, wk_ref[...]).astype(lowp)
    value = (dot(normed, wv_ref[...]) + vec_ref[3:4, :]).astype(lowp)
    q_ref[...] = spread_rows(query, rows)
    k_ref[...] = spread_rows(key, rows)
    v_ref[...] = spread_rows(value, rows)
    live = iota((rows, rows), 1) < seq
    lane = iota((rows, LANES), 1)
    mixed = []
    for image in range(pack):
        span = slice(image * rows, (image + 1) * rows)
        lse_all = jnp.zeros((rows, LANES), wide)
        joined = []
        for pair in range(HEADS // 2):
            cols = slice(pair * LANES, (pair + 1) * LANES)
            q2, k2, v2 = query[span, cols], key[span, cols], value[span, cols]
            outs = []
            for half in range(2):
                mine = (lane < HALF) if half == 0 else (lane >= HALF)
                scores = dot_nt(jnp.where(mine, q2, jnp.zeros_like(q2)), k2)
                scores = jnp.where(live, scores, -1e30)
                peak = jnp.max(scores, axis=1, keepdims=True)
                expo = jnp.exp(scores - peak)
                total = jnp.sum(expo, axis=1, keepdims=True)
                lse_all = jnp.where(lane == pair * 2 + half, peak + jnp.log(total), lse_all)
                outs.append(dot((expo / total).astype(lowp), v2))
            joined.append(jnp.where(lane < HALF, outs[0], outs[1]).astype(lowp))
        lse_ref[image] = lse_all
        mixed.append(jnp.concatenate(joined, axis=1))
    mixed = jnp.concatenate(mixed, axis=0)
    mix_ref[...] = spread_rows(mixed, rows)
    state = x + dot(mixed, wo_ref[...]) + vec_ref[4:5, :]
    state_ref[...] = spread_rows(state, rows)
    unit_two, _ = unit_norm(state)
    routed = (unit_two * vec_ref[5:6, :] + vec_ref[6:7, :]).astype(lowp)
    logits = dot(routed, wr_ref[...]) + noise_s[...]
    top = jnp.max(logits, axis=1, keepdims=True)
    expo = jnp.exp(logits - top)
    probs = expo / jnp.sum(expo, axis=1, keepdims=True)
    probs_ref[...] = spread_rows(probs, rows)
    shape = (experts, LANES)
    swap = jnp.where(iota(shape, 0) == (iota(shape, 1) ^ me_ref[0]), 1.0, 0.0).astype(lowp)
    aug_ref[:, :, 0:width] = spread_rows(routed, rows)
    aug_ref[:, :, width : width + LANES] = spread_rows(
        dot(probs.astype(lowp), swap).astype(lowp), rows)


def send_kernel(cap, gate_rows, first, me_ref, table_ref, aug_ref, *out_refs):
    cap_rows, width = out_refs[0].shape
    tokens = aug_ref.shape[0]
    for index, out_ref in enumerate(out_refs):
        chunk = me_ref[1] ^ (first + index)
        hits = token_hits(table_ref, chunk, cap_rows, tokens)
        full = dot(hits, aug_ref[...])
        rows = full[:, 0:width]
        lane = iota((cap_rows, LANES), 1)
        gate = jnp.sum(jnp.where(lane == chunk, full[:, width:], 0.0), axis=1, keepdims=True)
        at = iota((cap_rows, width), 0)
        for part in range(gate_rows):
            line = column_to_row(gate, width, part * width)
            rows = jnp.where(at == cap + part, line, rows)
        out_ref[...] = rows.astype(lowp)


def expert_kernel(cap, gate_rows, size, me_ref, *refs):
    x_refs, (g_ref, win_ref, wout_ref) = refs[:size], refs[size : size + 3]
    back_refs = refs[-size - 4 : -4]
    prod_ref, inner_ref, rows_ref, x_s = refs[-4:]
    cap_rows, width = x_s.shape
    step = pl.program_id(0)
    for index in range(size):

        @pl.when(step == index)
        def _(index=index):
            x_s[...] = x_refs[index][...]

    x = x_s[...]
    rows_ref[0] = x
    grad = g_ref[0].astype(wide)
    gate = jnp.zeros((cap_rows, 1), wide)
    for part in range(gate_rows):
        line = x_s[cap + part : cap + part + 1, :].astype(wide)
        gate = gate + row_to_column(line, cap_rows, part * width)
    gate = jnp.where(iota((cap_rows, 1), 0) < cap, gate, 0.0)
    slot_grad = (gate * grad).astype(lowp)
    rows_ref[1] = slot_grad
    outer = (2.0 / jnp.pi) ** 0.5
    pre = dot(x, win_ref[...])
    hidden = dot_nt(slot_grad, wout_ref[...])
    square = pre * pre
    half = 0.5 * jnp.tanh(pre * (outer + (outer * 0.044715) * square)) + 0.5
    act = (pre * half).astype(lowp)
    slope = half * (
        1.0 + (1.0 - half) * (pre * (2.0 * outer + (6.0 * outer * 0.044715) * square))
    )
    pre_grad = (hidden * slope).astype(lowp)
    inner_ref[0] = pre_grad
    inner_ref[1] = act
    back = dot_nt(pre_grad, win_ref[...])
    made = dot(act, wout_ref[...]).astype(lowp)
    prod_ref[0] = made
    gate_grad = jnp.sum(grad * made.astype(wide), axis=1, keepdims=True)
    at = iota((cap_rows, width), 0)
    for part in range(gate_rows):
        line = column_to_row(gate_grad, width, part * width)
        high = line.astype(lowp).astype(wide)
        back = jnp.where(at == cap + part, high, back)
        back = jnp.where(at == cap + gate_rows + part, line - high, back)
    for index in range(size):

        @pl.when(step == index)
        def _(index=index):
            back_refs[index][...] = back.astype(lowp)


def weight_kernel(n_dp, rows_ref, inner_ref, through_ref, out_ref, passed_ref, in_s, out_s):
    step = pl.program_id(0)
    width, inner = in_s.shape

    @pl.when(step == 0)
    def _():
        in_s[...] = jnp.zeros(in_s.shape, wide)
        out_s[...] = jnp.zeros(out_s.shape, wide)

    in_s[...] += dot_tn(rows_ref[0], inner_ref[0])
    out_s[...] += dot_tn(rows_ref[1], inner_ref[1])

    @pl.when(step == pl.num_programs(0) - 1)
    def _():
        tall, flat = inner // n_dp, width // n_dp
        for owner in range(n_dp):
            base = owner * 2 * tall
            for block in range(inner // width):
                out_ref[base + block * flat : base + (block + 1) * flat, :] = in_s[
                    owner * flat : (owner + 1) * flat, block * width : (block + 1) * width
                ].astype(lowp)
            out_ref[base + tall : base + 2 * tall, :] = (
                out_s[:, owner * tall : (owner + 1) * tall].T.astype(lowp))


def slot_hits(slots, shape):
    at = iota(shape, 1)
    return slots[:, 0:1] == at, slots[:, 1:2] == at


def combine_kernel(experts, cap, cap_rows, gate_rows, rows,
                   me_ref, slots_ref, cot_ref, mix_ref, state_ref, probs_ref, vec_ref, wo_ref,
                   wr_ref, *rest):
    rows_refs, (state_grad_ref, mixed_grad_ref, sums_ref, cot_s, aug_s) = (
        rest[:experts], rest[experts:])
    step = pl.program_id(0)
    width = cot_s.shape[1]

    @pl.when(step == 0)
    def _():
        cot_s[...] = jnp.zeros(cot_s.shape, wide)
        sums_ref[...] = jnp.zeros(sums_ref.shape, wide)
        for away in range(experts):
            rows_ref = rows_refs[away]
            chunk = me_ref[1] ^ away
            lane = iota((cap_rows, LANES), 1)
            extra = jnp.zeros((cap_rows, LANES), wide)
            for part in range(gate_rows):
                for piece in range(2):
                    row = cap + piece * gate_rows + part
                    line = rows_ref[row : row + 1, :].astype(wide)
                    column = row_to_column(line, cap_rows, part * width)
                    extra = jnp.where(lane == chunk + piece * HALF, extra + column, extra)
            at = pl.ds(pl.multiple_of(chunk * cap_rows, 16), cap_rows)
            aug_s[at, 0:width] = rows_ref[...]
            aug_s[at, width : width + LANES] = extra.astype(lowp)

    load_rows(cot_s, cot_ref, rows)
    slots = slots_ref[...].reshape(cot_s.shape[0], 4)
    first, second = slot_hits(slots, (cot_s.shape[0], experts * cap_rows))
    hits = jnp.where(first | second, 1.0, 0.0).astype(lowp)
    full = dot(hits, aug_s[...])
    shape = (LANES, experts)
    swap = jnp.where((iota(shape, 0) & (HALF - 1)) == (iota(shape, 1) ^ me_ref[0]), 1.0, 0.0)
    prob_grad = dot(full[:, width:].astype(lowp), swap.astype(lowp))
    flat = lambda ref: ref[...].reshape(cot_s.shape[0], ref.shape[2])
    probs = flat(probs_ref)
    logit_grad = (
        probs * (prob_grad - jnp.sum(probs * prob_grad, axis=1, keepdims=True))
    ).astype(lowp)
    routed_grad = full[:, 0:width] + dot_nt(logit_grad, wr_ref[...])
    unit_two, inverse_two = unit_norm(flat(state_ref))
    gain_two = vec_ref[5:6, :]
    routed = (unit_two * gain_two + vec_ref[6:7, :]).astype(lowp)
    state_grad = cot_s[...] + norm_back(routed_grad * gain_two, unit_two, inverse_two)
    branch = state_grad.astype(lowp)
    state_grad_ref[...] = spread_rows(state_grad, rows)
    mixed_grad_ref[...] = spread_rows(dot_nt(branch, wo_ref[...]).astype(lowp), rows)
    sums_ref[0:width, :] += dot_tn(flat(mix_ref), branch)
    lines = [branch.astype(wide), routed_grad * unit_two, routed_grad]
    small = jnp.concatenate(
        [jnp.sum(line, axis=0, keepdims=True) for line in lines]
        + [jnp.zeros((5, width), wide)], axis=0
    )
    sums_ref[width : width + 8, :] += small
    sums_ref[width + 8 : width + 8 + experts, :] += dot_tn(logit_grad, routed)


def back_kernel(seq, experts, small_rows, rows, last,
                me_ref, x_ref, q_ref, k_ref, v_ref, lse_ref, state_grad_ref, mixed_grad_ref,
                vec_ref, wq_ref, wk_ref, wv_ref, *rest):
    if last:
        early_ref, carry_ref, _, grad_ref, *piece_refs, x_s, sums_ref = rest
    else:
        grad_ref, sums_ref, x_s = rest
    step = pl.program_id(0)
    width = x_s.shape[1]
    pack = x_ref.shape[0]
    small_at = 4 * width

    @pl.when(step == 0)
    def _():
        x_s[...] = jnp.zeros(x_s.shape, wide)
        sums_ref[...] = carry_ref[...] if last else jnp.zeros(sums_ref.shape, wide)

    load_rows(x_s, x_ref, rows)
    live = iota((rows, rows), 1) < seq
    lane = iota((rows, LANES), 1)
    scale = (width // HEADS) ** -0.5
    parts = [[], [], []]
    for image in range(pack):
        query, key, value = q_ref[image], k_ref[image], v_ref[image]
        mixed_grad, lse = mixed_grad_ref[image], lse_ref[image]
        lines = [[], [], []]
        for pair in range(HEADS // 2):
            cols = slice(pair * LANES, (pair + 1) * LANES)
            q2, k2, v2, g2 = query[:, cols], key[:, cols], value[:, cols], mixed_grad[:, cols]
            outs = [[], [], []]
            for half in range(2):
                mine = (lane < HALF) if half == 0 else (lane >= HALF)
                scores = dot_nt(jnp.where(mine, q2, jnp.zeros_like(q2)), k2)
                head = pair * 2 + half
                weights = jnp.exp(jnp.where(live, scores - lse[:, head : head + 1], -1e30))
                weight_grad = dot_nt(jnp.where(mine, g2, jnp.zeros_like(g2)), v2)
                product = weights * weight_grad
                score_grad = (
                    product - weights * jnp.sum(product, axis=1, keepdims=True)
                ).astype(lowp)
                outs[0].append(dot(score_grad, k2))
                outs[1].append(dot_tn(score_grad, q2))
                outs[2].append(dot_tn(weights.astype(lowp), g2))
            for which in range(3):
                joined = jnp.where(lane < HALF, outs[which][0], outs[which][1])
                if which == 0:
                    joined = joined * scale
                lines[which].append(joined.astype(lowp))
        for which in range(3):
            parts[which].append(jnp.concatenate(lines[which], axis=1))
    query_grad, key_grad, value_grad = (jnp.concatenate(p, axis=0) for p in parts)
    unit_one, inverse_one = unit_norm(x_s[...])
    gain_one = vec_ref[0:1, :]
    normed = (unit_one * gain_one + vec_ref[1:2, :]).astype(lowp)
    sums_ref[0:width, :] += dot_tn(normed, query_grad)
    sums_ref[width : 2 * width, :] += dot_tn(normed, key_grad)
    sums_ref[2 * width : 3 * width, :] += dot_tn(normed, value_grad)
    normed_grad = (
        dot_nt(query_grad, wq_ref[...])
        + dot_nt(key_grad, wk_ref[...])
        + dot_nt(value_grad, wv_ref[...])
    )
    result = state_grad_ref[...].reshape(x_s.shape) + norm_back(
        normed_grad * gain_one, unit_one, inverse_one)
    grad_ref[...] = spread_rows(result.astype(lowp), rows)[:, 0:seq]
    lines = [query_grad.astype(wide), value_grad.astype(wide), normed_grad * unit_one, normed_grad]
    small = jnp.concatenate(
        [jnp.sum(line, axis=0, keepdims=True) for line in lines]
        + [jnp.zeros((4, width), wide)], axis=0
    )
    sums_ref[small_at : small_at + 8, :] += small

    if not last:
        return

    @pl.when(step == pl.num_programs(0) - 1)
    def _():
        part_rows = piece_refs[0].shape[0]
        sums_ref[3 * width : 4 * width, :] = early_ref[0:width, :]
        sums_ref[small_at + 8 : small_at + small_rows, :] = early_ref[width:, :]
        exact = sums_ref[small_at : small_at + small_rows, :]
        sums_ref[small_at + small_rows : small_at + 2 * small_rows, :] = (
            exact - exact.astype(lowp).astype(wide)
        )
        for away in range(experts):
            start = pl.multiple_of((me_ref[1] ^ away) * part_rows, 16)
            piece_refs[away][...] = sums_ref[pl.ds(start, part_rows), :].astype(lowp)


def sum_kernel(*refs):
    total = refs[0][...].astype(wide)
    for ref in refs[1:-1]:
        total = total + ref[...].astype(wide)
    refs[-1][...] = total.astype(lowp)


def unpack_kernel(experts, me_ref, *refs):
    piece_refs, weight_refs = refs[:experts], refs[experts : experts + 4]
    small_ref, all_s = refs[experts + 4], refs[experts + 5]
    part_rows, width = piece_refs[0].shape
    small_rows = small_ref.shape[0]
    for away in range(experts):
        start = pl.multiple_of((me_ref[1] ^ away) * part_rows, 16)
        all_s[pl.ds(start, part_rows), :] = piece_refs[away][...].astype(wide)
    for which in range(4):
        weight_refs[which][...] = all_s[which * width : (which + 1) * width, :]
    at = 4 * width
    small_ref[...] = (all_s[at : at + small_rows, :]
                      + all_s[at + small_rows : at + 2 * small_rows, :])


def out_kernel(slots_ref, aug_ref, state_ref, rows_ref, out_ref):
    _, rows, width = state_ref.shape
    seq = out_ref.shape[1]
    slot_total = rows_ref.shape[0]
    lane = iota((rows, LANES), 1)
    gates = aug_ref[0, :, width : width + LANES].astype(wide)
    gate = [
        jnp.sum(jnp.where(lane == slots_ref[0, :, 2 + k : 3 + k], gates, 0.0), axis=1, keepdims=True)
        for k in range(2)
    ]
    first, second = slot_hits(slots_ref[0], (rows, slot_total))
    hits = jnp.where(first, gate[0], jnp.where(second, gate[1], 0.0)).astype(lowp)
    out_ref[0] = (state_ref[0] + dot(hits, rows_ref[...])).astype(lowp)[0:seq]


def adam_kernel(*refs):
    grad_ref, states, results, rounded_ref = refs[0], refs[1:7], refs[7:13], refs[13]
    corr_one = 1.0 - BETA_ONE**adam_steps
    corr_two = 1.0 - BETA_TWO**adam_steps
    for which in range(2):
        master, moment, second = (ref[0] for ref in states[which::2])
        grad = grad_ref[which].astype(wide)
        new_moment = BETA_ONE * moment + (1.0 - BETA_ONE) * grad
        new_second = BETA_TWO * second + (1.0 - BETA_TWO) * grad * grad
        update = (
            LEARN_RATE * (new_moment / corr_one) / (jnp.sqrt(new_second / corr_two) + ADAM_EPS)
        )
        new_master = master - update
        for ref, value in zip(results[which::2], (new_master, new_moment, new_second)):
            ref[0] = value
        rounded_ref[which] = new_master.astype(lowp)


def spread_kernel(rounded_ref, in_ref, out_ref):
    _, flat, inner = in_ref.shape
    width = out_ref.shape[2]
    for block in range(inner // width):
        in_ref[0, :, block * width : (block + 1) * width] = rounded_ref[
            0, block * flat : (block + 1) * flat, :]
    out_ref[0] = rounded_ref[1]


def whole(shape):
    return pl.BlockSpec(shape, lambda i: (0,) * len(shape))


def one(shape, pack=1):
    return pl.BlockSpec((pack,) + shape, lambda i: (i,) + (0,) * len(shape))


def smem():
    return pl.BlockSpec(memory_space=pltpu.SMEM)


def hbm():
    return pl.BlockSpec(memory_space=pl.ANY)


def call(kernel, micros, megabytes, name, grid, inputs, in_specs, out_specs, out_shape,
         scratch=(), after=(), aliases=None, prefetch=0):
    count, extra = len(inputs), len(after)

    def body(*refs):
        kernel(*refs[:count], *refs[count + extra :])

    return pl.pallas_call(
        body,
        grid_spec=pltpu.PrefetchScalarGridSpec(
            num_scalar_prefetch=prefetch, grid=grid, in_specs=in_specs + [hbm()] * extra,
            out_specs=out_specs, scratch_shapes=list(scratch)),
        out_shape=out_shape,
        input_output_aliases=aliases or {},
        compiler_params=params(len(grid), megabytes),
        cost_estimate=cost(micros),
        name=name,
    )(*inputs, *after)


def like(shape, dtype):
    return jax.ShapeDtypeStruct(shape, dtype)


def swap_expert(value, away, n_expert):
    return lax.ppermute(value, "expert", [(i, i ^ away) for i in range(n_expert)])


def on_device(n_expert, n_dp, images, cotangent, router_noise, routes, seat_order,
              norm1_gain, norm1_shift, query_weight, query_bias, key_weight, value_weight,
              value_bias, output_weight, output_bias, norm2_gain, norm2_shift, router_weight,
              expert_in, expert_out, master_in, master_out, moment_in, moment_out,
              second_in, second_out):
    count, seq, width = images.shape
    experts = router_noise.shape[2]
    cap = (count * seq * 2 + experts - 1) // experts
    gate_rows = (cap + width - 1) // width
    cap_rows = round_up(cap + 2 * gate_rows, 16)
    seq_rows = round_up(seq, 16)
    tokens = count * seq_rows
    inner = expert_in.shape[2]
    slot_total = experts * cap_rows
    aug = width + LANES
    me = jnp.stack([jnp.int32(0), lax.axis_index("expert").astype(jnp.int32)])
    vecs = jnp.stack([norm1_gain, norm1_shift, query_bias, value_bias, output_bias,
                      norm2_gain, norm2_shift, norm2_shift])

    slots, table, grad_rows = call(
        functools.partial(seat_kernel, experts, cap, cap_rows, seq_rows), 17, 56, "seat",
        (experts,), (routes, seat_order.reshape(routes.shape), cotangent),
        [whole(routes.shape), whole(routes.shape), whole(cotangent.shape)],
        [whole((count, seq_rows, 4)), whole((experts * 8, LANES)), one((cap_rows, width))],
        [like((count, seq_rows, 4), jnp.int32), like((experts * 8, LANES), wide),
         like((experts, cap_rows, width), lowp)],
        [pltpu.VMEM((tokens, 2), jnp.int32), pltpu.VMEM((tokens, 2), jnp.int32),
         pltpu.VMEM((tokens, width), lowp)])
    grad_in = lax.all_to_all(grad_rows, "expert", split_axis=0, concat_axis=0, tiled=True)

    square = (width, width)
    token_shape = (count, seq_rows, width)
    pack = PACK if count % PACK == 0 else 1
    query, key, value, lse, mixed, state, routed, probs = call(
        functools.partial(front_kernel, seq, experts, seq_rows), 19, 56, "front", (count // pack,),
        (me, images, router_noise, vecs, query_weight, key_weight, value_weight, output_weight,
         router_weight),
        [smem(), one((seq, width), pack), one((seq, experts), pack), whole((8, width)),
         whole(square), whole(square), whole(square), whole(square), whole((width, experts))],
        [one((seq_rows, width), pack)] * 3 + [
            one((seq_rows, LANES), pack), one((seq_rows, width), pack), one((seq_rows, width), pack),
            one((seq_rows, aug), pack), one((seq_rows, experts), pack)],
        [like(token_shape, lowp)] * 3 + [
            like((count, seq_rows, LANES), wide), like(token_shape, lowp),
            like(token_shape, wide), like((count, seq_rows, aug), lowp),
            like((count, seq_rows, experts), wide)],
        [pltpu.VMEM((pack * seq_rows, width), wide),
         pltpu.VMEM((pack * seq_rows, experts), wide)])

    quarter = max(experts // 4, 1)
    spans = [(first, first + quarter) for first in range(0, experts, quarter)]
    sent = [None] * experts
    chunk_spec, chunk_like = whole((cap_rows, width)), like((cap_rows, width), lowp)
    before = ()
    for first, size in [(quarter, quarter), (2 * quarter, quarter), (3 * quarter, quarter),
                        (0, quarter)]:
        outs = call(
            functools.partial(send_kernel, cap, gate_rows, first), 0.3, 32, f"send{first}",
            (1,), (me, table, routed.reshape(tokens, aug)),
            [smem(), whole((experts * 8, LANES)), whole((tokens, aug))],
            [chunk_spec] * size, [chunk_like] * size, after=before)
        sent[first : first + size] = outs
        before = (outs[0],)
    arrived = [sent[0]] + [swap_expert(sent[away], away, n_expert) for away in range(1, experts)]

    buffers = ()
    back_rows = []
    for first, end in spans:
        size = end - first
        block = lambda i, ref, first=first: (ref[1] ^ (first + i), 0, 0)
        fixed = lambda i, ref: (0, 0)
        line = lambda i, ref, first=first: (0, first + i, 0)
        chunk_at = pl.BlockSpec((cap_rows, width), fixed)
        outs = call(
            functools.partial(expert_kernel, cap, gate_rows, size), 0.3, 52, f"expert{first}",
            (size,),
            (me, *arrived[first:end], grad_in, expert_in[0],
             expert_out[0], *buffers),
            [chunk_at] * size + [
                pl.BlockSpec((1, cap_rows, width), block),
                pl.BlockSpec((width, inner), fixed), pl.BlockSpec((inner, width), fixed)]
            + [hbm()] * len(buffers),
            [chunk_at] * size + [
                pl.BlockSpec((1, cap_rows, width), block),
                pl.BlockSpec((2, cap_rows, inner), line), pl.BlockSpec((2, cap_rows, width), line)],
            [chunk_like] * size + [
                like((experts, cap_rows, width), lowp),
                like((2, slot_total, inner), lowp), like((2, slot_total, width), lowp)],
            [pltpu.VMEM((cap_rows, width), lowp)], prefetch=1,
            aliases={size + 4 + k: size + k for k in range(len(buffers))})
        back_rows += outs[:size]
        buffers = tuple(outs[size:])
    produced, inner_rows, outer_rows = buffers
    back_rows = [back_rows[0]] + [
        swap_expert(back_rows[away], away, n_expert) for away in range(1, experts)]

    steps = 4
    per = slot_total // steps

    line = lambda size: pl.BlockSpec((2, per, size), lambda i: (0, i, 0))
    weight_grads, produced = call(
        functools.partial(weight_kernel, n_dp), 0.02, 52, "weight", (steps,),
        (outer_rows, inner_rows, produced), [line(width), line(inner), hbm()],
        [whole((2 * inner, width)), hbm()],
        [like((2 * inner, width), lowp), like(produced.shape, lowp)],
        [pltpu.VMEM((width, inner), wide), pltpu.VMEM((width, inner), wide)],
        after=back_rows[1 : 3 * quarter], aliases={2: 1})
    tall, flat = inner // n_dp, width // n_dp
    share = lax.psum_scatter(weight_grads, "dp", scatter_dimension=0, tiled=True)
    returned = lax.all_to_all(produced, "expert", split_axis=0, concat_axis=0, tiled=True)

    early_small = 8 + round_up(experts, 8)
    early_rows = width + early_small
    state_grad, mixed_grad, early = call(
        functools.partial(combine_kernel, experts, cap, cap_rows, gate_rows, seq_rows), 300,
        56,
        "combine", (count // pack,),
        (me, slots, cotangent, mixed, state, probs, vecs, output_weight, router_weight,
         *back_rows),
        [smem(), one((seq_rows, 4), pack), one((seq, width), pack), one((seq_rows, width), pack),
         one((seq_rows, width), pack), one((seq_rows, experts), pack), whole((8, width)), whole(square),
         whole((width, experts))] + [chunk_spec] * experts,
        [one((seq_rows, width), pack), one((seq_rows, width), pack), whole((early_rows, width))],
        [like(token_shape, wide), like(token_shape, lowp), like((early_rows, width), wide)],
        [pltpu.VMEM((pack * seq_rows, width), wide), pltpu.VMEM((slot_total, aug), lowp)],
        after=(weight_grads,))

    small_rows = 8 + early_small
    part_rows = round_up(4 * width + 2 * small_rows, 16 * experts) // experts
    part_spec, part_like = whole((part_rows, width)), like((part_rows, width), lowp)
    pack = 2 if count % 2 == 0 else 1
    sums_like = like((part_rows * experts, width), wide)
    sums_spec = whole(sums_like.shape)

    def backward(first, steps, name, extra, extra_specs, outs, out_specs, scratch, after, aliases):
        at = lambda shape: pl.BlockSpec(
            (pack,) + shape, lambda i: (i + first,) + (0,) * len(shape))
        return call(
            functools.partial(back_kernel, seq, experts, small_rows, seq_rows, bool(extra)),
            300, 56, name, (steps,),
            (me, images, query, key, value, lse, state_grad, mixed_grad, vecs, query_weight,
             key_weight, value_weight, *extra),
            [smem(), at((seq, width))] + [at((seq_rows, width))] * 3
            + [at((seq_rows, LANES)), at((seq_rows, width)), at((seq_rows, width)),
               whole((8, width)), whole(square), whole(square), whole(square)] + extra_specs,
            [at((seq, width))] + out_specs, [like(images.shape, lowp)] + outs,
            [pltpu.VMEM((pack * seq_rows, width), wide)] + scratch, after=after, aliases=aliases)

    back_steps = count // pack
    images_grad, sums = backward(
        0, back_steps - 1, "back_most", (), [], [sums_like], [sums_spec], [], (), None)
    across = pl.BlockSpec((1, flat, width), lambda i: (0, 0, i))
    down = pl.BlockSpec((1, flat, width), lambda i: (0, i, 0))
    both = pl.BlockSpec((2, flat, width), lambda i: (0, i, 0))
    *states, rounded = call(
        adam_kernel, 1, 56, "adam", (inner // width,),
        (share.reshape(2, tall, width), master_in, master_out, moment_in, moment_out,
         second_in, second_out),
        [both] + [across, down] * 3, [across, down] * 3 + [both],
        [like(master_in.shape, wide), like(master_out.shape, wide)] * 3
        + [like((2, tall, width), lowp)], after=(sums, returned))
    images_grad, *pieces = backward(
        back_steps - 1, 1, "back_rest", (early, sums, images_grad),
        [whole((early_rows, width)), sums_spec, hbm()], [part_like] * experts,
        [part_spec] * experts, [pltpu.VMEM(sums_like.shape, wide)], (rounded,), {14: 0})

    def add(parts, name, after=()):
        return call(sum_kernel, 1, 56, name, (1,), parts, [part_spec] * len(parts), part_spec,
                    part_like, after=after)

    spread = lax.all_gather(rounded, "dp", axis=0, tiled=True)
    new_expert_in, new_expert_out = call(
        spread_kernel, 2, 56, "spread", (n_dp,), (spread,), [
            pl.BlockSpec((2, tall, width), lambda i: (i, 0, 0))],
        [pl.BlockSpec((1, flat, inner), lambda i: (0, i, 0)),
         pl.BlockSpec((1, tall, width), lambda i: (0, i, 0))],
        [like(expert_in.shape, lowp), like(expert_out.shape, lowp)])
    mine = add([pieces[0]] + [swap_expert(pieces[away], away, n_expert)
                              for away in range(1, experts)], "sum_plane",
               (returned, rounded))
    block_out = call(
        out_kernel, 1, 56, "block_out", (count,),
        (slots, routed, state, returned.reshape(slot_total, width)),
        [one((seq_rows, 4)), one((seq_rows, aug)), one((seq_rows, width)),
         whole((slot_total, width))],
        one((seq, width)), like(images.shape, lowp), after=(mine,))
    share = add([mine] + [
        lax.ppermute(mine, "dp", [(i, (i + shift) % n_dp) for i in range(n_dp)])
        for shift in range(1, n_dp)], "sum_dp", (block_out,))
    shares = [share] + [swap_expert(share, away, n_expert) for away in range(1, experts)]

    *big, small_sum = call(
        functools.partial(unpack_kernel, experts), 3, 56, "unpack", (1,), (me, *shares),
        [smem()] + [part_spec] * experts,
        [whole(square)] * 4 + [whole((small_rows, width))],
        [like(square, wide)] * 4 + [like((small_rows, width), wide)],
        [pltpu.VMEM((part_rows * experts, width), wide)], after=(new_expert_in,))
    return (
        block_out,
        images_grad,
        small_sum[2],
        small_sum[3],
        big[0],
        small_sum[0],
        big[1],
        big[2],
        small_sum[1],
        big[3],
        small_sum[8],
        small_sum[9],
        small_sum[10],
        small_sum[16 : 16 + experts].T,
        new_expert_in,
        new_expert_out,
        *states,
    )


def solution(mesh):
    both = ("dp", "expert")
    in_specs = (
        (P(both, None, None),) * 4
        + (P(both, None),)
        + (P(),) * 12
        + (P("expert", None, None),) * 2
        + (P("expert", "dp", None),) * 6
    )
    out_specs = (
        (P(both, None, None),) * 2
        + (P(),) * 12
        + (P("expert", None, None),) * 2
        + (P("expert", "dp", None),) * 6
    )
    body = functools.partial(on_device, mesh.shape["expert"], mesh.shape["dp"])
    return jax.shard_map(body, mesh=mesh, in_specs=in_specs, out_specs=out_specs, check_vma=False)
```

```python
import functools

import jax
import jax.numpy as jnp
from jax import lax
from jax.experimental import pallas as pl
from jax.experimental.pallas import tpu as pltpu
from jax.sharding import PartitionSpec as P

HEADS = 6
EPS_NORM = 1e-06
BETA_ONE = 0.9
BETA_TWO = 0.999
LEARN_RATE = 0.03
ADAM_EPS = 1e-08
adam_steps = 100.0

lowp = jnp.bfloat16
wide = jnp.float32
LANES = 128
HALF = 64
SHIFT = 6
PACK = 4


def round_up(value, step):
    return (value + step - 1) // step * step


def dot(left, right):
    return jnp.dot(left, right, preferred_element_type=wide)


def dot_nt(left, right):
    return lax.dot_general(left, right, (((1,), (1,)), ((), ())), preferred_element_type=wide)


def dot_tn(left, right):
    return lax.dot_general(left, right, (((0,), (0,)), ((), ())), preferred_element_type=wide)


def iota(shape, dim):
    return lax.broadcasted_iota(jnp.int32, shape, dim)


def cost(micros):
    return pl.CostEstimate(
        flops=int(micros * 1.1e9), bytes_accessed=int(micros * 3.5e6), transcendentals=0
    )


def params(dims, megabytes=24):
    return pltpu.CompilerParams(
        dimension_semantics=("arbitrary",) * dims, vmem_limit_bytes=megabytes * 1024 * 1024
    )


def unit_norm(values):
    mean = jnp.mean(values, axis=-1, keepdims=True)
    centred = values - mean
    inverse = lax.rsqrt(jnp.mean(centred * centred, axis=-1, keepdims=True) + EPS_NORM)
    return centred * inverse, inverse


def norm_back(scaled, unit, inverse):
    return inverse * (
        scaled
        - jnp.mean(scaled, axis=-1, keepdims=True)
        - unit * jnp.mean(scaled * unit, axis=-1, keepdims=True)
    )


def column_to_row(column, width, offset):
    shape = (column.shape[0], width)
    hit = iota(shape, 0) == iota(shape, 1) + offset
    return jnp.sum(jnp.where(hit, column, 0.0), axis=0, keepdims=True)


def row_to_column(row, rows, offset):
    shape = (rows, row.shape[1])
    hit = iota(shape, 0) == iota(shape, 1) + offset
    return jnp.sum(jnp.where(hit, row, 0.0), axis=1, keepdims=True)


def token_hits(table_ref, chunk, rows, tokens):
    slot = iota((rows, LANES), 0)
    lane = iota((rows, LANES), 1)
    picked = jnp.zeros((rows, LANES), wide)
    for high in range((rows + HALF - 1) // HALF):
        line = table_ref[pl.ds(chunk * 8 + high, 1), :]
        picked = jnp.where((slot >> SHIFT) == high, line, picked)
    picked = jnp.where((slot & (HALF - 1)) == (lane & (HALF - 1)), picked, 0.0)
    picked = picked * jnp.where(lane < HALF, float(HALF), 1.0)
    token = jnp.sum(picked, axis=1, keepdims=True).astype(jnp.int32) - 1
    return jnp.where(token == iota((rows, tokens), 1), 1.0, 0.0).astype(lowp)


def seat_kernel(experts, cap, cap_rows, seq_rows,
                routes_ref, order_ref, cot_ref, slots_ref, table_ref, rows_ref,
                route_s, order_s, flat_s):
    images, seq, _ = routes_ref.shape
    tokens = images * seq_rows
    step = pl.program_id(0)

    @pl.when(step == 0)
    def _():
        route_s[...] = jnp.full(route_s.shape, -1, jnp.int32)
        order_s[...] = jnp.zeros(order_s.shape, jnp.int32)
        flat_s[...] = jnp.zeros(flat_s.shape, lowp)
        for image in range(images):
            rows = pl.ds(image * seq_rows, seq)
            route_s[rows, :] = routes_ref[image]
            order_s[rows, :] = order_ref[image]
            flat_s[rows, :] = cot_ref[image]
        lane = iota((tokens, LANES), 1)
        wide_lane = iota((tokens, experts * HALF), 1)
        route = [route_s[:, k : k + 1] for k in range(2)]
        order = [order_s[:, k : k + 1] for k in range(2)]
        low_hit = [(order[k] & (HALF - 1)) == (lane & (HALF - 1)) for k in range(2)]
        low_b = [jnp.where(low_hit[k], 1.0, 0.0).astype(lowp) for k in range(2)]
        high_b = [
            jnp.where((route[k] * HALF + (order[k] >> SHIFT)) == wide_lane, 1.0, 0.0).astype(lowp)
            for k in range(2)
        ]
        counts = (dot_tn(low_b[0], high_b[0]) + dot_tn(low_b[1], high_b[1])).astype(lowp)
        before = iota((LANES, LANES), 0)
        after = iota((LANES, LANES), 1)
        upper = jnp.where((after < HALF) & (after < (before & (HALF - 1))), 1.0, 0.0).astype(lowp)
        within = dot(upper, counts)
        block = (experts * HALF, experts * HALF)
        earlier = jnp.where(
            ((iota(block, 0) >> SHIFT) == (iota(block, 1) >> SHIFT)) & (iota(block, 0) < iota(block, 1)),
            1.0, 0.0,
        ).astype(lowp)
        base = jnp.sum(dot(counts, earlier)[:HALF], axis=0, keepdims=True)
        place = within + base
        place_high = jnp.floor(place * (1.0 / HALF))
        place_low = place - place_high * HALF
        split = jnp.where(iota(place.shape, 0) < HALF, place_high, place_low).astype(lowp)
        weight = jnp.where(lane < HALF, float(HALF), 1.0)
        token = iota((tokens, LANES), 0) + 1
        table = jnp.zeros((experts * 8, LANES), wide)
        row = iota((tokens, experts * 8), 1)
        columns = iota((tokens, 4), 1)
        found = jnp.zeros((tokens, 4), jnp.int32)
        for k in range(2):
            gathered = dot_nt(high_b[k], split)
            position = jnp.sum(
                jnp.where(low_hit[k], gathered * weight, 0.0), axis=1, keepdims=True
            ).astype(jnp.int32)
            seated = (position < cap) & (route[k] >= 0)
            slot = jnp.where(seated, route[k] * cap_rows + position, -1)
            found = jnp.where(columns == k, slot, found)
            found = jnp.where(columns == 2 + k, route[k], found)
            which = jnp.where(seated, route[k] * 8 + (position >> SHIFT), -1)
            which_b = jnp.where(which == row, 1.0, 0.0).astype(lowp)
            value = jnp.where(lane < HALF, token >> SHIFT, token & (HALF - 1)).astype(wide)
            value_b = jnp.where((position & (HALF - 1)) == (lane & (HALF - 1)), value, 0.0).astype(lowp)
            table = table + dot_tn(which_b, value_b)
        table_ref[...] = table
        for image in range(images):
            slots_ref[image] = found[image * seq_rows : (image + 1) * seq_rows]

    hits = token_hits(table_ref, step, cap_rows, tokens)
    rows_ref[0] = dot(hits, flat_s[...]).astype(lowp)


def spread_rows(flat, rows):
    return flat.reshape(flat.shape[0] // rows, rows, flat.shape[1])


def load_rows(scratch, ref, rows):
    for image in range(ref.shape[0]):
        scratch[image * rows : image * rows + ref.shape[1], :] = ref[image].astype(wide)


def front_kernel(seq, experts, rows,
                 me_ref, x_ref, noise_ref, vec_ref, wq_ref, wk_ref, wv_ref, wo_ref, wr_ref,
                 q_ref, k_ref, v_ref, lse_ref, mix_ref, state_ref, aug_ref, probs_ref,
                 x_s, noise_s):
    pack, width = x_ref.shape[0], x_s.shape[1]

    @pl.when(pl.program_id(0) == 0)
    def _():
        x_s[...] = jnp.zeros(x_s.shape, wide)
        noise_s[...] = jnp.zeros(noise_s.shape, wide)

    load_rows(x_s, x_ref, rows)
    for image in range(pack):
        noise_s[image * rows : image * rows + seq, :] = noise_ref[image].T
    x = x_s[...]
    unit, _ = unit_norm(x)
    normed = (unit * vec_ref[0:1, :] + vec_ref[1:2, :]).astype(lowp)
    head_size = width // HEADS
    query = (dot(normed, wq_ref[...]) + vec_ref[2:3, :]).astype(lowp)
    query = query * (head_size ** -0.5)
    key = dot(normed, wk_ref[...]).astype(lowp)
    value = (dot(normed, wv_ref[...]) + vec_ref[3:4, :]).astype(lowp)
    q_ref[...] = spread_rows(query, rows)
    k_ref[...] = spread_rows(key, rows)
    v_ref[...] = spread_rows(value, rows)
    live = iota((rows, rows), 1) < seq
    lane = iota((rows, LANES), 1)
    mixed = []
    for image in range(pack):
        span = slice(image * rows, (image + 1) * rows)
        lse_all = jnp.zeros((rows, LANES), wide)
        joined = []
        for pair in range(HEADS // 2):
            cols = slice(pair * LANES, (pair + 1) * LANES)
            q2, k2, v2 = query[span, cols], key[span, cols], value[span, cols]
            outs = []
            for half in range(2):
                mine = (lane < HALF) if half == 0 else (lane >= HALF)
                scores = dot_nt(jnp.where(mine, q2, jnp.zeros_like(q2)), k2)
                scores = jnp.where(live, scores, -1e30)
                peak = jnp.max(scores, axis=1, keepdims=True)
                expo = jnp.exp(scores - peak)
                total = jnp.sum(expo, axis=1, keepdims=True)
                lse_all = jnp.where(lane == pair * 2 + half, peak + jnp.log(total), lse_all)
                outs.append(dot((expo / total).astype(lowp), v2))
            joined.append(jnp.where(lane < HALF, outs[0], outs[1]).astype(lowp))
        lse_ref[image] = lse_all.T[0:8]
        mixed.append(jnp.concatenate(joined, axis=1))
    mixed = jnp.concatenate(mixed, axis=0)
    mix_ref[...] = spread_rows(mixed, rows)
    state = x + dot(mixed, wo_ref[...]) + vec_ref[4:5, :]
    state_ref[...] = spread_rows(state, rows)
    unit_two, _ = unit_norm(state)
    routed = (unit_two * vec_ref[5:6, :] + vec_ref[6:7, :]).astype(lowp)
    logits = dot_nt(routed, wr_ref[...]) + noise_s[...]
    top = jnp.max(logits, axis=1, keepdims=True)
    expo = jnp.exp(logits - top)
    probs = expo / jnp.sum(expo, axis=1, keepdims=True)
    probs_ref[...] = spread_rows(probs, rows)
    shape = (experts, LANES)
    widen = jnp.where(iota(shape, 0) == iota(shape, 1), 1.0, 0.0).astype(lowp)
    aug_ref[:, :, 0:width] = spread_rows(routed, rows)
    aug_ref[:, :, width : width + LANES] = spread_rows(
        dot(probs.astype(lowp), widen).astype(lowp), rows)


def send_kernel(cap, gate_rows, first, me_ref, table_ref, aug_ref, *out_refs):
    cap_rows, width = out_refs[0].shape
    tokens = aug_ref.shape[0]
    for index, out_ref in enumerate(out_refs):
        chunk = me_ref[0] ^ (first + index)
        hits = token_hits(table_ref, chunk, cap_rows, tokens)
        full = dot(hits, aug_ref[...])
        rows = full[:, 0:width]
        lane = iota((cap_rows, LANES), 1)
        gate = jnp.sum(jnp.where(lane == chunk, full[:, width:], 0.0), axis=1, keepdims=True)
        at = iota((cap_rows, width), 0)
        for part in range(gate_rows):
            line = column_to_row(gate, width, part * width)
            rows = jnp.where(at == cap + part, line, rows)
        out_ref[...] = rows.astype(lowp)


def expert_kernel(cap, gate_rows, size, me_ref, *refs):
    x_refs, (g_ref, win_ref, wout_ref) = refs[:size], refs[size : size + 3]
    back_refs = refs[-size - 4 : -4]
    prod_ref, inner_ref, rows_ref, x_s = refs[-4:]
    cap_rows, width = x_s.shape
    step = pl.program_id(0)
    for index in range(size):

        @pl.when(step == index)
        def _(index=index):
            x_s[...] = x_refs[index][...]

    x = x_s[...]
    rows_ref[0] = x
    grad = g_ref[0].astype(wide)
    gate = jnp.zeros((cap_rows, 1), wide)
    for part in range(gate_rows):
        line = x_s[cap + part : cap + part + 1, :].astype(wide)
        gate = gate + row_to_column(line, cap_rows, part * width)
    gate = jnp.where(iota((cap_rows, 1), 0) < cap, gate, 0.0)
    slot_grad = (gate * grad).astype(lowp)
    rows_ref[1] = slot_grad
    outer = (2.0 / jnp.pi) ** 0.5
    pre = dot(x, win_ref[...])
    hidden = dot_nt(slot_grad, wout_ref[...])
    square = pre * pre
    half = 0.5 * jnp.tanh(pre * (outer + (outer * 0.044715) * square)) + 0.5
    act = (pre * half).astype(lowp)
    slope = half * (
        1.0 + (1.0 - half) * (pre * (2.0 * outer + (6.0 * outer * 0.044715) * square))
    )
    pre_grad = (hidden * slope).astype(lowp)
    inner_ref[0] = pre_grad
    inner_ref[1] = act
    back = dot_nt(pre_grad, win_ref[...])
    made = dot(act, wout_ref[...]).astype(lowp)
    prod_ref[0] = made
    gate_grad = jnp.sum(grad * made.astype(wide), axis=1, keepdims=True)
    at = iota((cap_rows, width), 0)
    for part in range(gate_rows):
        line = column_to_row(gate_grad, width, part * width)
        high = line.astype(lowp).astype(wide)
        back = jnp.where(at == cap + part, high, back)
        back = jnp.where(at == cap + gate_rows + part, line - high, back)
    for index in range(size):

        @pl.when(step == index)
        def _(index=index):
            back_refs[index][...] = back.astype(lowp)


def weight_kernel(n_dp, rows_ref, inner_ref, through_ref, out_ref, passed_ref, in_s, out_s):
    step = pl.program_id(0)
    width, inner = in_s.shape

    @pl.when(step == 0)
    def _():
        in_s[...] = jnp.zeros(in_s.shape, wide)
        out_s[...] = jnp.zeros(out_s.shape, wide)

    in_s[...] += dot_tn(rows_ref[0], inner_ref[0])
    out_s[...] += dot_tn(rows_ref[1], inner_ref[1])

    @pl.when(step == pl.num_programs(0) - 1)
    def _():
        tall, flat = inner // n_dp, width // n_dp
        for owner in range(n_dp):
            base = owner * 2 * tall
            for block in range(inner // width):
                out_ref[base + block * flat : base + (block + 1) * flat, :] = in_s[
                    owner * flat : (owner + 1) * flat, block * width : (block + 1) * width
                ].astype(lowp)
            out_ref[base + tall : base + 2 * tall, :] = (
                out_s[:, owner * tall : (owner + 1) * tall].T.astype(lowp))


def slot_hits(slots, shape):
    at = iota(shape, 1)
    return slots[:, 0:1] == at, slots[:, 1:2] == at


def combine_kernel(experts, cap, cap_rows, gate_rows, rows,
                   me_ref, slots_ref, cot_ref, mix_ref, state_ref, probs_ref, vec_ref, wo_ref,
                   wr_ref, *rest):
    rows_refs, (state_grad_ref, mixed_grad_ref, sums_ref, cot_s, aug_s) = (
        rest[:experts], rest[experts:])
    step = pl.program_id(0)
    width = cot_s.shape[1]

    @pl.when(step == 0)
    def _():
        cot_s[...] = jnp.zeros(cot_s.shape, wide)
        sums_ref[...] = jnp.zeros(sums_ref.shape, wide)
        for away in range(experts):
            rows_ref = rows_refs[away]
            chunk = me_ref[0] ^ away
            lane = iota((cap_rows, LANES), 1)
            extra = jnp.zeros((cap_rows, LANES), wide)
            for part in range(gate_rows):
                for piece in range(2):
                    row = cap + piece * gate_rows + part
                    line = rows_ref[row : row + 1, :].astype(wide)
                    column = row_to_column(line, cap_rows, part * width)
                    extra = jnp.where(lane == chunk + piece * HALF, extra + column, extra)
            at = pl.ds(pl.multiple_of(chunk * cap_rows, 16), cap_rows)
            aug_s[at, 0:width] = rows_ref[...]
            aug_s[at, width : width + LANES] = extra.astype(lowp)

    load_rows(cot_s, cot_ref, rows)
    slots = slots_ref[...].reshape(cot_s.shape[0], 4)
    first, second = slot_hits(slots, (cot_s.shape[0], experts * cap_rows))
    hits = jnp.where(first | second, 1.0, 0.0).astype(lowp)
    full = dot(hits, aug_s[...])
    shape = (LANES, experts)
    narrow = jnp.where((iota(shape, 0) & (HALF - 1)) == iota(shape, 1), 1.0, 0.0)
    prob_grad = dot(full[:, width:].astype(lowp), narrow.astype(lowp))
    flat = lambda ref: ref[...].reshape(cot_s.shape[0], ref.shape[2])
    probs = flat(probs_ref)
    logit_grad = (
        probs * (prob_grad - jnp.sum(probs * prob_grad, axis=1, keepdims=True))
    ).astype(lowp)
    routed_grad = full[:, 0:width] + dot(logit_grad, wr_ref[...])
    unit_two, inverse_two = unit_norm(flat(state_ref))
    gain_two = vec_ref[5:6, :]
    routed = (unit_two * gain_two + vec_ref[6:7, :]).astype(lowp)
    state_grad = cot_s[...] + norm_back(routed_grad * gain_two, unit_two, inverse_two)
    branch = state_grad.astype(lowp)
    state_grad_ref[...] = spread_rows(state_grad, rows)
    mixed_grad_ref[...] = spread_rows(dot_nt(branch, wo_ref[...]).astype(lowp), rows)
    sums_ref[0:width, :] += dot_tn(flat(mix_ref), branch)
    lines = [branch.astype(wide), routed_grad * unit_two, routed_grad]
    small = jnp.concatenate(
        [jnp.sum(line, axis=0, keepdims=True) for line in lines]
        + [jnp.zeros((5, width), wide)], axis=0
    )
    sums_ref[width : width + 8, :] += small
    sums_ref[width + 8 : width + 8 + experts, :] += dot_tn(logit_grad, routed)


def back_kernel(seq, experts, small_rows, rows,
                me_ref, x_ref, q_ref, k_ref, v_ref, lse_ref, state_grad_ref, mixed_grad_ref,
                vec_ref, wq_ref, wk_ref, wv_ref, *rest):
    early_ref, grad_ref, *piece_refs, x_s, sums_ref = rest
    step = pl.program_id(0)
    width = x_s.shape[1]
    pack = x_ref.shape[0]
    small_at = 4 * width

    @pl.when(step == 0)
    def _():
        x_s[...] = jnp.zeros(x_s.shape, wide)
        sums_ref[...] = jnp.zeros(sums_ref.shape, wide)

    load_rows(x_s, x_ref, rows)
    live = iota((rows, rows), 0) < seq
    lane = iota((rows, LANES), 1)
    scale = (width // HEADS) ** -0.5
    parts = [[], [], []]
    for image in range(pack):
        query, key, value = q_ref[image], k_ref[image], v_ref[image]
        mixed_grad, lse = mixed_grad_ref[image], lse_ref[image]
        lines = [[], [], []]
        for pair in range(HEADS // 2):
            cols = slice(pair * LANES, (pair + 1) * LANES)
            q2, k2, v2, g2 = query[:, cols], key[:, cols], value[:, cols], mixed_grad[:, cols]
            outs = [[], [], []]
            for half in range(2):
                mine = (lane < HALF) if half == 0 else (lane >= HALF)
                scores = dot_nt(k2, jnp.where(mine, q2, jnp.zeros_like(q2)))
                head = pair * 2 + half
                weights = jnp.exp(jnp.where(live, scores - lse[head : head + 1, :], -1e30))
                weight_grad = dot_nt(v2, jnp.where(mine, g2, jnp.zeros_like(g2)))
                product = weights * weight_grad
                score_grad = (
                    product - weights * jnp.sum(product, axis=0, keepdims=True)
                ).astype(lowp)
                outs[0].append(dot_tn(score_grad, k2))
                outs[1].append(dot(score_grad, q2))
                outs[2].append(dot(weights.astype(lowp), g2))
            for which in range(3):
                joined = jnp.where(lane < HALF, outs[which][0], outs[which][1])
                if which == 0:
                    joined = joined * scale
                lines[which].append(joined.astype(lowp))
        for which in range(3):
            parts[which].append(jnp.concatenate(lines[which], axis=1))
    query_grad, key_grad, value_grad = (jnp.concatenate(p, axis=0) for p in parts)
    unit_one, inverse_one = unit_norm(x_s[...])
    gain_one = vec_ref[0:1, :]
    normed = (unit_one * gain_one + vec_ref[1:2, :]).astype(lowp)
    sums_ref[0:width, :] += dot_tn(normed, query_grad)
    sums_ref[width : 2 * width, :] += dot_tn(normed, key_grad)
    sums_ref[2 * width : 3 * width, :] += dot_tn(normed, value_grad)
    normed_grad = (
        dot_nt(query_grad, wq_ref[...])
        + dot_nt(key_grad, wk_ref[...])
        + dot_nt(value_grad, wv_ref[...])
    )
    result = state_grad_ref[...].reshape(x_s.shape) + norm_back(
        normed_grad * gain_one, unit_one, inverse_one)
    grad_ref[...] = spread_rows(result.astype(lowp), rows)[:, 0:seq]
    lines = [query_grad.astype(wide), value_grad.astype(wide), normed_grad * unit_one, normed_grad]
    small = jnp.concatenate(
        [jnp.sum(line, axis=0, keepdims=True) for line in lines]
        + [jnp.zeros((4, width), wide)], axis=0
    )
    sums_ref[small_at : small_at + 8, :] += small

    @pl.when(step == pl.num_programs(0) - 1)
    def _():
        part_rows = piece_refs[0].shape[0]
        sums_ref[3 * width : 4 * width, :] = early_ref[0:width, :]
        sums_ref[small_at + 8 : small_at + small_rows, :] = early_ref[width:, :]
        exact = sums_ref[small_at : small_at + small_rows, :]
        sums_ref[small_at + small_rows : small_at + 2 * small_rows, :] = (
            exact - exact.astype(lowp).astype(wide)
        )
        for away in range(experts):
            start = pl.multiple_of((me_ref[0] ^ away) * part_rows, 16)
            piece_refs[away][...] = sums_ref[pl.ds(start, part_rows), :].astype(lowp)


def sum_kernel(*refs):
    total = refs[0][...].astype(wide)
    for ref in refs[1:-1]:
        total = total + ref[...].astype(wide)
    refs[-1][...] = total.astype(lowp)


def unpack_kernel(experts, me_ref, *refs):
    piece_refs, weight_refs = refs[:experts], refs[experts : experts + 4]
    small_ref, all_s = refs[experts + 4], refs[experts + 5]
    part_rows, width = piece_refs[0].shape
    small_rows = small_ref.shape[0]
    for away in range(experts):
        start = pl.multiple_of((me_ref[0] ^ away) * part_rows, 16)
        all_s[pl.ds(start, part_rows), :] = piece_refs[away][...].astype(wide)
    for which in range(4):
        weight_refs[which][...] = all_s[which * width : (which + 1) * width, :]
    at = 4 * width
    small_ref[...] = (all_s[at : at + small_rows, :]
                      + all_s[at + small_rows : at + 2 * small_rows, :])


def out_kernel(slots_ref, aug_ref, state_ref, rows_ref, out_ref):
    _, rows, width = state_ref.shape
    seq = out_ref.shape[1]
    slot_total = rows_ref.shape[0]
    lane = iota((rows, LANES), 1)
    gates = aug_ref[0, :, width : width + LANES].astype(wide)
    gate = [
        jnp.sum(jnp.where(lane == slots_ref[0, :, 2 + k : 3 + k], gates, 0.0), axis=1, keepdims=True)
        for k in range(2)
    ]
    first, second = slot_hits(slots_ref[0], (rows, slot_total))
    hits = jnp.where(first, gate[0], jnp.where(second, gate[1], 0.0)).astype(lowp)
    out_ref[0] = (state_ref[0] + dot(hits, rows_ref[...])).astype(lowp)[0:seq]


def adam_kernel(*refs):
    grad_ref, states, results, rounded_ref = refs[0], refs[1:7], refs[7:13], refs[13]
    corr_one = 1.0 - BETA_ONE**adam_steps
    corr_two = 1.0 - BETA_TWO**adam_steps
    for which in range(2):
        master, moment, second = (ref[0] for ref in states[which::2])
        grad = grad_ref[which].astype(wide)
        new_moment = BETA_ONE * moment + (1.0 - BETA_ONE) * grad
        new_second = BETA_TWO * second + (1.0 - BETA_TWO) * grad * grad
        update = (
            LEARN_RATE * (new_moment / corr_one) / (jnp.sqrt(new_second / corr_two) + ADAM_EPS)
        )
        new_master = master - update
        for ref, value in zip(results[which::2], (new_master, new_moment, new_second)):
            ref[0] = value
        rounded_ref[which] = new_master.astype(lowp)


def spread_kernel(rounded_ref, in_ref, out_ref):
    _, flat, inner = in_ref.shape
    width = out_ref.shape[2]
    for block in range(inner // width):
        in_ref[0, :, block * width : (block + 1) * width] = rounded_ref[
            0, block * flat : (block + 1) * flat, :]
    out_ref[0] = rounded_ref[1]


def whole(shape):
    return pl.BlockSpec(shape, lambda i: (0,) * len(shape))


def one(shape, pack=1):
    return pl.BlockSpec((pack,) + shape, lambda i: (i,) + (0,) * len(shape))


def smem():
    return pl.BlockSpec(memory_space=pltpu.SMEM)


def hbm():
    return pl.BlockSpec(memory_space=pl.ANY)


def call(kernel, micros, megabytes, name, grid, inputs, in_specs, out_specs, out_shape,
         scratch=(), after=(), aliases=None, prefetch=0):
    count, extra = len(inputs), len(after)

    def body(*refs):
        kernel(*refs[:count], *refs[count + extra :])

    return pl.pallas_call(
        body,
        grid_spec=pltpu.PrefetchScalarGridSpec(
            num_scalar_prefetch=prefetch, grid=grid, in_specs=in_specs + [hbm()] * extra,
            out_specs=out_specs, scratch_shapes=list(scratch)),
        out_shape=out_shape,
        input_output_aliases=aliases or {},
        compiler_params=params(len(grid), megabytes),
        cost_estimate=cost(micros),
        name=name,
    )(*inputs, *after)


def like(shape, dtype):
    return jax.ShapeDtypeStruct(shape, dtype)


def swap_expert(value, away, n_expert):
    return lax.ppermute(value, "expert", [(i, i ^ away) for i in range(n_expert)])


def on_device(n_expert, n_dp, images, cotangent, router_noise, routes, seat_order,
              norm1_gain, norm1_shift, query_weight, query_bias, key_weight, value_weight,
              value_bias, output_weight, output_bias, norm2_gain, norm2_shift, router_weight,
              expert_in, expert_out, master_in, master_out, moment_in, moment_out,
              second_in, second_out):
    count, seq, width = images.shape
    experts = router_noise.shape[2]
    cap = (count * seq * 2 + experts - 1) // experts
    gate_rows = (cap + width - 1) // width
    cap_rows = round_up(cap + 2 * gate_rows, 16)
    seq_rows = round_up(seq, 16)
    tokens = count * seq_rows
    inner = expert_in.shape[2]
    slot_total = experts * cap_rows
    aug = width + LANES
    me = lax.axis_index("expert").astype(jnp.int32).reshape(1)
    router_rows = router_weight.T
    noise_rows = router_noise.transpose(0, 2, 1)
    vecs = jnp.stack([norm1_gain, norm1_shift, query_bias, value_bias, output_bias,
                      norm2_gain, norm2_shift, norm2_shift])

    slots, table, grad_rows = call(
        functools.partial(seat_kernel, experts, cap, cap_rows, seq_rows), 17, 56, "seat",
        (experts,), (routes, seat_order.reshape(routes.shape), cotangent),
        [whole(routes.shape), whole(routes.shape), whole(cotangent.shape)],
        [whole((count, seq_rows, 4)), whole((experts * 8, LANES)), one((cap_rows, width))],
        [like((count, seq_rows, 4), jnp.int32), like((experts * 8, LANES), wide),
         like((experts, cap_rows, width), lowp)],
        [pltpu.VMEM((tokens, 2), jnp.int32), pltpu.VMEM((tokens, 2), jnp.int32),
         pltpu.VMEM((tokens, width), lowp)])
    grad_in = lax.all_to_all(grad_rows, "expert", split_axis=0, concat_axis=0, tiled=True)

    square = (width, width)
    token_shape = (count, seq_rows, width)
    pack = PACK if count % PACK == 0 else 1
    query, key, value, lse, mixed, state, routed, probs = call(
        functools.partial(front_kernel, seq, experts, seq_rows), 19, 56, "front", (count // pack,),
        (me, images, noise_rows, vecs, query_weight, key_weight, value_weight, output_weight,
         router_rows),
        [smem(), one((seq, width), pack), one((experts, seq), pack), whole((8, width)),
         whole(square), whole(square), whole(square), whole(square), whole((experts, width))],
        [one((seq_rows, width), pack)] * 3 + [
            one((8, seq_rows), pack), one((seq_rows, width), pack), one((seq_rows, width), pack),
            one((seq_rows, aug), pack), one((seq_rows, experts), pack)],
        [like(token_shape, lowp)] * 3 + [
            like((count, 8, seq_rows), wide), like(token_shape, lowp),
            like(token_shape, wide), like((count, seq_rows, aug), lowp),
            like((count, seq_rows, experts), wide)],
        [pltpu.VMEM((pack * seq_rows, width), wide),
         pltpu.VMEM((pack * seq_rows, experts), wide)])

    quarter = max(experts // 4, 1)
    spans = [(first, first + quarter) for first in range(0, experts, quarter)]
    sent = [None] * experts
    chunk_spec, chunk_like = whole((cap_rows, width)), like((cap_rows, width), lowp)
    before = ()
    for first, size in [(quarter, quarter), (2 * quarter, quarter), (3 * quarter, quarter),
                        (0, quarter)]:
        outs = call(
            functools.partial(send_kernel, cap, gate_rows, first), 0.3, 32, f"send{first}",
            (1,), (me, table, routed.reshape(tokens, aug)),
            [smem(), whole((experts * 8, LANES)), whole((tokens, aug))],
            [chunk_spec] * size, [chunk_like] * size, after=before)
        sent[first : first + size] = outs
        before = (outs[0],)
    arrived = [sent[0]] + [swap_expert(sent[away], away, n_expert) for away in range(1, experts)]

    buffers = ()
    back_rows = []
    for first, end in spans:
        size = end - first
        block = lambda i, ref, first=first: (ref[0] ^ (first + i), 0, 0)
        fixed = lambda i, ref: (0, 0)
        line = lambda i, ref, first=first: (0, first + i, 0)
        chunk_at = pl.BlockSpec((cap_rows, width), fixed)
        outs = call(
            functools.partial(expert_kernel, cap, gate_rows, size), 0.3, 52, f"expert{first}",
            (size,),
            (me, *arrived[first:end], grad_in, expert_in[0],
             expert_out[0], *buffers),
            [chunk_at] * size + [
                pl.BlockSpec((1, cap_rows, width), block),
                pl.BlockSpec((width, inner), fixed), pl.BlockSpec((inner, width), fixed)]
            + [hbm()] * len(buffers),
            [chunk_at] * size + [
                pl.BlockSpec((1, cap_rows, width), block),
                pl.BlockSpec((2, cap_rows, inner), line), pl.BlockSpec((2, cap_rows, width), line)],
            [chunk_like] * size + [
                like((experts, cap_rows, width), lowp),
                like((2, slot_total, inner), lowp), like((2, slot_total, width), lowp)],
            [pltpu.VMEM((cap_rows, width), lowp)], prefetch=1,
            aliases={size + 4 + k: size + k for k in range(len(buffers))})
        back_rows += outs[:size]
        buffers = tuple(outs[size:])
    produced, inner_rows, outer_rows = buffers
    back_rows = [back_rows[0]] + [
        swap_expert(back_rows[away], away, n_expert) for away in range(1, experts)]

    steps = 4
    per = slot_total // steps

    line = lambda size: pl.BlockSpec((2, per, size), lambda i: (0, i, 0))
    weight_grads, produced = call(
        functools.partial(weight_kernel, n_dp), 0.02, 52, "weight", (steps,),
        (outer_rows, inner_rows, produced), [line(width), line(inner), hbm()],
        [whole((2 * inner, width)), hbm()],
        [like((2 * inner, width), lowp), like(produced.shape, lowp)],
        [pltpu.VMEM((width, inner), wide), pltpu.VMEM((width, inner), wide)],
        after=back_rows[1 : 3 * quarter], aliases={2: 1})
    tall, flat = inner // n_dp, width // n_dp
    share = lax.psum_scatter(weight_grads, "dp", scatter_dimension=0, tiled=True)
    returned = lax.all_to_all(produced, "expert", split_axis=0, concat_axis=0, tiled=True)

    early_small = 8 + round_up(experts, 8)
    early_rows = width + early_small
    state_grad, mixed_grad, early = call(
        functools.partial(combine_kernel, experts, cap, cap_rows, gate_rows, seq_rows), 300,
        56,
        "combine", (count // pack,),
        (me, slots, cotangent, mixed, state, probs, vecs, output_weight, router_rows,
         *back_rows),
        [smem(), one((seq_rows, 4), pack), one((seq, width), pack), one((seq_rows, width), pack),
         one((seq_rows, width), pack), one((seq_rows, experts), pack), whole((8, width)), whole(square),
         whole((experts, width))] + [chunk_spec] * experts,
        [one((seq_rows, width), pack), one((seq_rows, width), pack), whole((early_rows, width))],
        [like(token_shape, wide), like(token_shape, lowp), like((early_rows, width), wide)],
        [pltpu.VMEM((pack * seq_rows, width), wide), pltpu.VMEM((slot_total, aug), lowp)],
        after=(weight_grads,))

    small_rows = 8 + early_small
    part_rows = round_up(4 * width + 2 * small_rows, 16 * experts) // experts
    part_spec, part_like = whole((part_rows, width)), like((part_rows, width), lowp)
    pack = 2 if count % 2 == 0 else 1
    images_grad, *pieces = call(
        functools.partial(back_kernel, seq, experts, small_rows, seq_rows), 300, 56, "back",
        (count // pack,),
        (me, images, query, key, value, lse, state_grad, mixed_grad, vecs, query_weight,
         key_weight, value_weight, early),
        [smem(), one((seq, width), pack)] + [one((seq_rows, width), pack)] * 3
        + [one((8, seq_rows), pack), one((seq_rows, width), pack), one((seq_rows, width), pack),
           whole((8, width)), whole(square), whole(square), whole(square),
           whole((early_rows, width))],
        [one((seq, width), pack)] + [part_spec] * experts,
        [like(images.shape, lowp)] + [part_like] * experts,
        [pltpu.VMEM((pack * seq_rows, width), wide), pltpu.VMEM((part_rows * experts, width), wide)])
    across = pl.BlockSpec((1, flat, width), lambda i: (0, 0, i))
    down = pl.BlockSpec((1, flat, width), lambda i: (0, i, 0))
    both = pl.BlockSpec((2, flat, width), lambda i: (0, i, 0))
    *states, rounded = call(
        adam_kernel, 1, 56, "adam", (inner // width,),
        (share.reshape(2, tall, width), master_in, master_out, moment_in, moment_out,
         second_in, second_out),
        [both] + [across, down] * 3, [across, down] * 3 + [both],
        [like(master_in.shape, wide), like(master_out.shape, wide)] * 3
        + [like((2, tall, width), lowp)], after=(pieces[0], returned))

    def add(parts, name, after=()):
        return call(sum_kernel, 1, 56, name, (1,), parts, [part_spec] * len(parts), part_spec,
                    part_like, after=after)

    spread = lax.all_gather(rounded, "dp", axis=0, tiled=True)
    new_expert_in, new_expert_out = call(
        spread_kernel, 2, 56, "spread", (n_dp,), (spread,), [
            pl.BlockSpec((2, tall, width), lambda i: (i, 0, 0))],
        [pl.BlockSpec((1, flat, inner), lambda i: (0, i, 0)),
         pl.BlockSpec((1, tall, width), lambda i: (0, i, 0))],
        [like(expert_in.shape, lowp), like(expert_out.shape, lowp)])
    mine = add([pieces[0]] + [swap_expert(pieces[away], away, n_expert)
                              for away in range(1, experts)], "sum_plane",
               (returned, rounded))
    block_out = call(
        out_kernel, 1, 56, "block_out", (count,),
        (slots, routed, state, returned.reshape(slot_total, width)),
        [one((seq_rows, 4)), one((seq_rows, aug)), one((seq_rows, width)),
         whole((slot_total, width))],
        one((seq, width)), like(images.shape, lowp), after=(mine,))
    share = add([mine] + [
        lax.ppermute(mine, "dp", [(i, (i + shift) % n_dp) for i in range(n_dp)])
        for shift in range(1, n_dp)], "sum_dp", (block_out,))
    shares = [share] + [swap_expert(share, away, n_expert) for away in range(1, experts)]

    *big, small_sum = call(
        functools.partial(unpack_kernel, experts), 3, 56, "unpack", (1,), (me, *shares),
        [smem()] + [part_spec] * experts,
        [whole(square)] * 4 + [whole((small_rows, width))],
        [like(square, wide)] * 4 + [like((small_rows, width), wide)],
        [pltpu.VMEM((part_rows * experts, width), wide)], after=(new_expert_in,))
    return (
        block_out,
        images_grad,
        small_sum[2],
        small_sum[3],
        big[0],
        small_sum[0],
        big[1],
        big[2],
        small_sum[1],
        big[3],
        small_sum[8],
        small_sum[9],
        small_sum[10],
        small_sum[16 : 16 + experts].T,
        new_expert_in,
        new_expert_out,
        *states,
    )


def solution(mesh):
    both = ("dp", "expert")
    in_specs = (
        (P(both, None, None),) * 4
        + (P(both, None),)
        + (P(),) * 12
        + (P("expert", None, None),) * 2
        + (P("expert", "dp", None),) * 6
    )
    out_specs = (
        (P(both, None, None),) * 2
        + (P(),) * 12
        + (P("expert", None, None),) * 2
        + (P("expert", "dp", None),) * 6
    )
    body = functools.partial(on_device, mesh.shape["expert"], mesh.shape["dp"])
    return jax.shard_map(body, mesh=mesh, in_specs=in_specs, out_specs=out_specs, check_vma=False)
```

```python
import functools

import jax
import jax.numpy as jnp
from jax import lax
from jax.experimental import pallas as pl
from jax.experimental.pallas import tpu as pltpu
from jax.sharding import PartitionSpec as P

HEADS = 6
EPS_NORM = 1e-06
BETA_ONE = 0.9
BETA_TWO = 0.999
LEARN_RATE = 0.03
ADAM_EPS = 1e-08
adam_steps = 100.0

lowp = jnp.bfloat16
wide = jnp.float32
LANES = 128
HALF = 64
SHIFT = 6
PACK = 4


def round_up(value, step):
    return (value + step - 1) // step * step


def dot(left, right):
    return jnp.dot(left, right, preferred_element_type=wide)


def dot_nt(left, right):
    return lax.dot_general(left, right, (((1,), (1,)), ((), ())), preferred_element_type=wide)


def dot_tn(left, right):
    return lax.dot_general(left, right, (((0,), (0,)), ((), ())), preferred_element_type=wide)


def iota(shape, dim):
    return lax.broadcasted_iota(jnp.int32, shape, dim)


def cost(micros):
    return pl.CostEstimate(
        flops=int(micros * 1.1e9), bytes_accessed=int(micros * 3.5e6), transcendentals=0
    )


def params(dims, megabytes=24):
    return pltpu.CompilerParams(
        dimension_semantics=("arbitrary",) * dims, vmem_limit_bytes=megabytes * 1024 * 1024
    )


def unit_norm(values):
    mean = jnp.mean(values, axis=-1, keepdims=True)
    centred = values - mean
    inverse = lax.rsqrt(jnp.mean(centred * centred, axis=-1, keepdims=True) + EPS_NORM)
    return centred * inverse, inverse


def norm_back(scaled, unit, inverse):
    return inverse * (
        scaled
        - jnp.mean(scaled, axis=-1, keepdims=True)
        - unit * jnp.mean(scaled * unit, axis=-1, keepdims=True)
    )


def column_to_row(column, width, offset):
    shape = (column.shape[0], width)
    hit = iota(shape, 0) == iota(shape, 1) + offset
    return jnp.sum(jnp.where(hit, column, 0.0), axis=0, keepdims=True)


def row_to_column(row, rows, offset):
    shape = (rows, row.shape[1])
    hit = iota(shape, 0) == iota(shape, 1) + offset
    return jnp.sum(jnp.where(hit, row, 0.0), axis=1, keepdims=True)


def token_hits(table_ref, chunk, rows, tokens):
    slot = iota((rows, LANES), 0)
    lane = iota((rows, LANES), 1)
    picked = jnp.zeros((rows, LANES), wide)
    for high in range((rows + HALF - 1) // HALF):
        line = table_ref[pl.ds(chunk * 8 + high, 1), :]
        picked = jnp.where((slot >> SHIFT) == high, line, picked)
    picked = jnp.where((slot & (HALF - 1)) == (lane & (HALF - 1)), picked, 0.0)
    picked = picked * jnp.where(lane < HALF, float(HALF), 1.0)
    token = jnp.sum(picked, axis=1, keepdims=True).astype(jnp.int32) - 1
    return jnp.where(token == iota((rows, tokens), 1), 1.0, 0.0).astype(lowp)


def seat_kernel(experts, cap, cap_rows, seq_rows,
                routes_ref, order_ref, cot_ref, slots_ref, table_ref, rows_ref,
                route_s, order_s, flat_s):
    images, seq, _ = routes_ref.shape
    tokens = images * seq_rows
    step = pl.program_id(0)

    @pl.when(step == 0)
    def _():
        route_s[...] = jnp.full(route_s.shape, -1, jnp.int32)
        order_s[...] = jnp.zeros(order_s.shape, jnp.int32)
        flat_s[...] = jnp.zeros(flat_s.shape, lowp)
        for image in range(images):
            rows = pl.ds(image * seq_rows, seq)
            route_s[rows, :] = routes_ref[image]
            order_s[rows, :] = order_ref[image]
            flat_s[rows, :] = cot_ref[image]
        lane = iota((tokens, LANES), 1)
        wide_lane = iota((tokens, experts * HALF), 1)
        route = [route_s[:, k : k + 1] for k in range(2)]
        order = [order_s[:, k : k + 1] for k in range(2)]
        low_hit = [(order[k] & (HALF - 1)) == (lane & (HALF - 1)) for k in range(2)]
        low_b = [jnp.where(low_hit[k], 1.0, 0.0).astype(lowp) for k in range(2)]
        high_b = [
            jnp.where((route[k] * HALF + (order[k] >> SHIFT)) == wide_lane, 1.0, 0.0).astype(lowp)
            for k in range(2)
        ]
        counts = (dot_tn(low_b[0], high_b[0]) + dot_tn(low_b[1], high_b[1])).astype(lowp)
        before = iota((LANES, LANES), 0)
        after = iota((LANES, LANES), 1)
        upper = jnp.where((after < HALF) & (after < (before & (HALF - 1))), 1.0, 0.0).astype(lowp)
        within = dot(upper, counts)
        block = (experts * HALF, experts * HALF)
        earlier = jnp.where(
            ((iota(block, 0) >> SHIFT) == (iota(block, 1) >> SHIFT)) & (iota(block, 0) < iota(block, 1)),
            1.0, 0.0,
        ).astype(lowp)
        base = jnp.sum(dot(counts, earlier)[:HALF], axis=0, keepdims=True)
        place = within + base
        place_high = jnp.floor(place * (1.0 / HALF))
        place_low = place - place_high * HALF
        split = jnp.where(iota(place.shape, 0) < HALF, place_high, place_low).astype(lowp)
        weight = jnp.where(lane < HALF, float(HALF), 1.0)
        token = iota((tokens, LANES), 0) + 1
        table = jnp.zeros((experts * 8, LANES), wide)
        row = iota((tokens, experts * 8), 1)
        columns = iota((tokens, 4), 1)
        found = jnp.zeros((tokens, 4), jnp.int32)
        for k in range(2):
            gathered = dot_nt(high_b[k], split)
            position = jnp.sum(
                jnp.where(low_hit[k], gathered * weight, 0.0), axis=1, keepdims=True
            ).astype(jnp.int32)
            seated = (position < cap) & (route[k] >= 0)
            slot = jnp.where(seated, route[k] * cap_rows + position, -1)
            found = jnp.where(columns == k, slot, found)
            found = jnp.where(columns == 2 + k, route[k], found)
            which = jnp.where(seated, route[k] * 8 + (position >> SHIFT), -1)
            which_b = jnp.where(which == row, 1.0, 0.0).astype(lowp)
            value = jnp.where(lane < HALF, token >> SHIFT, token & (HALF - 1)).astype(wide)
            value_b = jnp.where((position & (HALF - 1)) == (lane & (HALF - 1)), value, 0.0).astype(lowp)
            table = table + dot_tn(which_b, value_b)
        table_ref[...] = table
        for image in range(images):
            slots_ref[image] = found[image * seq_rows : (image + 1) * seq_rows]

    hits = token_hits(table_ref, step, cap_rows, tokens)
    rows_ref[0] = dot(hits, flat_s[...]).astype(lowp)


def spread_rows(flat, rows):
    return flat.reshape(flat.shape[0] // rows, rows, flat.shape[1])


def load_rows(scratch, ref, rows):
    for image in range(ref.shape[0]):
        scratch[image * rows : image * rows + ref.shape[1], :] = ref[image].astype(wide)


def front_kernel(seq, experts, rows,
                 me_ref, x_ref, noise_ref, vec_ref, wq_ref, wk_ref, wv_ref, wo_ref, wr_ref,
                 q_ref, k_ref, v_ref, lse_ref, mix_ref, state_ref, aug_ref, probs_ref,
                 x_s, noise_s):
    pack, width = x_ref.shape[0], x_s.shape[1]

    @pl.when(pl.program_id(0) == 0)
    def _():
        x_s[...] = jnp.zeros(x_s.shape, wide)
        noise_s[...] = jnp.zeros(noise_s.shape, wide)

    load_rows(x_s, x_ref, rows)
    for image in range(pack):
        noise_s[image * rows : image * rows + seq, :] = noise_ref[image].T
    x = x_s[...]
    unit, _ = unit_norm(x)
    normed = (unit * vec_ref[0:1, :] + vec_ref[1:2, :]).astype(lowp)
    head_size = width // HEADS
    query = (dot(normed, wq_ref[...]) + vec_ref[2:3, :]).astype(lowp)
    query = query * (head_size ** -0.5)
    key = dot(normed, wk_ref[...]).astype(lowp)
    value = (dot(normed, wv_ref[...]) + vec_ref[3:4, :]).astype(lowp)
    q_ref[...] = spread_rows(query, rows)
    k_ref[...] = spread_rows(key, rows)
    v_ref[...] = spread_rows(value, rows)
    live = iota((rows, rows), 1) < seq
    lane = iota((rows, LANES), 1)
    mixed = []
    for image in range(pack):
        span = slice(image * rows, (image + 1) * rows)
        lse_all = jnp.zeros((rows, LANES), wide)
        joined = []
        for pair in range(HEADS // 2):
            cols = slice(pair * LANES, (pair + 1) * LANES)
            q2, k2, v2 = query[span, cols], key[span, cols], value[span, cols]
            outs = []
            for half in range(2):
                mine = (lane < HALF) if half == 0 else (lane >= HALF)
                scores = dot_nt(jnp.where(mine, q2, jnp.zeros_like(q2)), k2)
                scores = jnp.where(live, scores, -1e30)
                peak = jnp.max(scores, axis=1, keepdims=True)
                expo = jnp.exp(scores - peak)
                total = jnp.sum(expo, axis=1, keepdims=True)
                lse_all = jnp.where(lane == pair * 2 + half, peak + jnp.log(total), lse_all)
                outs.append(dot((expo / total).astype(lowp), v2))
            joined.append(jnp.where(lane < HALF, outs[0], outs[1]).astype(lowp))
        lse_ref[image] = lse_all.T[0:8]
        mixed.append(jnp.concatenate(joined, axis=1))
    mixed = jnp.concatenate(mixed, axis=0)
    mix_ref[...] = spread_rows(mixed, rows)
    state = x + dot(mixed, wo_ref[...]) + vec_ref[4:5, :]
    state_ref[...] = spread_rows(state, rows)
    unit_two, _ = unit_norm(state)
    routed = (unit_two * vec_ref[5:6, :] + vec_ref[6:7, :]).astype(lowp)
    logits = dot_nt(routed, wr_ref[...]) + noise_s[...]
    top = jnp.max(logits, axis=1, keepdims=True)
    expo = jnp.exp(logits - top)
    probs = expo / jnp.sum(expo, axis=1, keepdims=True)
    probs_ref[...] = spread_rows(probs, rows)
    shape = (experts, LANES)
    widen = jnp.where(iota(shape, 0) == iota(shape, 1), 1.0, 0.0).astype(lowp)
    aug_ref[:, :, 0:width] = spread_rows(routed, rows)
    aug_ref[:, :, width : width + LANES] = spread_rows(
        dot(probs.astype(lowp), widen).astype(lowp), rows)


def send_kernel(cap, gate_rows, first, me_ref, table_ref, aug_ref, *out_refs):
    cap_rows, width = out_refs[0].shape
    tokens = aug_ref.shape[0]
    for index, out_ref in enumerate(out_refs):
        chunk = me_ref[0] ^ (first + index)
        hits = token_hits(table_ref, chunk, cap_rows, tokens)
        full = dot(hits, aug_ref[...])
        rows = full[:, 0:width]
        lane = iota((cap_rows, LANES), 1)
        gate = jnp.sum(jnp.where(lane == chunk, full[:, width:], 0.0), axis=1, keepdims=True)
        at = iota((cap_rows, width), 0)
        for part in range(gate_rows):
            line = column_to_row(gate, width, part * width)
            rows = jnp.where(at == cap + part, line, rows)
        out_ref[...] = rows.astype(lowp)


def expert_kernel(cap, gate_rows, size, me_ref, *refs):
    x_refs, (g_ref, win_ref, wout_ref) = refs[:size], refs[size : size + 3]
    back_refs = refs[-size - 4 : -4]
    prod_ref, inner_ref, rows_ref, x_s = refs[-4:]
    cap_rows, width = x_s.shape
    step = pl.program_id(0)
    for index in range(size):

        @pl.when(step == index)
        def _(index=index):
            x_s[...] = x_refs[index][...]

    x = x_s[...]
    rows_ref[0] = x
    grad = g_ref[0].astype(wide)
    gate = jnp.zeros((cap_rows, 1), wide)
    for part in range(gate_rows):
        line = x_s[cap + part : cap + part + 1, :].astype(wide)
        gate = gate + row_to_column(line, cap_rows, part * width)
    gate = jnp.where(iota((cap_rows, 1), 0) < cap, gate, 0.0)
    slot_grad = (gate * grad).astype(lowp)
    rows_ref[1] = slot_grad
    outer = (2.0 / jnp.pi) ** 0.5
    pre = dot(x, win_ref[...])
    hidden = dot_nt(slot_grad, wout_ref[...])
    square = pre * pre
    half = 0.5 * jnp.tanh(pre * (outer + (outer * 0.044715) * square)) + 0.5
    act = (pre * half).astype(lowp)
    slope = half * (
        1.0 + (1.0 - half) * (pre * (2.0 * outer + (6.0 * outer * 0.044715) * square))
    )
    pre_grad = (hidden * slope).astype(lowp)
    inner_ref[0] = pre_grad
    inner_ref[1] = act
    back = dot_nt(pre_grad, win_ref[...])
    made = dot(act, wout_ref[...]).astype(lowp)
    prod_ref[0] = made
    gate_grad = jnp.sum(grad * made.astype(wide), axis=1, keepdims=True)
    at = iota((cap_rows, width), 0)
    for part in range(gate_rows):
        line = column_to_row(gate_grad, width, part * width)
        high = line.astype(lowp).astype(wide)
        back = jnp.where(at == cap + part, high, back)
        back = jnp.where(at == cap + gate_rows + part, line - high, back)
    for index in range(size):

        @pl.when(step == index)
        def _(index=index):
            back_refs[index][...] = back.astype(lowp)


def weight_kernel(n_dp, rows_ref, inner_ref, through_ref, out_ref, passed_ref, in_s, out_s):
    step = pl.program_id(0)
    width, inner = in_s.shape

    @pl.when(step == 0)
    def _():
        in_s[...] = jnp.zeros(in_s.shape, wide)
        out_s[...] = jnp.zeros(out_s.shape, wide)

    in_s[...] += dot_tn(rows_ref[0], inner_ref[0])
    out_s[...] += dot_tn(rows_ref[1], inner_ref[1])

    @pl.when(step == pl.num_programs(0) - 1)
    def _():
        tall, flat = inner // n_dp, width // n_dp
        for owner in range(n_dp):
            base = owner * 2 * tall
            for block in range(inner // width):
                out_ref[base + block * flat : base + (block + 1) * flat, :] = in_s[
                    owner * flat : (owner + 1) * flat, block * width : (block + 1) * width
                ].astype(lowp)
            out_ref[base + tall : base + 2 * tall, :] = (
                out_s[:, owner * tall : (owner + 1) * tall].T.astype(lowp))


def slot_hits(slots, shape):
    at = iota(shape, 1)
    return slots[:, 0:1] == at, slots[:, 1:2] == at


def combine_kernel(experts, cap, cap_rows, gate_rows, rows,
                   me_ref, slots_ref, cot_ref, mix_ref, state_ref, probs_ref, vec_ref, wo_ref,
                   wr_ref, *rest):
    rows_refs, (state_grad_ref, mixed_grad_ref, sums_ref, cot_s, aug_s) = (
        rest[:experts], rest[experts:])
    step = pl.program_id(0)
    width = cot_s.shape[1]

    @pl.when(step == 0)
    def _():
        cot_s[...] = jnp.zeros(cot_s.shape, wide)
        sums_ref[...] = jnp.zeros(sums_ref.shape, wide)
        for away in range(experts):
            rows_ref = rows_refs[away]
            chunk = me_ref[0] ^ away
            lane = iota((cap_rows, LANES), 1)
            extra = jnp.zeros((cap_rows, LANES), wide)
            for part in range(gate_rows):
                for piece in range(2):
                    row = cap + piece * gate_rows + part
                    line = rows_ref[row : row + 1, :].astype(wide)
                    column = row_to_column(line, cap_rows, part * width)
                    extra = jnp.where(lane == chunk + piece * HALF, extra + column, extra)
            at = pl.ds(pl.multiple_of(chunk * cap_rows, 16), cap_rows)
            aug_s[at, 0:width] = rows_ref[...]
            aug_s[at, width : width + LANES] = extra.astype(lowp)

    load_rows(cot_s, cot_ref, rows)
    slots = slots_ref[...].reshape(cot_s.shape[0], 4)
    first, second = slot_hits(slots, (cot_s.shape[0], experts * cap_rows))
    hits = jnp.where(first | second, 1.0, 0.0).astype(lowp)
    full = dot(hits, aug_s[...])
    shape = (LANES, experts)
    narrow = jnp.where((iota(shape, 0) & (HALF - 1)) == iota(shape, 1), 1.0, 0.0)
    prob_grad = dot(full[:, width:].astype(lowp), narrow.astype(lowp))
    flat = lambda ref: ref[...].reshape(cot_s.shape[0], ref.shape[2])
    probs = flat(probs_ref)
    logit_grad = (
        probs * (prob_grad - jnp.sum(probs * prob_grad, axis=1, keepdims=True))
    ).astype(lowp)
    routed_grad = full[:, 0:width] + dot(logit_grad, wr_ref[...])
    unit_two, inverse_two = unit_norm(flat(state_ref))
    gain_two = vec_ref[5:6, :]
    routed = (unit_two * gain_two + vec_ref[6:7, :]).astype(lowp)
    state_grad = cot_s[...] + norm_back(routed_grad * gain_two, unit_two, inverse_two)
    branch = state_grad.astype(lowp)
    state_grad_ref[...] = spread_rows(state_grad, rows)
    mixed_grad_ref[...] = spread_rows(dot_nt(branch, wo_ref[...]).astype(lowp), rows)
    sums_ref[0:width, :] += dot_tn(flat(mix_ref), branch)
    lines = [branch.astype(wide), routed_grad * unit_two, routed_grad]
    small = jnp.concatenate(
        [jnp.sum(line, axis=0, keepdims=True) for line in lines]
        + [jnp.zeros((5, width), wide)], axis=0
    )
    sums_ref[width : width + 8, :] += small
    sums_ref[width + 8 : width + 8 + experts, :] += dot_tn(logit_grad, routed)


def back_kernel(seq, experts, small_rows, rows,
                me_ref, x_ref, q_ref, k_ref, v_ref, lse_ref, state_grad_ref, mixed_grad_ref,
                vec_ref, wq_ref, wk_ref, wv_ref, *rest):
    early_ref, grad_ref, *piece_refs, x_s, sums_ref = rest
    step = pl.program_id(0)
    width = x_s.shape[1]
    pack = x_ref.shape[0]
    small_at = 4 * width

    @pl.when(step == 0)
    def _():
        x_s[...] = jnp.zeros(x_s.shape, wide)
        sums_ref[...] = jnp.zeros(sums_ref.shape, wide)

    load_rows(x_s, x_ref, rows)
    live = iota((rows, rows), 0) < seq
    lane = iota((rows, LANES), 1)
    scale = (width // HEADS) ** -0.5
    parts = [[], [], []]
    for image in range(pack):
        query, key, value = q_ref[image], k_ref[image], v_ref[image]
        mixed_grad, lse = mixed_grad_ref[image], lse_ref[image]
        lines = [[], [], []]
        for pair in range(HEADS // 2):
            cols = slice(pair * LANES, (pair + 1) * LANES)
            q2, k2, v2, g2 = query[:, cols], key[:, cols], value[:, cols], mixed_grad[:, cols]
            outs = [[], [], []]
            for half in range(2):
                mine = (lane < HALF) if half == 0 else (lane >= HALF)
                scores = dot_nt(k2, jnp.where(mine, q2, jnp.zeros_like(q2)))
                head = pair * 2 + half
                weights = jnp.exp(jnp.where(live, scores - lse[head : head + 1, :], -1e30))
                weight_grad = dot_nt(v2, jnp.where(mine, g2, jnp.zeros_like(g2)))
                product = weights * weight_grad
                score_grad = (
                    product - weights * jnp.sum(product, axis=0, keepdims=True)
                ).astype(lowp)
                outs[0].append(dot_tn(score_grad, k2))
                outs[1].append(dot(score_grad, q2))
                outs[2].append(dot(weights.astype(lowp), g2))
            for which in range(3):
                joined = jnp.where(lane < HALF, outs[which][0], outs[which][1])
                if which == 0:
                    joined = joined * scale
                lines[which].append(joined.astype(lowp))
        for which in range(3):
            parts[which].append(jnp.concatenate(lines[which], axis=1))
    query_grad, key_grad, value_grad = (jnp.concatenate(p, axis=0) for p in parts)
    unit_one, inverse_one = unit_norm(x_s[...])
    gain_one = vec_ref[0:1, :]
    normed = (unit_one * gain_one + vec_ref[1:2, :]).astype(lowp)
    sums_ref[0:width, :] += dot_tn(normed, query_grad)
    sums_ref[width : 2 * width, :] += dot_tn(normed, key_grad)
    sums_ref[2 * width : 3 * width, :] += dot_tn(normed, value_grad)
    normed_grad = (
        dot_nt(query_grad, wq_ref[...])
        + dot_nt(key_grad, wk_ref[...])
        + dot_nt(value_grad, wv_ref[...])
    )
    result = state_grad_ref[...].reshape(x_s.shape) + norm_back(
        normed_grad * gain_one, unit_one, inverse_one)
    grad_ref[...] = spread_rows(result.astype(lowp), rows)[:, 0:seq]
    lines = [query_grad.astype(wide), value_grad.astype(wide), normed_grad * unit_one, normed_grad]
    small = jnp.concatenate(
        [jnp.sum(line, axis=0, keepdims=True) for line in lines]
        + [jnp.zeros((4, width), wide)], axis=0
    )
    sums_ref[small_at : small_at + 8, :] += small

    @pl.when(step == pl.num_programs(0) - 1)
    def _():
        part_rows = piece_refs[0].shape[0]
        sums_ref[3 * width : 4 * width, :] = early_ref[0:width, :]
        sums_ref[small_at + 8 : small_at + small_rows, :] = early_ref[width:, :]
        exact = sums_ref[small_at : small_at + small_rows, :]
        sums_ref[small_at + small_rows : small_at + 2 * small_rows, :] = (
            exact - exact.astype(lowp).astype(wide)
        )
        for away in range(experts):
            start = pl.multiple_of((me_ref[0] ^ away) * part_rows, 16)
            piece_refs[away][...] = sums_ref[pl.ds(start, part_rows), :].astype(lowp)


def sum_kernel(*refs):
    total = refs[0][...].astype(wide)
    for ref in refs[1:-1]:
        total = total + ref[...].astype(wide)
    refs[-1][...] = total.astype(lowp)


def unpack_kernel(experts, me_ref, *refs):
    piece_refs, weight_refs = refs[:experts], refs[experts : experts + 4]
    small_ref, all_s = refs[experts + 4], refs[experts + 5]
    part_rows, width = piece_refs[0].shape
    small_rows = small_ref.shape[0]
    for away in range(experts):
        start = pl.multiple_of((me_ref[0] ^ away) * part_rows, 16)
        all_s[pl.ds(start, part_rows), :] = piece_refs[away][...].astype(wide)
    for which in range(4):
        weight_refs[which][...] = all_s[which * width : (which + 1) * width, :]
    at = 4 * width
    small_ref[...] = (all_s[at : at + small_rows, :]
                      + all_s[at + small_rows : at + 2 * small_rows, :])


def out_kernel(slots_ref, aug_ref, state_ref, rows_ref, out_ref):
    _, rows, width = state_ref.shape
    seq = out_ref.shape[1]
    slot_total = rows_ref.shape[0]
    lane = iota((rows, LANES), 1)
    gates = aug_ref[0, :, width : width + LANES].astype(wide)
    gate = [
        jnp.sum(jnp.where(lane == slots_ref[0, :, 2 + k : 3 + k], gates, 0.0), axis=1, keepdims=True)
        for k in range(2)
    ]
    first, second = slot_hits(slots_ref[0], (rows, slot_total))
    hits = jnp.where(first, gate[0], jnp.where(second, gate[1], 0.0)).astype(lowp)
    out_ref[0] = (state_ref[0] + dot(hits, rows_ref[...])).astype(lowp)[0:seq]


def adam_kernel(*refs):
    grad_ref, states, results, rounded_ref = refs[0], refs[1:7], refs[7:13], refs[13]
    corr_one = 1.0 - BETA_ONE**adam_steps
    corr_two = 1.0 - BETA_TWO**adam_steps
    for which in range(2):
        master, moment, second = (ref[0] for ref in states[which::2])
        grad = grad_ref[which].astype(wide)
        new_moment = BETA_ONE * moment + (1.0 - BETA_ONE) * grad
        new_second = BETA_TWO * second + (1.0 - BETA_TWO) * grad * grad
        update = (
            LEARN_RATE * (new_moment / corr_one) / (jnp.sqrt(new_second / corr_two) + ADAM_EPS)
        )
        new_master = master - update
        for ref, value in zip(results[which::2], (new_master, new_moment, new_second)):
            ref[0] = value
        rounded_ref[which] = new_master.astype(lowp)


def spread_kernel(rounded_ref, in_ref, out_ref):
    _, flat, inner = in_ref.shape
    width = out_ref.shape[2]
    for block in range(inner // width):
        in_ref[0, :, block * width : (block + 1) * width] = rounded_ref[
            0, block * flat : (block + 1) * flat, :]
    out_ref[0] = rounded_ref[1]


def whole(shape):
    return pl.BlockSpec(shape, lambda i: (0,) * len(shape))


def one(shape, pack=1):
    return pl.BlockSpec((pack,) + shape, lambda i: (i,) + (0,) * len(shape))


def smem():
    return pl.BlockSpec(memory_space=pltpu.SMEM)


def hbm():
    return pl.BlockSpec(memory_space=pl.ANY)


def call(kernel, micros, megabytes, name, grid, inputs, in_specs, out_specs, out_shape,
         scratch=(), after=(), aliases=None, prefetch=0):
    count, extra = len(inputs), len(after)

    def body(*refs):
        kernel(*refs[:count], *refs[count + extra :])

    return pl.pallas_call(
        body,
        grid_spec=pltpu.PrefetchScalarGridSpec(
            num_scalar_prefetch=prefetch, grid=grid, in_specs=in_specs + [hbm()] * extra,
            out_specs=out_specs, scratch_shapes=list(scratch)),
        out_shape=out_shape,
        input_output_aliases=aliases or {},
        compiler_params=params(len(grid), megabytes),
        cost_estimate=cost(micros),
        name=name,
    )(*inputs, *after)


def like(shape, dtype):
    return jax.ShapeDtypeStruct(shape, dtype)


def swap_expert(value, away, n_expert):
    return lax.ppermute(value, "expert", [(i, i ^ away) for i in range(n_expert)])


def on_device(n_expert, n_dp, images, cotangent, router_noise, routes, seat_order,
              norm1_gain, norm1_shift, query_weight, query_bias, key_weight, value_weight,
              value_bias, output_weight, output_bias, norm2_gain, norm2_shift, router_weight,
              expert_in, expert_out, master_in, master_out, moment_in, moment_out,
              second_in, second_out):
    count, seq, width = images.shape
    experts = router_noise.shape[2]
    cap = (count * seq * 2 + experts - 1) // experts
    gate_rows = (cap + width - 1) // width
    cap_rows = round_up(cap + 2 * gate_rows, 16)
    seq_rows = round_up(seq, 16)
    tokens = count * seq_rows
    inner = expert_in.shape[2]
    slot_total = experts * cap_rows
    aug = width + LANES
    me = lax.axis_index("expert").astype(jnp.int32).reshape(1)
    router_rows = router_weight.T
    noise_rows = router_noise.transpose(0, 2, 1)
    vecs = jnp.stack([norm1_gain, norm1_shift, query_bias, value_bias, output_bias,
                      norm2_gain, norm2_shift, norm2_shift])

    slots, table, grad_rows = call(
        functools.partial(seat_kernel, experts, cap, cap_rows, seq_rows), 17, 56, "seat",
        (experts,), (routes, seat_order.reshape(routes.shape), cotangent),
        [whole(routes.shape), whole(routes.shape), whole(cotangent.shape)],
        [whole((count, seq_rows, 4)), whole((experts * 8, LANES)), one((cap_rows, width))],
        [like((count, seq_rows, 4), jnp.int32), like((experts * 8, LANES), wide),
         like((experts, cap_rows, width), lowp)],
        [pltpu.VMEM((tokens, 2), jnp.int32), pltpu.VMEM((tokens, 2), jnp.int32),
         pltpu.VMEM((tokens, width), lowp)])
    grad_in = lax.all_to_all(grad_rows, "expert", split_axis=0, concat_axis=0, tiled=True)

    square = (width, width)
    token_shape = (count, seq_rows, width)
    pack = PACK if count % PACK == 0 else 1
    query, key, value, lse, mixed, state, routed, probs = call(
        functools.partial(front_kernel, seq, experts, seq_rows), 19, 56, "front", (count // pack,),
        (me, images, noise_rows, vecs, query_weight, key_weight, value_weight, output_weight,
         router_rows),
        [smem(), one((seq, width), pack), one((experts, seq), pack), whole((8, width)),
         whole(square), whole(square), whole(square), whole(square), whole((experts, width))],
        [one((seq_rows, width), pack)] * 3 + [
            one((8, seq_rows), pack), one((seq_rows, width), pack), one((seq_rows, width), pack),
            one((seq_rows, aug), pack), one((seq_rows, experts), pack)],
        [like(token_shape, lowp)] * 3 + [
            like((count, 8, seq_rows), wide), like(token_shape, lowp),
            like(token_shape, wide), like((count, seq_rows, aug), lowp),
            like((count, seq_rows, experts), wide)],
        [pltpu.VMEM((pack * seq_rows, width), wide),
         pltpu.VMEM((pack * seq_rows, experts), wide)])

    quarter = max(experts // 4, 1)
    spans = [(first, first + quarter) for first in range(0, experts, quarter)]
    sent = [None] * experts
    chunk_spec, chunk_like = whole((cap_rows, width)), like((cap_rows, width), lowp)
    before = ()
    for first, size in [(quarter, quarter), (2 * quarter, quarter), (0, quarter),
                        (3 * quarter, quarter)]:
        outs = call(
            functools.partial(send_kernel, cap, gate_rows, first), 0.3, 32, f"send{first}",
            (1,), (me, table, routed.reshape(tokens, aug)),
            [smem(), whole((experts * 8, LANES)), whole((tokens, aug))],
            [chunk_spec] * size, [chunk_like] * size, after=before)
        sent[first : first + size] = outs
        before = (outs[0],)
    arrived = [sent[0]] + [swap_expert(sent[away], away, n_expert) for away in range(1, experts)]

    buffers = ()
    back_rows = []
    for first, end in spans:
        size = end - first
        block = lambda i, ref, first=first: (ref[0] ^ (first + i), 0, 0)
        fixed = lambda i, ref: (0, 0)
        line = lambda i, ref, first=first: (0, first + i, 0)
        chunk_at = pl.BlockSpec((cap_rows, width), fixed)
        outs = call(
            functools.partial(expert_kernel, cap, gate_rows, size), 0.3, 52, f"expert{first}",
            (size,),
            (me, *arrived[first:end], grad_in, expert_in[0],
             expert_out[0], *buffers),
            [chunk_at] * size + [
                pl.BlockSpec((1, cap_rows, width), block),
                pl.BlockSpec((width, inner), fixed), pl.BlockSpec((inner, width), fixed)]
            + [hbm()] * len(buffers),
            [chunk_at] * size + [
                pl.BlockSpec((1, cap_rows, width), block),
                pl.BlockSpec((2, cap_rows, inner), line), pl.BlockSpec((2, cap_rows, width), line)],
            [chunk_like] * size + [
                like((experts, cap_rows, width), lowp),
                like((2, slot_total, inner), lowp), like((2, slot_total, width), lowp)],
            [pltpu.VMEM((cap_rows, width), lowp)], prefetch=1,
            aliases={size + 4 + k: size + k for k in range(len(buffers))})
        back_rows += outs[:size]
        buffers = tuple(outs[size:])
    produced, inner_rows, outer_rows = buffers
    back_rows = [back_rows[0]] + [
        swap_expert(back_rows[away], away, n_expert) for away in range(1, experts)]

    steps = 4
    per = slot_total // steps

    line = lambda size: pl.BlockSpec((2, per, size), lambda i: (0, i, 0))
    weight_grads, produced = call(
        functools.partial(weight_kernel, n_dp), 0.02, 52, "weight", (steps,),
        (outer_rows, inner_rows, produced), [line(width), line(inner), hbm()],
        [whole((2 * inner, width)), hbm()],
        [like((2 * inner, width), lowp), like(produced.shape, lowp)],
        [pltpu.VMEM((width, inner), wide), pltpu.VMEM((width, inner), wide)],
        after=back_rows[1 : 3 * quarter], aliases={2: 1})
    tall, flat = inner // n_dp, width // n_dp
    share = lax.psum_scatter(weight_grads, "dp", scatter_dimension=0, tiled=True)
    returned = lax.all_to_all(produced, "expert", split_axis=0, concat_axis=0, tiled=True)

    early_small = 8 + round_up(experts, 8)
    early_rows = width + early_small
    state_grad, mixed_grad, early = call(
        functools.partial(combine_kernel, experts, cap, cap_rows, gate_rows, seq_rows), 300,
        56,
        "combine", (count // pack,),
        (me, slots, cotangent, mixed, state, probs, vecs, output_weight, router_rows,
         *back_rows),
        [smem(), one((seq_rows, 4), pack), one((seq, width), pack), one((seq_rows, width), pack),
         one((seq_rows, width), pack), one((seq_rows, experts), pack), whole((8, width)), whole(square),
         whole((experts, width))] + [chunk_spec] * experts,
        [one((seq_rows, width), pack), one((seq_rows, width), pack), whole((early_rows, width))],
        [like(token_shape, wide), like(token_shape, lowp), like((early_rows, width), wide)],
        [pltpu.VMEM((pack * seq_rows, width), wide), pltpu.VMEM((slot_total, aug), lowp)],
        after=(weight_grads,))

    small_rows = 8 + early_small
    part_rows = round_up(4 * width + 2 * small_rows, 16 * experts) // experts
    part_spec, part_like = whole((part_rows, width)), like((part_rows, width), lowp)
    pack = 2 if count % 2 == 0 else 1
    images_grad, *pieces = call(
        functools.partial(back_kernel, seq, experts, small_rows, seq_rows), 300, 56, "back",
        (count // pack,),
        (me, images, query, key, value, lse, state_grad, mixed_grad, vecs, query_weight,
         key_weight, value_weight, early),
        [smem(), one((seq, width), pack)] + [one((seq_rows, width), pack)] * 3
        + [one((8, seq_rows), pack), one((seq_rows, width), pack), one((seq_rows, width), pack),
           whole((8, width)), whole(square), whole(square), whole(square),
           whole((early_rows, width))],
        [one((seq, width), pack)] + [part_spec] * experts,
        [like(images.shape, lowp)] + [part_like] * experts,
        [pltpu.VMEM((pack * seq_rows, width), wide), pltpu.VMEM((part_rows * experts, width), wide)])
    across = pl.BlockSpec((1, flat, width), lambda i: (0, 0, i))
    down = pl.BlockSpec((1, flat, width), lambda i: (0, i, 0))
    both = pl.BlockSpec((2, flat, width), lambda i: (0, i, 0))
    *states, rounded = call(
        adam_kernel, 1, 56, "adam", (inner // width,),
        (share.reshape(2, tall, width), master_in, master_out, moment_in, moment_out,
         second_in, second_out),
        [both] + [across, down] * 3, [across, down] * 3 + [both],
        [like(master_in.shape, wide), like(master_out.shape, wide)] * 3
        + [like((2, tall, width), lowp)], after=(pieces[0], returned))

    def add(parts, name, after=()):
        return call(sum_kernel, 1, 56, name, (1,), parts, [part_spec] * len(parts), part_spec,
                    part_like, after=after)

    spread = lax.all_gather(rounded, "dp", axis=0, tiled=True)
    new_expert_in, new_expert_out = call(
        spread_kernel, 2, 56, "spread", (n_dp,), (spread,), [
            pl.BlockSpec((2, tall, width), lambda i: (i, 0, 0))],
        [pl.BlockSpec((1, flat, inner), lambda i: (0, i, 0)),
         pl.BlockSpec((1, tall, width), lambda i: (0, i, 0))],
        [like(expert_in.shape, lowp), like(expert_out.shape, lowp)])
    mine = add([pieces[0]] + [swap_expert(pieces[away], away, n_expert)
                              for away in range(1, experts)], "sum_plane",
               (returned, rounded))
    block_out = call(
        out_kernel, 1, 56, "block_out", (count,),
        (slots, routed, state, returned.reshape(slot_total, width)),
        [one((seq_rows, 4)), one((seq_rows, aug)), one((seq_rows, width)),
         whole((slot_total, width))],
        one((seq, width)), like(images.shape, lowp), after=(mine,))
    share = add([mine] + [
        lax.ppermute(mine, "dp", [(i, (i + shift) % n_dp) for i in range(n_dp)])
        for shift in range(1, n_dp)], "sum_dp", (block_out,))
    shares = [share] + [swap_expert(share, away, n_expert) for away in range(1, experts)]

    *big, small_sum = call(
        functools.partial(unpack_kernel, experts), 3, 56, "unpack", (1,), (me, *shares),
        [smem()] + [part_spec] * experts,
        [whole(square)] * 4 + [whole((small_rows, width))],
        [like(square, wide)] * 4 + [like((small_rows, width), wide)],
        [pltpu.VMEM((part_rows * experts, width), wide)], after=(new_expert_in,))
    return (
        block_out,
        images_grad,
        small_sum[2],
        small_sum[3],
        big[0],
        small_sum[0],
        big[1],
        big[2],
        small_sum[1],
        big[3],
        small_sum[8],
        small_sum[9],
        small_sum[10],
        small_sum[16 : 16 + experts].T,
        new_expert_in,
        new_expert_out,
        *states,
    )


def solution(mesh):
    both = ("dp", "expert")
    in_specs = (
        (P(both, None, None),) * 4
        + (P(both, None),)
        + (P(),) * 12
        + (P("expert", None, None),) * 2
        + (P("expert", "dp", None),) * 6
    )
    out_specs = (
        (P(both, None, None),) * 2
        + (P(),) * 12
        + (P("expert", None, None),) * 2
        + (P("expert", "dp", None),) * 6
    )
    body = functools.partial(on_device, mesh.shape["expert"], mesh.shape["dp"])
    return jax.shard_map(body, mesh=mesh, in_specs=in_specs, out_specs=out_specs, check_vma=False)
```
